32 devices in a mesh: dp: 8 (over z, x), tensor: 4 (over y, core).
Axes of the slice: x: 2, y: 2, z: 4, core: 2. Of those that a mesh axis runs over, the one named last changes fastest.
Arguments:
- inputs: bfloat16 [8192, 768], P('dp'), may hold values from -6 to 6
- lengths: int32 [8], P('dp'), may hold values from 32 to 1024, as said below
- qkv_weight: bfloat16 [2, 768, 3, 768], P(None, None, None, 'tensor'), may hold values from -0.21875 to 0.21875
- out_weight: bfloat16 [2, 768, 768], P(None, 'tensor'), may hold values from -0.875 to 0.875
- up_weight: bfloat16 [2, 768, 3072], P(None, None, 'tensor'), may hold values from -0.21875 to 0.21875
- down_weight: bfloat16 [2, 3072, 768], P(None, 'tensor'), may hold values from -0.15625 to 0.15625
- norm_gain: float32 [2, 2, 768], replicated, may hold values from 0.5 to 1.5
- norm_bias: float32 [2, 2, 768], replicated, may hold values from -1.5 to 1.5
- cotangent: bfloat16 [8192, 768], P('dp'), may hold values from -6 to 6
Outputs:
- activations: bfloat16 [8192, 768], P('dp')
- input_grad: float32 [8192, 768], P('dp')
- grad_qkv: float32 [2, 768, 3, 768], P(None, None, None, 'tensor')
- grad_out: float32 [2, 768, 768], P(None, 'tensor')
- grad_up: float32 [2, 768, 3072], P(None, None, 'tensor')
- grad_down: float32 [2, 3072, 768], P(None, 'tensor')
- grad_gain: float32 [2, 2, 768], replicated
- grad_bias: float32 [2, 2, 768], replicated
The draws below stay inside these ranges and needn't reach their ends.
Inputs may be any that keep to these rules, and one draw needn't show every extreme that they name: `lengths`: slots from a sequence's length on are padding; in every draw some sequence uses all 1024 slots.
All inputs are finite; a program needn't handle non-finite values.
Results may differ from the reference program's by a relative error of at most 0.035.
Values may be sent and summed in bfloat16 or wider, within the bound.
A program may use at most 128 MiB of HBM per device.

```python
import jax
import jax.numpy as jnp
from jax import lax

D = 768
HEADS = 12
HEAD_DIM = 64
FF = 3072
LEN = 1024
MIN_LEN = 32
LAYERS = 2
SEQS = 8
TOKENS = 8192


def draw_lengths(key, part):
    key = jax.random.fold_in(key, 17)
    first_key, second_key = jax.random.split(key)
    drawn = jax.random.randint(first_key, (SEQS,), MIN_LEN, LEN + 1, dtype=jnp.int32)
    longest = jax.random.randint(second_key, (), 0, SEQS, dtype=jnp.int32)
    return jnp.where(jnp.arange(SEQS, dtype=jnp.int32) == longest, LEN, drawn).astype(jnp.int32)


def block_levels(key, dims, shards, smallest, top_value):
    factor_of = 1.0
    for position, parts in shards:
        draws = jax.random.uniform(jax.random.fold_in(jax.random.fold_in(key, 6), position), (parts,), jnp.float32, smallest / len(shards), top_value / len(shards))
        factor_of = factor_of * jnp.repeat(jnp.exp(draws), dims[position] // parts).reshape((-1,) + (1,) * (len(dims) - 1 - position))
    return factor_of


def bell_draw(rng, extent, scale, most, cuts=(), kind=jnp.bfloat16):
    gain = block_levels(rng, extent, cuts, -0.22, 0.18) if cuts else 1.0
    values = jax.random.normal(rng, extent, jnp.float32) * scale * gain
    return jnp.minimum(jnp.maximum(values, -most), most).astype(kind)


def setup_inputs(seed: int = 0) -> dict:
    key_of = jax.random.split(jax.random.key(seed), 10)
    inputs = bell_draw(key_of[0], (TOKENS, D), 1.0, 6.0, ((0, 8),))
    lengths = draw_lengths(jax.random.fold_in(key_of[9], 71), 0)
    qkv_weight = bell_draw(key_of[2], (LAYERS, D, 3, D), D ** -0.5, 0.21875, ((3, 4),))
    out_weight = bell_draw(key_of[3], (LAYERS, D, D), (D // 16) ** -0.5, 0.875, ((1, 4),))
    up_weight = bell_draw(key_of[4], (LAYERS, D, FF), D ** -0.5, 0.21875, ((2, 4),))
    down_weight = bell_draw(key_of[5], (LAYERS, FF, D), (FF // 2) ** -0.5, 0.15625, ((1, 4),))
    norm_gain = jnp.clip(1.0 + 0.1 * jax.random.normal(key_of[6], (LAYERS, 2, D), jnp.float32), 0.5, 1.5)
    norm_bias = bell_draw(key_of[7], (LAYERS, 2, D), 0.3, 1.5, (), jnp.float32)
    cotangent = bell_draw(key_of[8], (TOKENS, D), 1.0, 6.0, ((0, 8),))
    return {"inputs": inputs, "lengths": lengths, "qkv_weight": qkv_weight, "out_weight": out_weight, "up_weight": up_weight, "down_weight": down_weight, "norm_gain": norm_gain, "norm_bias": norm_bias, "cotangent": cotangent}


@jax.custom_vjp
def low(v):
    return lax.optimization_barrier(v.astype(jnp.bfloat16)).astype(jnp.float32)

@jax.custom_vjp
def low_back(v):
    return v

def low_keep(v):
    return (low(v), None)

def low_pass(kept, grad):
    return (grad,)

def back_keep(v):
    return (v, None)

def back_low(kept, grad):
    return (low(grad),)
low.defvjp(low_keep, low_pass)
low_back.defvjp(back_keep, back_low)

def layer_norm(values_in, gain_row, bias_row):
    centre = values_in - lax.optimization_barrier(jnp.mean(values_in, axis=-1, keepdims=True))
    spread = lax.optimization_barrier(jnp.mean(centre * centre, axis=-1, keepdims=True))
    return centre * lax.rsqrt(spread + 1e-05) * gain_row + bias_row

def residual_block(stream, weights, valid_rows, allowed):
    proj_qkv, proj_out, proj_up, proj_down, gain_rows, bias_rows = weights
    highest = lax.Precision.HIGHEST
    normed = low(layer_norm(stream, gain_rows[0], bias_rows[0]))
    projected = low_back(low(jnp.einsum('td,dje->jte', normed, proj_qkv, precision=highest)))
    queries = projected[0].reshape(LEN, HEADS, HEAD_DIM)
    key_rows = projected[1].reshape(LEN, HEADS, HEAD_DIM)
    value_rows = projected[2].reshape(LEN, HEADS, HEAD_DIM)
    scores = low_back(jnp.einsum('qhe,khe->hqk', queries, key_rows, precision=highest) * HEAD_DIM ** (-0.5))
    scores = jnp.where(allowed[None], scores, -1e+30)
    maximum = lax.optimization_barrier(jnp.max(scores, axis=-1, keepdims=True))
    exponent = jnp.exp(scores - maximum)
    softmax_rows = exponent / lax.optimization_barrier(jnp.sum(exponent, axis=-1, keepdims=True))
    context = jnp.einsum('hqk,khe->qhe', low(softmax_rows), value_rows, precision=highest).reshape(LEN, D)
    context = low_back(low(context))
    middle = stream + low_back(jnp.dot(context, proj_out, precision=highest))
    normed_mid = low(layer_norm(middle, gain_rows[1], bias_rows[1]))
    hidden = low_back(jnp.dot(normed_mid, proj_up, precision=highest))
    activated = low(jax.nn.gelu(hidden, approximate=False))
    branch = low_back(jnp.dot(activated, proj_down, precision=highest))
    return valid_rows[:, None] * (middle + branch)

def reference(inputs, lengths, qkv_weight, out_weight, up_weight, down_weight, norm_gain, norm_bias, cotangent):
    params = tuple((weight_in.astype(jnp.float32) for weight_in in (qkv_weight, out_weight, up_weight, down_weight, norm_gain, norm_bias)))
    positions = jnp.arange(LEN, dtype=jnp.int32)

    def one_sequence(totals, scan_item):
        rows_in, length_one, cotangent_rows = scan_item
        valid_rows = (positions < length_one).astype(jnp.float32)
        allowed = (positions[None, :] <= positions[:, None]) & (positions[None, :] < length_one)

        def forward(stream, weights):
            for layer_id in range(LAYERS):
                stream = residual_block(stream, tuple((weight_one[layer_id] for weight_one in weights)), valid_rows, allowed)
            return stream
        result, pullback = jax.vjp(forward, rows_in.astype(jnp.float32), params)
        stream_grad, weight_grads = pullback(cotangent_rows.astype(jnp.float32))
        totals = jax.tree.map(jnp.add, totals, weight_grads)
        return (totals, (result.astype(jnp.bfloat16), stream_grad))
    zeros_tree = jax.tree.map(jnp.zeros_like, params)
    totals, (outputs, stream_grads) = lax.scan(one_sequence, zeros_tree, (inputs.reshape(SEQS, LEN, D), lengths, cotangent.reshape(SEQS, LEN, D)))
    return (outputs.reshape(TOKENS, D), stream_grads.reshape(TOKENS, D), totals[0], totals[1], totals[2], totals[3], totals[4], totals[5])
```

```python
import functools

import jax
import jax.numpy as jnp
from jax import lax
from jax.experimental import pallas as pl
from jax.experimental.pallas import tpu as pltpu
from jax.sharding import PartitionSpec as P

HEAD_DIM = 64
LANES = 128
BF16 = jnp.bfloat16
F32 = jnp.float32
MESH = pl.DeviceIdType.MESH
ANY = pl.BlockSpec(memory_space=pl.ANY)
VMEM = pl.BlockSpec(memory_space=pltpu.VMEM)
SMEM = pl.BlockSpec(memory_space=pltpu.SMEM)


def dot_nn(a, b):
    return lax.dot_general(a, b, (((1,), (0,)), ((), ())), preferred_element_type=F32)


def dot_nt(a, b):
    return lax.dot_general(a, b, (((1,), (1,)), ((), ())), preferred_element_type=F32)


def dot_tn(a, b):
    return lax.dot_general(a, b, (((0,), (0,)), ((), ())), preferred_element_type=F32)


def norm_rows(values_in, gain_row, bias_row):
    centre = values_in - jnp.mean(values_in, axis=-1, keepdims=True)
    spread = jnp.mean(centre * centre, axis=-1, keepdims=True)
    return centre * lax.rsqrt(spread + 1e-05) * gain_row + bias_row


def gelu_pair(u):
    bell = jnp.exp(u * u * -0.5)
    t = 1.0 / (1.0 + 0.23164189 * jnp.abs(u))
    series = t * (0.127414796 + t * (-0.142248368 + t * (0.7107068705 + t * (-0.7265760135 + t * 0.5307027145))))
    tail = series * bell
    phi_cdf = jnp.where(u >= 0.0, 1.0 - tail, tail)
    return u * phi_cdf, phi_cdf + u * bell * 0.3989422804014327


class Chunks:
    def __init__(self, rows, count):
        self.rows, self.count = rows, count
        self.half = rows // 2

    def all(self, c):
        return pl.ds(c * self.rows, self.rows)

    def part(self, c, b):
        return pl.ds(pl.multiple_of(c * self.rows + b * self.half, self.half), self.half)


def forward_kernel(n_tensor, len_ref, x_hbm, wqkv_hbm, wout_hbm, wup_hbm, wdown_hbm, gain_ref, bias_ref, act_out,
                   xin, wqkv, wout, wup, wdown, normed, nmid, q_s, k_s, kt_s, v_s, ctx, lse, xh, midh, act, gpr,
                   part, rsbuf, ysend, yrecv, result, sems_in, rs_sem, y_sem, ag_sem, out_sem):
    layers = wqkv.shape[0]
    rows_all, width = xin.shape
    ch = Chunks(256, rows_all // 256)
    C = ch.count
    dp, t = lax.axis_index("dp"), lax.axis_index("tensor")
    b = lax.rem(t, 2)
    sib = (dp, t + 1 - 2 * b)
    peer = (dp, lax.rem(t + 2, n_tensor))
    length = len_ref[0]

    loads = [(x_hbm, xin), (wqkv_hbm, wqkv), (wout_hbm, wout), (wup_hbm, wup), (wdown_hbm, wdown)]
    loads = [pltpu.make_async_copy(a, o, sems_in.at[i]) for i, (a, o) in enumerate(loads)]
    for cp in loads:
        cp.start()
    waited = set()

    def need(i):
        if i not in waited:
            waited.add(i)
            loads[i].wait()

    barrier = pltpu.get_barrier_semaphore()
    for other in (sib, peer):
        pl.semaphore_signal(barrier, inc=1, device_id=other, device_id_type=MESH)
    pl.semaphore_wait(barrier, 2)

    def remote(src, dst, sem, dev):
        return pltpu.make_async_remote_copy(src_ref=src, dst_ref=dst, send_sem=sem.at[0], recv_sem=sem.at[1],
                                            device_id=dev, device_id_type=MESH)

    mine, others = pl.ds(pl.multiple_of(b * ch.half, ch.half), ch.half), pl.ds(pl.multiple_of((1 - b) * ch.half, ch.half), ch.half)

    def rs_copy(p, c):
        s = p % 2
        return remote(part.at[s, c, others], rsbuf.at[s, c], rs_sem.at[s, c], sib)

    def y_copy(p, c):
        s = p % 2
        return remote(ysend.at[s, c], yrecv.at[s, c], y_sem.at[s, c], peer)

    def ag_copy(p, c):
        buf = {0: nmid.at[0], 1: normed.at[1], 2: nmid.at[1], 3: result}[p]
        rows = ch.part(c, b)
        return remote(buf.at[rows], buf.at[rows], ag_sem.at[p % 2, c], sib)

    gain = lambda l, i: gain_ref[pl.ds(2 * l + i, 1), :]
    bias = lambda l, i: bias_ref[pl.ds(2 * l + i, 1), :]
    lane = lax.broadcasted_iota(jnp.int32, (ch.rows, LANES), 1)
    low = lane < HEAD_DIM

    def attend(l, c):
        need(1)
        rows = ch.all(c)
        if l == 0:
            need(0)
            normed[0, rows] = norm_rows(xin[rows].astype(F32), gain(0, 0), bias(0, 0)).astype(BF16)
        nc = normed[l, rows]
        q = dot_nn(nc, wqkv[l, 0]).astype(BF16) * jnp.asarray(HEAD_DIM ** (-0.5), BF16)
        k = dot_nn(nc, wqkv[l, 1])
        q_s[l, rows] = q
        k_s[l, rows] = k.astype(BF16)
        kt_s[l, :, rows] = k.T.astype(BF16)
        v_s[l, rows] = dot_nn(nc, wqkv[l, 2]).astype(BF16)
        wide = (c + 1) * ch.rows
        key_pos = lax.broadcasted_iota(jnp.int32, (ch.rows, wide), 1)
        query_pos = lax.broadcasted_iota(jnp.int32, (ch.rows, wide), 0) + c * ch.rows
        allowed = (key_pos <= query_pos) & (key_pos < length)
        outs = []
        logs = jnp.zeros((ch.rows, LANES), F32)
        for h in range(3):
            lanes = slice(0, LANES) if h < 2 else slice(LANES, 2 * LANES)
            qh = q[:, lanes]
            if h == 0:
                qh = jnp.where(low, qh, jnp.zeros_like(qh))
            elif h == 1:
                qh = jnp.where(low, jnp.zeros_like(qh), qh)
            s = dot_nt(qh, k_s[l, 0:wide, lanes])
            s = jnp.where(allowed, s, -1e30)
            m = jnp.max(s, axis=-1, keepdims=True)
            p = jnp.exp(s - m)
            z = jnp.sum(p, axis=-1, keepdims=True)
            outs.append(dot_nn(p.astype(BF16), v_s[l, 0:wide, lanes]) / z)
            logs = jnp.where(lane == h, m + jnp.log(z), logs)
        lse[l, :, rows] = logs.T[0:8, :]
        ctx[l, rows, 0:LANES] = jnp.where(low, outs[0], outs[1]).astype(BF16)
        ctx[l, rows, LANES:2 * LANES] = outs[2].astype(BF16)
        need(2)
        part[0, c] = dot_nn(ctx[l, rows], wout[l]).astype(BF16)

    def feed(l, c):
        need(3)
        rows = ch.all(c)
        nm = nmid[l, rows]
        ff = wup.shape[2]
        for n in range(0, ff, 256):
            u = dot_nn(nm, wup[l, :, n:n + 256])
            a, g = gelu_pair(u)
            act[l, rows, n:n + 256] = a.astype(BF16)
            gpr[l, rows, n:n + 256] = g.astype(BF16)
        need(4)
        part[1, c] = dot_nn(act[l, rows], wdown[l]).astype(BF16)

    def compute(p, c):
        (attend if p % 2 == 0 else feed)(p // 2, c)

    def sum_pair(p, c):
        s = p % 2
        rs_copy(p, c).wait()
        ysend[s, c] = (part[s, c, mine, :].astype(F32) + rsbuf[s, c].astype(F32)).astype(BF16)
        y_copy(p, c).start()

    def finish(p, c):
        s, l = p % 2, p // 2
        y_copy(p, c).wait()
        rows = ch.part(c, b)
        total = ysend[s, c].astype(F32) + yrecv[s, c].astype(F32)
        if s == 0:
            before = xin[rows].astype(F32) if l == 0 else xh[c]
            middle = before + total
            midh[l, c] = middle
            nmid[l, rows] = norm_rows(middle, gain(l, 1), bias(l, 1)).astype(BF16)
        else:
            pos = lax.broadcasted_iota(jnp.int32, (ch.half, width), 0) + c * ch.rows + b * ch.half
            after = jnp.where(pos < length, midh[l, c] + total, 0.0)
            if l + 1 < layers:
                xh[c] = after
                normed[l + 1, rows] = norm_rows(after, gain(l + 1, 0), bias(l + 1, 0)).astype(BF16)
            else:
                result[rows] = after.astype(BF16)
        ag_copy(p, c).start()

    steps = [(p, c) for p in range(2 * layers) for c in range(C)]
    lag = C - 1
    for i, (p, c) in enumerate(steps):
        if p > 0:
            ag_copy(p - 1, c).wait()
        compute(p, c)
        rs_copy(p, c).start()
        if i >= lag:
            finish(*steps[i - lag])
        sum_pair(p, c)
    for i in range(len(steps) - lag, len(steps)):
        finish(*steps[i])
    for c in range(C):
        ag_copy(2 * layers - 1, c).wait()
    out = pltpu.make_async_copy(result, act_out, out_sem.at[0])
    out.start()
    out.wait()


def forward_call(mesh, lengths, x, wqkv, wout, wup, wdown, gain, bias):
    rows, width = x.shape
    layers, ff = wup.shape[0], wup.shape[2]
    C = rows // 256
    half = (C, 128, width)
    scratch = [
        pltpu.VMEM(x.shape, BF16), pltpu.VMEM(wqkv.shape, BF16), pltpu.VMEM(wout.shape, BF16),
        pltpu.VMEM(wup.shape, BF16), pltpu.VMEM(wdown.shape, BF16),
        pltpu.VMEM((layers, rows, width), BF16), pltpu.VMEM((layers, rows, width), BF16),
        pltpu.VMEM((layers, rows, 256), BF16), pltpu.VMEM((layers, rows, 256), BF16),
        pltpu.VMEM((layers, 256, rows), BF16), pltpu.VMEM((layers, rows, 256), BF16),
        pltpu.VMEM((layers, rows, 256), BF16), pltpu.VMEM((layers, 8, rows), F32),
        pltpu.VMEM(half, F32), pltpu.VMEM((layers,) + half, F32),
        pltpu.VMEM((layers, rows, ff), BF16), pltpu.VMEM((layers, rows, ff), BF16),
        pltpu.VMEM((2, C, 256, width), BF16), pltpu.VMEM((2,) + half, BF16), pltpu.VMEM((2,) + half, BF16),
        pltpu.VMEM((2,) + half, BF16), pltpu.VMEM((rows, width), BF16),
        pltpu.SemaphoreType.DMA((5,)), pltpu.SemaphoreType.DMA((2, C, 2)), pltpu.SemaphoreType.DMA((2, C, 2)),
        pltpu.SemaphoreType.DMA((2, C, 2)), pltpu.SemaphoreType.DMA((1,)),
    ]
    return pl.pallas_call(
        functools.partial(forward_kernel, mesh.shape["tensor"]),
        out_shape=jax.ShapeDtypeStruct((rows, width), BF16),
        in_specs=[SMEM, ANY, ANY, ANY, ANY, ANY, VMEM, VMEM], out_specs=ANY, scratch_shapes=scratch,
        compiler_params=pltpu.CompilerParams(collective_id=0, has_side_effects=True, vmem_limit_bytes=60 * 2**20),
        name="forward",
    )(lengths, x, wqkv, wout, wup, wdown, gain, bias)


def pad_weights(qkv_weight, out_weight):
    layers, width, three, part_width = qkv_weight.shape
    wqkv = jnp.pad(jnp.swapaxes(qkv_weight, 1, 2), ((0, 0), (0, 0), (0, 0), (0, 256 - part_width)))
    wout = jnp.pad(out_weight, ((0, 0), (0, 256 - part_width), (0, 0)))
    return wqkv, wout


def norm_rows_full(values_in, gain_row, bias_row):
    centre = values_in - jnp.mean(values_in, axis=-1, keepdims=True)
    spread = jnp.mean(centre * centre, axis=-1, keepdims=True)
    return centre * lax.rsqrt(spread + 1e-05) * gain_row + bias_row


def exact_gelu(values_in):
    return jax.nn.gelu(values_in, approximate=False)


def allowed_block(row_start, block_rows, seq_len, length_one):
    query_pos = row_start + jnp.arange(block_rows, dtype=jnp.int32)[:, None]
    key_pos = jnp.arange(seq_len, dtype=jnp.int32)[None, :]
    return (key_pos <= query_pos) & (key_pos < length_one)


def block_inputs(queries, key_rows, value_rows, lengths, block_id, per_seq, block_rows):
    seq_id = block_id // per_seq
    row_start = block_id % per_seq * block_rows
    query_seq = lax.dynamic_index_in_dim(queries, seq_id, 0, False)
    query_block = lax.dynamic_slice_in_dim(query_seq, row_start, block_rows, 0)
    keys_seq = lax.dynamic_index_in_dim(key_rows, seq_id, 0, False)
    values_seq = lax.dynamic_index_in_dim(value_rows, seq_id, 0, False)
    length_one = lax.dynamic_index_in_dim(lengths, seq_id, 0, False)
    return (seq_id, row_start, query_block, keys_seq, values_seq, length_one)


def attend_forward(queries, key_rows, value_rows, lengths, factor):
    seq_count, seq_len = (queries.shape[0], queries.shape[1])
    block_rows = min(512, seq_len)
    per_seq = seq_len // block_rows

    def one_block(block_id):
        seq_id, row_start, query_block, keys_seq, values_seq, length_one = block_inputs(
            queries, key_rows, value_rows, lengths, block_id, per_seq, block_rows
        )
        scores = (
            jnp.einsum("qhe,khe->hqk", query_block, keys_seq, preferred_element_type=jnp.float32)
            * factor
        )
        scores = jnp.where(
            allowed_block(row_start, block_rows, seq_len, length_one)[None], scores, -1e30
        )
        maximum = jnp.max(scores, axis=-1, keepdims=True)
        exponent = jnp.exp(scores - maximum)
        summed = jnp.sum(exponent, axis=-1, keepdims=True)
        softmax_low = (exponent / summed).astype(jnp.bfloat16)
        context = jnp.einsum(
            "hqk,khe->qhe", softmax_low, values_seq, preferred_element_type=jnp.float32
        )
        return (context.astype(jnp.bfloat16), (maximum + jnp.log(summed))[..., 0])

    context, log_total = lax.map(one_block, jnp.arange(seq_count * per_seq, dtype=jnp.int32))
    return (context.reshape(seq_count * seq_len, -1), log_total)


def attend_backward(queries, key_rows, value_rows, lengths, log_total, context_grad, factor):
    seq_count, seq_len = (queries.shape[0], queries.shape[1])
    block_rows = min(512, seq_len)
    per_seq = seq_len // block_rows
    zeros_acc = jnp.zeros(key_rows.shape, jnp.float32)

    def one_block(accumulated, block_id):
        key_acc, value_acc = accumulated
        seq_id, row_start, query_block, keys_seq, values_seq, length_one = block_inputs(
            queries, key_rows, value_rows, lengths, block_id, per_seq, block_rows
        )
        grad_block = lax.dynamic_slice_in_dim(
            lax.dynamic_index_in_dim(context_grad, seq_id, 0, False), row_start, block_rows, 0
        )
        scores = (
            jnp.einsum("qhe,khe->hqk", query_block, keys_seq, preferred_element_type=jnp.float32)
            * factor
        )
        scores = jnp.where(
            allowed_block(row_start, block_rows, seq_len, length_one)[None], scores, -1e30
        )
        softmax_rows = jnp.exp(
            scores - lax.dynamic_index_in_dim(log_total, block_id, 0, False)[:, :, None]
        )
        softmax_low = softmax_rows.astype(jnp.bfloat16)
        prob_grad = jnp.einsum(
            "qhe,khe->hqk", grad_block, values_seq, preferred_element_type=jnp.float32
        )
        inner_sum = jnp.sum(softmax_rows * prob_grad, axis=-1, keepdims=True)
        score_grad = (softmax_rows * (prob_grad - inner_sum)).astype(jnp.bfloat16)
        query_grad = (
            jnp.einsum("hqk,khe->qhe", score_grad, keys_seq, preferred_element_type=jnp.float32)
            * factor
        )
        key_part = (
            jnp.einsum("hqk,qhe->khe", score_grad, query_block, preferred_element_type=jnp.float32)
            * factor
        )
        value_part = jnp.einsum(
            "hqk,qhe->khe", softmax_low, grad_block, preferred_element_type=jnp.float32
        )
        key_acc = lax.dynamic_update_index_in_dim(
            key_acc, lax.dynamic_index_in_dim(key_acc, seq_id, 0, False) + key_part, seq_id, 0
        )
        value_acc = lax.dynamic_update_index_in_dim(
            value_acc, lax.dynamic_index_in_dim(value_acc, seq_id, 0, False) + value_part, seq_id, 0
        )
        return ((key_acc, value_acc), query_grad)

    (key_acc, value_acc), query_grad = lax.scan(
        one_block, (zeros_acc, zeros_acc), jnp.arange(seq_count * per_seq, dtype=jnp.int32)
    )
    return (query_grad.reshape(queries.shape), key_acc, value_acc)


def per_device(
    mesh, inputs, lengths, qkv_weight, out_weight, up_weight, down_weight, norm_gain, norm_bias, cotangent
):
    layer_total = qkv_weight.shape[0]
    row_total, width_all = inputs.shape
    seq_count = lengths.shape[0]
    seq_len = row_total // seq_count
    part_width = qkv_weight.shape[3]
    head_count = part_width // HEAD_DIM
    factor = HEAD_DIM ** (-0.5)
    positions = jnp.arange(seq_len, dtype=jnp.int32)
    valid_rows = (positions[None, :] < lengths[:, None]).astype(jnp.float32).reshape(row_total, 1)

    def group_total(partial_value):
        return lax.psum(partial_value.astype(jnp.bfloat16), "tensor").astype(jnp.float32)

    def layer_weights(layer_id):
        return (
            qkv_weight[layer_id].reshape(width_all, -1),
            out_weight[layer_id],
            up_weight[layer_id],
            down_weight[layer_id],
            norm_gain[layer_id],
            norm_bias[layer_id],
        )

    stream = inputs.astype(jnp.float32)
    stored = []
    for layer_id in range(layer_total):
        proj_qkv, proj_out, proj_up, proj_down, gain_rows, biases = layer_weights(layer_id)
        normed = norm_rows_full(stream, gain_rows[0], biases[0]).astype(jnp.bfloat16)
        projected = jnp.dot(normed, proj_qkv, preferred_element_type=jnp.float32).astype(
            jnp.bfloat16
        )
        projected = projected.reshape(seq_count, seq_len, 3, head_count, HEAD_DIM)
        queries, key_rows, value_rows = (projected[:, :, 0], projected[:, :, 1], projected[:, :, 2])
        context, log_total = attend_forward(queries, key_rows, value_rows, lengths, factor)
        middle = stream + group_total(
            jnp.dot(context, proj_out, preferred_element_type=jnp.float32)
        )
        normed_mid = norm_rows_full(middle, gain_rows[1], biases[1]).astype(jnp.bfloat16)
        hidden = jnp.dot(normed_mid, proj_up, preferred_element_type=jnp.float32)
        activated = exact_gelu(hidden).astype(jnp.bfloat16)
        stored.append(
            (stream, middle, normed, normed_mid, queries, key_rows, value_rows, context, log_total)
        )
        stream = valid_rows * (
            middle + group_total(jnp.dot(activated, proj_down, preferred_element_type=jnp.float32))
        )
    wqkv, wout = pad_weights(qkv_weight, out_weight)
    outputs = forward_call(mesh, lengths, inputs, wqkv, wout, up_weight, down_weight, norm_gain.reshape(-1, width_all), norm_bias.reshape(-1, width_all))
    upstream = cotangent.astype(jnp.float32)
    grad_layers = []
    for layer_id in reversed(range(layer_total)):
        proj_qkv, proj_out, proj_up, proj_down, gain_rows, biases = layer_weights(layer_id)
        stream_in, middle, normed, normed_mid, queries, key_rows, value_rows, context, log_total = (
            stored[layer_id]
        )
        upstream = valid_rows * upstream
        down_grad = upstream.astype(jnp.bfloat16)
        hidden = jnp.dot(normed_mid, proj_up, preferred_element_type=jnp.float32)
        activated, gelu_pull = jax.vjp(exact_gelu, hidden)
        grad_down = jnp.einsum(
            "tf,td->fd",
            activated.astype(jnp.bfloat16),
            down_grad,
            preferred_element_type=jnp.float32,
        )
        act_grad = jnp.einsum("td,fd->tf", down_grad, proj_down, preferred_element_type=jnp.float32)
        hidden_grad = gelu_pull(act_grad)[0].astype(jnp.bfloat16)
        grad_up = jnp.einsum(
            "td,tf->df", normed_mid, hidden_grad, preferred_element_type=jnp.float32
        )
        mid_norm_grad = group_total(
            jnp.einsum("tf,df->td", hidden_grad, proj_up, preferred_element_type=jnp.float32)
        )
        unused_mid, norm_pull = jax.vjp(norm_rows_full, middle, gain_rows[1], biases[1])
        middle_grad, gain_mid, bias_mid = norm_pull(mid_norm_grad)
        upstream = upstream + middle_grad
        out_grad = upstream.astype(jnp.bfloat16)
        grad_out = jnp.einsum("te,td->ed", context, out_grad, preferred_element_type=jnp.float32)
        context_grad = jnp.einsum(
            "td,ed->te", out_grad, proj_out, preferred_element_type=jnp.float32
        ).astype(jnp.bfloat16)
        context_grad = context_grad.reshape(seq_count, seq_len, head_count, HEAD_DIM)
        query_grad, key_grad, value_grad = attend_backward(
            queries, key_rows, value_rows, lengths, log_total, context_grad, factor
        )
        proj_grad = (
            jnp.stack((query_grad, key_grad, value_grad), axis=2)
            .astype(jnp.bfloat16)
            .reshape(row_total, -1)
        )
        grad_qkv = jnp.einsum(
            "td,tc->dc", normed, proj_grad, preferred_element_type=jnp.float32
        ).reshape(width_all, 3, part_width)
        in_norm_grad = group_total(
            jnp.einsum("tc,dc->td", proj_grad, proj_qkv, preferred_element_type=jnp.float32)
        )
        unused_in, norm_pull = jax.vjp(norm_rows_full, stream_in, gain_rows[0], biases[0])
        stream_grad, gain_in, bias_in = norm_pull(in_norm_grad)
        upstream = upstream + stream_grad
        grad_layers.append(
            (
                grad_qkv,
                grad_out,
                grad_up,
                grad_down,
                jnp.stack((gain_in, gain_mid)),
                jnp.stack((bias_in, bias_mid)),
            )
        )
    grad_layers = grad_layers[::-1]
    stacked = tuple((jnp.stack([entry[member] for entry in grad_layers]) for member in range(6)))
    totals = (
        lax.psum(stacked[0].astype(jnp.bfloat16), "dp").astype(jnp.float32),
        lax.psum(stacked[1].astype(jnp.bfloat16), "dp").astype(jnp.float32),
        lax.psum(stacked[2].astype(jnp.bfloat16), "dp").astype(jnp.float32),
        lax.psum(stacked[3].astype(jnp.bfloat16), "dp").astype(jnp.float32),
        lax.psum(stacked[4].astype(jnp.bfloat16), "dp").astype(jnp.float32),
        lax.psum(stacked[5].astype(jnp.bfloat16), "dp").astype(jnp.float32),
    )
    return (outputs, upstream, totals[0], totals[1], totals[2], totals[3], totals[4], totals[5])


def solution(mesh):
    in_specs = (
        P("dp", None),
        P("dp"),
        P(None, None, None, "tensor"),
        P(None, "tensor", None),
        P(None, None, "tensor"),
        P(None, "tensor", None),
        P(),
        P(),
        P("dp", None),
    )
    out_specs = (
        P("dp", None),
        P("dp", None),
        P(None, None, None, "tensor"),
        P(None, "tensor", None),
        P(None, None, "tensor"),
        P(None, "tensor", None),
        P(),
        P(),
    )
    return jax.shard_map(
        functools.partial(per_device, mesh), mesh=mesh, in_specs=in_specs, out_specs=out_specs, check_vma=False
    )
```

```python
import functools

import jax
import jax.numpy as jnp
from jax import lax
from jax.experimental import pallas as pl
from jax.experimental.pallas import tpu as pltpu
from jax.sharding import PartitionSpec as P

HEAD_DIM = 64
LANES = 128
PAD = 256
CHUNK = 256
BF16 = jnp.bfloat16
F32 = jnp.float32
MESH = pl.DeviceIdType.MESH
ANY = pl.BlockSpec(memory_space=pl.ANY)
VMEM = pl.BlockSpec(memory_space=pltpu.VMEM)
SMEM = pl.BlockSpec(memory_space=pltpu.SMEM)


def dot_nn(a, b):
    return lax.dot_general(a, b, (((1,), (0,)), ((), ())), preferred_element_type=F32)


def dot_nt(a, b):
    return lax.dot_general(a, b, (((1,), (1,)), ((), ())), preferred_element_type=F32)


def dot_tn(a, b):
    return lax.dot_general(a, b, (((0,), (0,)), ((), ())), preferred_element_type=F32)


def norm_parts(v):
    centre = v - jnp.mean(v, axis=-1, keepdims=True)
    r = lax.rsqrt(jnp.mean(centre * centre, axis=-1, keepdims=True) + 1e-05)
    return centre * r, r


def norm_rows(v, gain_row, bias_row):
    return norm_parts(v)[0] * gain_row + bias_row


def gelu_pair(u):
    bell = jnp.exp(u * u * -0.5)
    t = 1.0 / (1.0 + 0.23164189 * jnp.abs(u))
    series = t * (0.127414796 + t * (-0.142248368 + t * (0.7107068705 + t * (-0.7265760135 + t * 0.5307027145))))
    tail = series * bell
    phi_cdf = jnp.where(u >= 0.0, 1.0 - tail, tail)
    return u * phi_cdf, phi_cdf + u * bell * 0.3989422804014327


def step_kernel(n_tensor, len_ref, x_hbm, cot_hbm, wqkv_hbm, wout_hbm, wup_hbm, wdown_hbm, gain_ref, bias_ref,
                act_out, ig_out, grads_out, gnorm_out,
                xin, dzb, wqkv, wout, wup, wdown, normed, nmid, q_s, k_s, kt_s, v_s, ctx, lse, xh, midh, act, gpr,
                part, rsbuf, ysend, yrecv, dmidb, dmh, pg, dk_s, dv_s, grads, gacc,
                sems_in, rs_sem, y_sem, ag_sem, out_sem):
    layers = wqkv.shape[0]
    rows_all, width = xin.shape
    ff = wup.shape[2]
    C, half = rows_all // CHUNK, CHUNK // 2
    part_width = 3 * HEAD_DIM
    dp, t = lax.axis_index("dp"), lax.axis_index("tensor")
    b = lax.rem(t, 2)
    sib = (dp, t + 1 - 2 * b)
    peer = (dp, lax.rem(t + 2, n_tensor))
    length = len_ref[0]

    pairs = [(x_hbm, xin), (wqkv_hbm, wqkv), (wout_hbm, wout), (wup_hbm, wup), (wdown_hbm, wdown), (cot_hbm, dzb)]
    loads = [pltpu.make_async_copy(a, o, sems_in.at[i]) for i, (a, o) in enumerate(pairs)]
    for cp in loads:
        cp.start()
    waited = set()

    def need(i):
        if i not in waited:
            waited.add(i)
            loads[i].wait()

    barrier = pltpu.get_barrier_semaphore()
    for other in (sib, peer):
        pl.semaphore_signal(barrier, inc=1, device_id=other, device_id_type=MESH)
    pl.semaphore_wait(barrier, 2)

    def remote(src, dst, sem, dev):
        return pltpu.make_async_remote_copy(src_ref=src, dst_ref=dst, send_sem=sem.at[0], recv_sem=sem.at[1],
                                            device_id=dev, device_id_type=MESH)

    def chunk(c):
        return pl.ds(c * CHUNK, CHUNK)

    def mine(c):
        return pl.ds(pl.multiple_of(c * CHUNK + b * half, half), half)

    def rs_copy(o, c):
        theirs = pl.ds(pl.multiple_of((1 - b) * half, half), half)
        return remote(part.at[c, theirs], rsbuf.at[c], rs_sem.at[c], sib)

    def y_copy(o, c):
        return remote(ysend.at[c], yrecv.at[o % 2, c], y_sem.at[o % 2, c], peer)

    def ag_pair(o, c):
        rows = mine(c)
        whole = {0: nmid.at[0], 1: normed.at[1], 2: nmid.at[1], 3: dmidb, 4: dzb, 5: dmidb}
        if o in whole:
            return whole[o].at[rows], whole[o].at[rows]
        return (dmh.at[c], ig_out.at[rows]) if o == 6 else (ysend.at[c], act_out.at[rows])

    def ag_copy(o, c):
        return remote(*ag_pair(o, c), ag_sem.at[o % 2, c], sib)

    def own_copy(o, c):
        return pltpu.make_async_copy(*ag_pair(o, c), out_sem.at[o - 6, c])

    def gain(l, i):
        return gain_ref[pl.ds(2 * l + i, 1), :]

    def bias(l, i):
        return bias_ref[pl.ds(2 * l + i, 1), :]

    low = lax.broadcasted_iota(jnp.int32, (CHUNK, LANES), 1) < HEAD_DIM
    head_lanes = (slice(0, LANES), slice(0, LANES), slice(LANES, 2 * LANES))

    def one_head(v, h):
        w = v[:, head_lanes[h]]
        if h == 0:
            return jnp.where(low, w, jnp.zeros_like(w))
        return jnp.where(low, jnp.zeros_like(w), w) if h == 1 else w

    def attend(l, c):
        need(1)
        rows = chunk(c)
        if l == 0:
            need(0)
            normed[0, rows] = norm_rows(xin[rows].astype(F32), gain(0, 0), bias(0, 0)).astype(BF16)
        nc = normed[l, rows]
        q = dot_nn(nc, wqkv[l, :, 0:PAD]).astype(BF16) * jnp.asarray(HEAD_DIM ** (-0.5), BF16)
        k = dot_nn(nc, wqkv[l, :, PAD:2 * PAD])
        q_s[l, rows] = q
        k_s[l, rows] = k.astype(BF16)
        kt_s[l, :, rows] = k.T.astype(BF16)
        v_s[l, rows] = dot_nn(nc, wqkv[l, :, 2 * PAD:3 * PAD]).astype(BF16)
        wide = (c + 1) * CHUNK
        key_pos = lax.broadcasted_iota(jnp.int32, (CHUNK, wide), 1)
        query_pos = lax.broadcasted_iota(jnp.int32, (CHUNK, wide), 0) + c * CHUNK
        allowed = (key_pos <= query_pos) & (key_pos < length)
        lane = lax.broadcasted_iota(jnp.int32, (CHUNK, LANES), 1)
        outs = []
        logs = jnp.zeros((CHUNK, LANES), F32)
        for h in range(3):
            s = dot_nt(one_head(q, h), k_s[l, 0:wide, head_lanes[h]])
            s = jnp.where(allowed, s, -1e30)
            m = jnp.max(s, axis=-1, keepdims=True)
            p = jnp.exp(s - m)
            z = jnp.sum(p, axis=-1, keepdims=True)
            outs.append(dot_nn(p.astype(BF16), v_s[l, 0:wide, head_lanes[h]]) / z)
            logs = jnp.where(lane == h, m + jnp.log(z), logs)
        lse[l, :, rows] = logs.T[0:8, :]
        ctx[l, rows, 0:LANES] = jnp.where(low, outs[0], outs[1]).astype(BF16)
        ctx[l, rows, LANES:2 * LANES] = outs[2].astype(BF16)
        need(2)
        part[c] = dot_nn(ctx[l, rows], wout[l]).astype(BF16)

    def feed(l, c):
        need(3)
        need(4)
        rows = chunk(c)
        nm = nmid[l, rows]
        last = l + 1 == layers
        if last:
            need(5)
            pos = lax.broadcasted_iota(jnp.int32, (CHUNK, width), 0) + c * CHUNK
            dz = jnp.where(pos < length, dzb[rows].astype(F32), 0.0).astype(BF16)
            dzb[rows] = dz
        for n in range(0, ff, 256):
            a, g = gelu_pair(dot_nn(nm, wup[l, :, n:n + 256]))
            act[l, rows, n:n + 256] = a.astype(BF16)
            if last:
                g = g * dot_nt(dz, wdown[l, n:n + 256, :])
            gpr[l, rows, n:n + 256] = g.astype(BF16)
        if last:
            part[c] = dot_nt(gpr[l, rows], wup[l]).astype(BF16)
        else:
            part[c] = dot_nn(act[l, rows], wdown[l]).astype(BF16)

    def feed_back(l, c):
        rows = chunk(c)
        dz = dzb[rows]
        for n in range(0, ff, 256):
            g = gpr[l, rows, n:n + 256].astype(F32) * dot_nt(dz, wdown[l, n:n + 256, :])
            gpr[l, rows, n:n + 256] = g.astype(BF16)
        part[c] = dot_nt(gpr[l, rows], wup[l]).astype(BF16)

    def attend_back(l, c):
        rows = chunk(c)
        dctx = dot_nt(dmidb[rows], wout[l]).astype(BF16)
        prod = dctx.astype(F32) * ctx[l, rows].astype(F32)
        lane = lax.broadcasted_iota(jnp.int32, (CHUNK, LANES), 1)
        inner = jnp.zeros((CHUNK, LANES), F32)
        for h in range(3):
            inner = jnp.where(lane == h, jnp.sum(one_head(prod, h), axis=-1, keepdims=True), inner)
        inner = inner.T
        wide = (c + 1) * CHUNK
        key_pos = lax.broadcasted_iota(jnp.int32, (wide, CHUNK), 0)
        query_pos = lax.broadcasted_iota(jnp.int32, (wide, CHUNK), 1) + c * CHUNK
        allowed = (key_pos <= query_pos) & (key_pos < length)
        q = q_s[l, rows]
        dqs = []
        keys = slice(0, wide)
        for h in range(3):
            lanes = head_lanes[h]
            qh, dch = one_head(q, h), one_head(dctx, h)
            s = jnp.where(allowed, dot_nt(k_s[l, keys, lanes], qh), -1e30)
            p = jnp.exp(s - lse[l, h:h + 1, rows])
            dp_ = dot_nt(v_s[l, keys, lanes], dch)
            ds = (p * (dp_ - inner[h:h + 1, :])).astype(BF16)
            dv = dot_nn(p.astype(BF16), dch)
            dk = dot_nn(ds, qh)
            if c == C - 1 and h != 1:
                dv_s[keys, lanes] = dv
                dk_s[keys, lanes] = dk
            else:
                dv_s[keys, lanes] += dv
                dk_s[keys, lanes] += dk
            dqs.append(dot_nn(kt_s[l, h * HEAD_DIM:(h + 1) * HEAD_DIM, keys], ds) * HEAD_DIM ** (-0.5))
        dqs.append(jnp.zeros((PAD - part_width, CHUNK), F32))
        pg[rows, 0:PAD] = jnp.concatenate(dqs, axis=0).T.astype(BF16)
        pg[rows, PAD:2 * PAD] = dk_s[rows].astype(BF16)
        pg[rows, 2 * PAD:3 * PAD] = dv_s[rows].astype(BF16)
        part[c] = dot_nt(pg[rows], wqkv[l]).astype(BF16)

    def compute(o, c):
        if o == 7:
            part[c] = dot_nn(act[1, chunk(c)], wdown[1]).astype(BF16)
        elif o < 4:
            (attend if o % 2 == 0 else feed)(o // 2, c)
        else:
            (attend_back if o % 2 == 0 else feed_back)(1 if o == 4 else 0, c)

    up_at, down_at, out_at, qkv_at = 0, width, width + ff, width + ff + part_width

    def weights_of_feed(l):
        for m in range(0, width, 256):
            grads[l, up_at + m:up_at + m + 256] = dot_tn(nmid[l, :, m:m + 256], gpr[l]).astype(BF16)
        for m in range(0, ff, 256):
            grads[l, down_at + m:down_at + m + 256] = dot_tn(act[l, :, m:m + 256], dzb[...]).astype(BF16)

    def weights_of_attend(l):
        grads[l, out_at:out_at + part_width] = dot_tn(ctx[l], dmidb[...])[0:part_width].astype(BF16)
        for j in range(3):
            at = qkv_at + j * part_width
            grads[l, at:at + part_width] = dot_tn(pg[:, j * PAD:(j + 1) * PAD], normed[l])[0:part_width].astype(BF16)

    def sum_pair(o, c):
        rs_copy(o, c).wait()
        own = part[c, pl.ds(pl.multiple_of(b * half, half), half), :]
        ysend[c] = (own.astype(F32) + rsbuf[c].astype(F32)).astype(BF16)
        y_copy(o, c).start()

    def norm_back(l, i, v, e):
        xhat, r = norm_parts(v)
        for at, term in ((2 * l + i, e * xhat), (4 + 2 * l + i, e)):
            gacc[at] += jnp.sum(term.reshape(half // 8, 8, width), axis=0)
        eg = e * gain(l, i)
        return r * (eg - jnp.mean(eg, axis=-1, keepdims=True) - xhat * jnp.mean(eg * xhat, axis=-1, keepdims=True))

    def valid_half(c, v):
        pos = lax.broadcasted_iota(jnp.int32, (half, width), 0) + (c * CHUNK + b * half)
        return jnp.where(pos < length, v, 0.0)

    def finish(o, c):
        y_copy(o, c).wait()
        rows = mine(c)
        total = ysend[c].astype(F32) + yrecv[o % 2, c].astype(F32)
        if o in (0, 2):
            l = o // 2
            middle = (xin[rows].astype(F32) if l == 0 else xh[c]) + total
            midh[l, c] = middle
            nmid[l, rows] = norm_rows(middle, gain(l, 1), bias(l, 1)).astype(BF16)
        elif o == 1:
            after = valid_half(c, midh[0, c] + total)
            xh[c] = after
            normed[1, rows] = norm_rows(after, gain(1, 0), bias(1, 0)).astype(BF16)
        elif o in (3, 5):
            l, dz = (1, dzb[rows].astype(F32)) if o == 3 else (0, xh[c])
            dmiddle = dz + norm_back(l, 1, midh[l, c], total)
            dmh[c] = dmiddle
            dmidb[rows] = dmiddle.astype(BF16)
        elif o == 4:
            dz = valid_half(c, dmh[c] + norm_back(1, 0, xh[c], total))
            xh[c] = dz
            dzb[rows] = dz.astype(BF16)
        elif o == 6:
            dmh[c] = dmh[c] + norm_back(0, 0, xin[rows].astype(F32), total)
        else:
            ysend[c] = valid_half(c, midh[1, c] + total).astype(BF16)
        ag_copy(o, c).start()
        if o >= 6:
            own_copy(o, c).start()

    gacc[...] = jnp.zeros_like(gacc)
    pending, done = [], set()

    def finish_next():
        step = pending.pop(0)
        finish(*step)
        done.add(step)

    for o in range(8):
        for c in (range(C) if o < 4 else reversed(range(C))):
            if o > 0:
                while (o - 1, c) not in done:
                    finish_next()
                ag_copy(o - 1, c).wait()
                if o == 7:
                    own_copy(6, c).wait()
            compute(o, c)
            rs_copy(o, c).start()
            if len(pending) >= C - 1:
                finish_next()
            sum_pair(o, c)
            pending.append((o, c))
        if o in (3, 5):
            weights_of_feed(1 if o == 3 else 0)
        if o in (4, 6):
            weights_of_attend(1 if o == 4 else 0)
    while pending:
        finish_next()
    for c in range(C):
        ag_copy(7, c).wait()
        own_copy(7, c).wait()
    for i in range(8):
        gnorm_out[i:i + 1, :] = jnp.sum(gacc[i], axis=0, keepdims=True)
    out = pltpu.make_async_copy(grads, grads_out, sems_in.at[6])
    out.start()
    out.wait()


def step_call(mesh, lengths, x, cot, wqkv, wout, wup, wdown, gain, bias):
    rows, width = x.shape
    layers, ff = wup.shape[0], wup.shape[2]
    C = rows // CHUNK
    half = (C, CHUNK // 2, width)
    grads = (layers, width + ff + 4 * 3 * HEAD_DIM, width)
    two = (layers, rows, PAD)

    def vmem(shape, kind=BF16):
        return pltpu.VMEM(shape, kind)

    scratch = [
        vmem(x.shape), vmem(x.shape), vmem(wqkv.shape), vmem(wout.shape), vmem(wup.shape), vmem(wdown.shape),
        vmem((layers, rows, width)), vmem((layers, rows, width)),
        vmem(two), vmem(two), vmem((layers, PAD, rows)), vmem(two), vmem(two), vmem((layers, 8, rows), F32),
        vmem(half, F32), vmem((layers,) + half, F32), vmem((layers, rows, ff)), vmem((layers, rows, ff)),
        vmem((C, CHUNK, width)), vmem(half), vmem(half), vmem((2,) + half),
        vmem(x.shape), vmem(half, F32), vmem((rows, 3 * PAD)), vmem((rows, PAD), F32), vmem((rows, PAD), F32),
        vmem(grads), vmem((8, 8, width), F32),
        pltpu.SemaphoreType.DMA((7,)), pltpu.SemaphoreType.DMA((C, 2)), pltpu.SemaphoreType.DMA((2, C, 2)),
        pltpu.SemaphoreType.DMA((2, C, 2)), pltpu.SemaphoreType.DMA((2, C)),
    ]
    return pl.pallas_call(
        functools.partial(step_kernel, mesh.shape["tensor"]),
        out_shape=(jax.ShapeDtypeStruct(x.shape, BF16), jax.ShapeDtypeStruct(x.shape, F32),
                   jax.ShapeDtypeStruct(grads, BF16), jax.ShapeDtypeStruct((8, width), F32)),
        in_specs=[SMEM] + [ANY] * 6 + [VMEM, VMEM], out_specs=(ANY, ANY, ANY, VMEM), scratch_shapes=scratch,
        compiler_params=pltpu.CompilerParams(collective_id=0, has_side_effects=True, vmem_limit_bytes=62 * 2**20),
        name="step",
    )(lengths, x, cot, wqkv, wout, wup, wdown, gain, bias)


def per_device(
    mesh, inputs, lengths, qkv_weight, out_weight, up_weight, down_weight, norm_gain, norm_bias, cotangent
):
    layers, width, three, part_width = qkv_weight.shape
    ff = up_weight.shape[2]
    wqkv = jnp.pad(qkv_weight, ((0, 0), (0, 0), (0, 0), (0, PAD - part_width))).reshape(layers, width, three * PAD)
    wout = jnp.pad(out_weight, ((0, 0), (0, PAD - part_width), (0, 0)))
    outputs, input_grad, grads, gnorm = step_call(
        mesh, lengths, inputs, cotangent, wqkv, wout, up_weight, down_weight,
        norm_gain.reshape(2 * layers, width), norm_bias.reshape(2 * layers, width),
    )
    grads = lax.psum(grads, "dp").astype(F32)
    gnorm = lax.psum(gnorm, ("dp", "tensor")) * 0.5
    gnorm = gnorm.reshape(2, layers, 2, width)
    grad_up, grad_down, grad_out, grad_qkv = jnp.split(grads, (width, width + ff, width + ff + part_width), axis=1)
    grad_qkv = grad_qkv.reshape(layers, three, part_width, width).transpose(0, 3, 1, 2)
    return (outputs, input_grad, grad_qkv, grad_out, grad_up, grad_down, gnorm[0], gnorm[1])


def solution(mesh):
    in_specs = (
        P("dp", None),
        P("dp"),
        P(None, None, None, "tensor"),
        P(None, "tensor", None),
        P(None, None, "tensor"),
        P(None, "tensor", None),
        P(),
        P(),
        P("dp", None),
    )
    out_specs = (
        P("dp", None),
        P("dp", None),
        P(None, None, None, "tensor"),
        P(None, "tensor", None),
        P(None, None, "tensor"),
        P(None, "tensor", None),
        P(),
        P(),
    )
    return jax.shard_map(
        functools.partial(per_device, mesh), mesh=mesh, in_specs=in_specs, out_specs=out_specs, check_vma=False
    )
```

```python
import functools

import jax
import jax.numpy as jnp
from jax import lax
from jax.experimental import pallas as pl
from jax.experimental.pallas import tpu as pltpu
from jax.sharding import PartitionSpec as P

HEAD_DIM = 64
LANES = 128
PAD = 256
CHUNK = 256
STEP_US = 4.35
HOP_US = 3.0
US_PER_ROW = 0.0335
BF16 = jnp.bfloat16
F32 = jnp.float32
MESH = pl.DeviceIdType.MESH
ANY = pl.BlockSpec(memory_space=pl.ANY)
VMEM = pl.BlockSpec(memory_space=pltpu.VMEM)
SMEM = pl.BlockSpec(memory_space=pltpu.SMEM)


def dot_nn(a, b):
    return lax.dot_general(a, b, (((1,), (0,)), ((), ())), preferred_element_type=F32)


def dot_nt(a, b):
    return lax.dot_general(a, b, (((1,), (1,)), ((), ())), preferred_element_type=F32)


def dot_tn(a, b):
    return lax.dot_general(a, b, (((0,), (0,)), ((), ())), preferred_element_type=F32)


def norm_parts(v):
    centre = v - jnp.mean(v, axis=-1, keepdims=True)
    r = lax.rsqrt(jnp.mean(centre * centre, axis=-1, keepdims=True) + 1e-05)
    return centre * r, r


def norm_rows(v, gain_row, bias_row):
    return norm_parts(v)[0] * gain_row + bias_row


def gelu_pair(u):
    bell = jnp.exp(u * u * -0.5)
    t = 1.0 / (1.0 + 0.23164189 * jnp.abs(u))
    series = t * (0.127414796 + t * (-0.142248368 + t * (0.7107068705 + t * (-0.7265760135 + t * 0.5307027145))))
    tail = series * bell
    phi_cdf = jnp.where(u >= 0.0, 1.0 - tail, tail)
    return u * phi_cdf, phi_cdf + u * bell * 0.3989422804014327


def cut_pieces(rows):
    kinds = ("x", "z")
    pieces = [(kinds[i % 2], 1, at, 384) for i, at in enumerate(range(0, rows, 384))]
    late = rows - 768
    pieces += [(kinds[i % 2], 0, at, 384) for i, at in enumerate(range(0, late, 384))]
    return pieces + [(kinds[i // 2 % 2], 0, at, 192) for i, at in enumerate(range(late, rows, 192))]


def ring_free_rows(pieces):
    return sum((n if kind == "x" else n + n // 2) + n for kind, l, _, n in pieces if l == 1)


def step_kernel(n_tensor, n_dp, pieces, len_ref, x_hbm, cot_hbm, wqkv_hbm, wout_hbm, wup_hbm, wdown_hbm, gain_ref, bias_ref,
                act_out, ig_out, grads_out, gnorm_out,
                xin, dzb, wqkv, wout, wup, wdown, normed, nmid, q_s, k_s, kt_s, v_s, ctx, lse, xh, midh, act, gpr,
                part, rsbuf, ysend, yrecv, dmidb, dmh, pg, dk_s, dv_s, grads, gacc, art, nsum, nrecv,
                sems_in, rs_sem, y_sem, ag_sem, out_sem, ar_sem, own_sem, norm_sem, extra_sem, ready_sem):
    layers = wqkv.shape[0]
    rows_all, width = xin.shape
    ff = wup.shape[2]
    C, half = rows_all // CHUNK, CHUNK // 2
    part_width = 3 * HEAD_DIM
    dp, t = lax.axis_index("dp"), lax.axis_index("tensor")
    b = lax.rem(t, 2)
    sib = (dp, t + 1 - 2 * b)
    peer = (dp, lax.rem(t + 2, n_tensor))
    x_at, z_at = lax.rem(dp, 2), lax.rem(lax.div(dp, 2), 4)
    x_dev = (dp + 1 - 2 * x_at, t)
    z_dev = (dp + 2 - 4 * lax.rem(z_at, 2), t)
    mid_dev = (dp + 6 - 4 * z_at, t)
    more = [(dp + d - 2 * d * lax.rem(lax.div(dp, d), 2), t) for d in (8 * 2**i for i in range((n_dp // 8).bit_length() - 1))]
    outer = lax.rem(z_at, 3) == 0
    inner = jnp.logical_not(outer)
    z_half = lax.div(z_at, 2)
    length = len_ref[0]

    pairs = [(x_hbm, xin), (wqkv_hbm, wqkv), (wout_hbm, wout), (wup_hbm, wup), (wdown_hbm, wdown), (cot_hbm, dzb)]
    loads = [pltpu.make_async_copy(a, o, sems_in.at[i]) for i, (a, o) in enumerate(pairs)]
    for cp in loads:
        cp.start()
    waited = set()

    def need(i):
        if i not in waited:
            waited.add(i)
            loads[i].wait()

    barrier = pltpu.get_barrier_semaphore()
    greeted = [sib, peer, x_dev, z_dev, mid_dev] + more
    for other in greeted:
        pl.semaphore_signal(barrier, inc=1, device_id=other, device_id_type=MESH)
    pl.semaphore_wait(barrier, len(greeted))

    def remote(src, dst, sem, dev):
        return pltpu.make_async_remote_copy(src_ref=src, dst_ref=dst, send_sem=sem.at[0], recv_sem=sem.at[1],
                                            device_id=dev, device_id_type=MESH)

    def chunk(c):
        return pl.ds(c * CHUNK, CHUNK)

    def mine(c):
        return pl.ds(pl.multiple_of(c * CHUNK + b * half, half), half)

    def rs_copy(o, c):
        theirs = pl.ds(pl.multiple_of((1 - b) * half, half), half)
        return remote(part.at[c, theirs], rsbuf.at[c], rs_sem.at[c], sib)

    def y_copy(o, c):
        return remote(ysend.at[c], yrecv.at[o % 2, c], y_sem.at[o % 2, c], peer)

    def ag_pair(o, c):
        rows = mine(c)
        whole = {0: nmid.at[0], 1: normed.at[1], 2: nmid.at[1], 3: dmidb, 4: dzb, 5: dmidb}
        if o in whole:
            return whole[o].at[rows], whole[o].at[rows]
        return (dmh.at[c], ig_out.at[rows]) if o == 6 else (ysend.at[c], act_out.at[rows])

    def ag_copy(o, c):
        return remote(*ag_pair(o, c), ag_sem.at[o % 2, c], sib)

    def own_copy(o, c):
        return pltpu.make_async_copy(*ag_pair(o, c), out_sem.at[o - 6, c])

    def gain(l, i):
        return gain_ref[pl.ds(2 * l + i, 1), :]

    def bias(l, i):
        return bias_ref[pl.ds(2 * l + i, 1), :]

    low = lax.broadcasted_iota(jnp.int32, (CHUNK, LANES), 1) < HEAD_DIM
    head_lanes = (slice(0, LANES), slice(0, LANES), slice(LANES, 2 * LANES))

    def one_head(v, h):
        w = v[:, head_lanes[h]]
        if h == 0:
            return jnp.where(low, w, jnp.zeros_like(w))
        return jnp.where(low, jnp.zeros_like(w), w) if h == 1 else w

    def attend(l, c):
        need(1)
        rows = chunk(c)
        if l == 0:
            need(0)
            normed[0, rows] = norm_rows(xin[rows].astype(F32), gain(0, 0), bias(0, 0)).astype(BF16)
        nc = normed[l, rows]
        q = dot_nn(nc, wqkv[l, :, 0:PAD]).astype(BF16) * jnp.asarray(HEAD_DIM ** (-0.5), BF16)
        k = dot_nn(nc, wqkv[l, :, PAD:2 * PAD])
        q_s[l, rows] = q
        k_s[l, rows] = k.astype(BF16)
        kt_s[l, :, rows] = k.T.astype(BF16)
        v_s[l, rows] = dot_nn(nc, wqkv[l, :, 2 * PAD:3 * PAD]).astype(BF16)
        wide = (c + 1) * CHUNK
        key_pos = lax.broadcasted_iota(jnp.int32, (CHUNK, wide), 1)
        query_pos = lax.broadcasted_iota(jnp.int32, (CHUNK, wide), 0) + c * CHUNK
        allowed = (key_pos <= query_pos) & (key_pos < length)
        lane = lax.broadcasted_iota(jnp.int32, (CHUNK, LANES), 1)
        outs = []
        logs = jnp.zeros((CHUNK, LANES), F32)
        for h in range(3):
            s = dot_nt(one_head(q, h), k_s[l, 0:wide, head_lanes[h]])
            s = jnp.where(allowed, s, -1e30)
            m = jnp.max(s, axis=-1, keepdims=True)
            p = jnp.exp(s - m)
            z = jnp.sum(p, axis=-1, keepdims=True)
            outs.append(dot_nn(p.astype(BF16), v_s[l, 0:wide, head_lanes[h]]) / z)
            logs = jnp.where(lane == h, m + jnp.log(z), logs)
        lse[l, :, rows] = logs.T[0:8, :]
        ctx[l, rows, 0:LANES] = jnp.where(low, outs[0], outs[1]).astype(BF16)
        ctx[l, rows, LANES:2 * LANES] = outs[2].astype(BF16)
        need(2)
        part[c] = dot_nn(ctx[l, rows], wout[l]).astype(BF16)

    def feed(l, c):
        need(3)
        need(4)
        rows = chunk(c)
        nm = nmid[l, rows]
        last = l + 1 == layers
        if last:
            need(5)
            pos = lax.broadcasted_iota(jnp.int32, (CHUNK, width), 0) + c * CHUNK
            dz = jnp.where(pos < length, dzb[rows].astype(F32), 0.0).astype(BF16)
            dzb[rows] = dz
        for n in range(0, ff, 256):
            a, g = gelu_pair(dot_nn(nm, wup[l, :, n:n + 256]))
            act[l, rows, n:n + 256] = a.astype(BF16)
            if last:
                g = g * dot_nt(dz, wdown[l, n:n + 256, :])
            gpr[l, rows, n:n + 256] = g.astype(BF16)
        if last:
            part[c] = dot_nt(gpr[l, rows], wup[l]).astype(BF16)
        else:
            part[c] = dot_nn(act[l, rows], wdown[l]).astype(BF16)

    def feed_back(l, c):
        rows = chunk(c)
        dz = dzb[rows]
        for n in range(0, ff, 256):
            g = gpr[l, rows, n:n + 256].astype(F32) * dot_nt(dz, wdown[l, n:n + 256, :])
            gpr[l, rows, n:n + 256] = g.astype(BF16)
        part[c] = dot_nt(gpr[l, rows], wup[l]).astype(BF16)

    def attend_back(l, c):
        rows = chunk(c)
        dctx = dot_nt(dmidb[rows], wout[l]).astype(BF16)
        prod = dctx.astype(F32) * ctx[l, rows].astype(F32)
        lane = lax.broadcasted_iota(jnp.int32, (CHUNK, LANES), 1)
        inner = jnp.zeros((CHUNK, LANES), F32)
        for h in range(3):
            inner = jnp.where(lane == h, jnp.sum(one_head(prod, h), axis=-1, keepdims=True), inner)
        inner = inner.T
        wide = (c + 1) * CHUNK
        key_pos = lax.broadcasted_iota(jnp.int32, (wide, CHUNK), 0)
        query_pos = lax.broadcasted_iota(jnp.int32, (wide, CHUNK), 1) + c * CHUNK
        allowed = (key_pos <= query_pos) & (key_pos < length)
        q = q_s[l, rows]
        dqs = []
        keys = slice(0, wide)
        for h in range(3):
            lanes = head_lanes[h]
            qh, dch = one_head(q, h), one_head(dctx, h)
            s = jnp.where(allowed, dot_nt(k_s[l, keys, lanes], qh), -1e30)
            p = jnp.exp(s - lse[l, h:h + 1, rows])
            dp_ = dot_nt(v_s[l, keys, lanes], dch)
            ds = (p * (dp_ - inner[h:h + 1, :])).astype(BF16)
            dv = dot_nn(p.astype(BF16), dch)
            dk = dot_nn(ds, qh)
            if c == C - 1 and h != 1:
                dv_s[keys, lanes] = dv
                dk_s[keys, lanes] = dk
            else:
                dv_s[keys, lanes] += dv
                dk_s[keys, lanes] += dk
            dqs.append(dot_nn(kt_s[l, h * HEAD_DIM:(h + 1) * HEAD_DIM, keys], ds) * HEAD_DIM ** (-0.5))
        dqs.append(jnp.zeros((PAD - part_width, CHUNK), F32))
        pg[rows, 0:PAD] = jnp.concatenate(dqs, axis=0).T.astype(BF16)
        pg[rows, PAD:2 * PAD] = dk_s[rows].astype(BF16)
        pg[rows, 2 * PAD:3 * PAD] = dv_s[rows].astype(BF16)
        part[c] = dot_nt(pg[rows], wqkv[l]).astype(BF16)

    def compute(o, c):
        if o == 7:
            part[c] = dot_nn(act[1, chunk(c)], wdown[1]).astype(BF16)
        elif o < 4:
            (attend if o % 2 == 0 else feed)(o // 2, c)
        else:
            (attend_back if o % 2 == 0 else feed_back)(1 if o == 4 else 0, c)

    up_at, down_at, out_at, qkv_at = 0, width, width + ff, width + ff + part_width

    def weights_of_feed(l):
        for m in range(0, width, 384):
            grads[l, up_at + m:up_at + m + 384] = dot_tn(nmid[l, :, m:m + 384], gpr[l]).astype(BF16)
            launch(l, up_at + m)
        for m in range(0, ff, 384):
            grads[l, down_at + m:down_at + m + 384] = dot_tn(act[l, :, m:m + 384], dzb[...]).astype(BF16)
            launch(l, down_at + m)

    def weights_of_attend(l):
        grads[l, out_at:out_at + part_width] = dot_tn(ctx[l], dmidb[...])[0:part_width].astype(BF16)
        launch(l, out_at)
        for j in range(3):
            at = qkv_at + j * part_width
            grads[l, at:at + part_width] = dot_tn(pg[:, j * PAD:(j + 1) * PAD], normed[l])[0:part_width].astype(BF16)
            launch(l, at)

    def rows_at(at, n):
        return pl.ds(pl.multiple_of(at, 16), n)

    def add_rows(l, at, tmp_at, n):
        def block(i, carry):
            rows = rows_at(at + i * 96, 96)
            grads[l, rows] = (grads[l, rows].astype(F32) + art[rows_at(tmp_at + i * 96, 96)].astype(F32)).astype(BF16)
            return carry

        lax.fori_loop(0, n // 96, block, 0)

    def extra_sums(l, at, tmp_at, n):
        for i, dev in enumerate(more):
            pl.semaphore_signal(ready_sem.at[i], inc=1, device_id=dev, device_id_type=MESH)
            pl.semaphore_wait(ready_sem.at[i], 1)
            copy = remote(grads.at[l, rows_at(at, n)], art.at[pl.ds(tmp_at, n)], extra_sem.at[i], dev)
            copy.start()
            copy.wait()
            add_rows(l, at, tmp_at, n)

    class Piece:
        def __init__(self, kind, l, at, n, slot, tmp):
            self.kind, self.l, self.n, self.at, self.turn, self.ready = kind, l, n, at, 0, 0.0
            h = n // 2
            pick = x_at if kind == "x" else z_half
            self.keep, self.give = at + pick * h, at + (1 - pick) * h
            keep, give, whole = (grads.at[l, rows_at(self.keep, h)], grads.at[l, rows_at(self.give, h)], grads.at[l, pl.ds(at, n)])
            sizes = (h, h, h) if kind == "x" else (n, h, h)
            self.tmp = tmp
            land = [art.at[pl.ds(a, m)] for a, m in zip(tmp, sizes)]
            done_keep, done_give = grads_out.at[l, rows_at(self.keep, h)], grads_out.at[l, rows_at(self.give, h)]
            self.own = pltpu.make_async_copy(keep, done_keep, own_sem.at[slot])
            if kind == "x":
                ends = [(give, land[0], x_dev), (keep, land[1], z_dev), (keep, land[2], mid_dev), (keep, done_keep, z_dev),
                        (keep, done_keep, x_dev), (done_keep, done_keep, x_dev)]
            else:
                ends = [(whole, land[0], z_dev), (give, land[1], mid_dev), (keep, land[2], x_dev), (keep, done_keep, mid_dev),
                        (keep, done_keep, z_dev), (done_give, done_give, z_dev)]
            at_sem = (0, 1, 2, 3, 4, 4) if kind == "x" else (0, 1, 2, 3, 4, 5)
            self.copies = [remote(src, dst, ar_sem.at[slot, i], dev) for i, (src, dst, dev) in zip(at_sem, ends)]
            self.links = ((("x", h),), (("in", h),), (("mid", h),), (("out", h),), (("x", h),)) if kind == "x" else (
                (("in", n),), (("mid", h),), (("x", h),), (("mid", h), ("out", h)), (("out", h),))

        def step(self):
            c, l, n, h = self.copies, self.l, self.n, self.n // 2
            if self.kind == "x":
                if self.turn == 0:
                    c[0].start()
                elif self.turn == 1:
                    c[0].wait()
                    add_rows(l, self.keep, self.tmp[0], h)
                    pl.when(outer)(c[1].start)
                elif self.turn == 2:
                    @pl.when(inner)
                    def _():
                        c[1].wait_recv()
                        add_rows(l, self.keep, self.tmp[1], h)
                        c[2].start()
                    pl.when(outer)(c[1].wait_send)
                elif self.turn == 3:
                    @pl.when(inner)
                    def _():
                        c[2].wait()
                        add_rows(l, self.keep, self.tmp[2], h)
                        extra_sums(l, self.keep, self.tmp[0], h)
                        c[3].start()
                        c[4].start()
                        self.own.start()
                elif self.turn == 4:
                    @pl.when(outer)
                    def _():
                        c[3].wait_recv()
                        c[5].start()
                else:
                    @pl.when(inner)
                    def _():
                        c[3].wait_send()
                        self.own.wait()
                    c[4].wait()
            else:
                if self.turn == 0:
                    pl.when(outer)(c[0].start)
                elif self.turn == 1:
                    @pl.when(inner)
                    def _():
                        c[0].wait_recv()
                        add_rows(l, self.at, self.tmp[0], n)
                        c[1].start()
                    pl.when(outer)(c[0].wait_send)
                elif self.turn == 2:
                    @pl.when(inner)
                    def _():
                        c[1].wait()
                        add_rows(l, self.keep, self.tmp[1], h)
                        c[2].start()
                elif self.turn == 3:
                    @pl.when(inner)
                    def _():
                        c[2].wait()
                        add_rows(l, self.keep, self.tmp[2], h)
                        extra_sums(l, self.keep, self.tmp[1], h)
                        c[3].start()
                        c[4].start()
                        self.own.start()
                elif self.turn == 4:
                    @pl.when(inner)
                    def _():
                        c[3].wait()
                        c[5].start()
                else:
                    @pl.when(inner)
                    def _():
                        c[4].wait_send()
                        c[5].wait_send()
                        self.own.wait()

                    @pl.when(outer)
                    def _():
                        c[4].wait_recv()
                        c[5].wait_recv()
            if self.turn < 5:
                self.ready = 0.0
                for link, rows in self.links[self.turn]:
                    free[link] = max(clock[0], free.get(link, 0.0)) + rows * US_PER_ROW
                    self.ready = max(self.ready, free[link] + HOP_US)
            self.turn += 1

    class Norms:
        def __init__(self):
            self.turn, self.ready = 0, clock[0]
            nsum[0] = jnp.concatenate([jnp.sum(gacc[i], axis=0, keepdims=True) for i in range(8)], axis=0)
            partners = [sib, x_dev, z_dev, mid_dev] + more
            self.copies = [remote(nsum.at[i], nrecv.at[i], norm_sem.at[i], dev) for i, dev in enumerate(partners)]

        def step(self):
            i = self.turn
            if i > 0:
                self.copies[i - 1].wait()
                nsum[i] = nsum[i - 1] + nrecv[i - 1]
            if i < len(self.copies):
                self.copies[i].start()
            self.turn += 1
            self.ready = clock[0] + HOP_US

        def over(self):
            return self.turn > len(self.copies)

    clock, free, jobs, held, over = [0.0], {}, [], [], set()
    first, second, slots = {}, {}, {}
    cursor = 0
    for kind, l, at, n in pieces:
        h = n // 2
        if l == 1:
            sizes = (h, h, h) if kind == "x" else (n, h, h)
            tmp = []
            for m in sizes:
                tmp.append(cursor)
                cursor += m
            tail = cursor
            cursor += h
            slots[(l, at)] = (kind, n, len(slots), tmp, tail, None)
        else:
            (at1,) = [a for (l1, a), v in slots.items() if l1 == 1 and a <= at < a + v[1]]
            _, n1, slot1, tmp1, tail1, _ = slots[(1, at1)]
            shift = at - at1
            tmp = [tmp1[0] + (shift if kind == "z" else shift // 2), tmp1[1] + shift // 2, tail1 + shift // 2]
            slot = slot1 if shift == 0 else len(slots)
            slots[(l, at)] = (kind, n, slot, tmp, None, (1, at1))

    def launch(l, at):
        block_end = at + (384 if at < out_at else part_width)
        for (l2, at2), (kind, n, slot, tmp, _, before) in slots.items():
            if l2 == l and at < at2 + n <= block_end:
                held.append((l2, at2))
        release()

    def release():
        for key in list(held):
            kind, n, slot, tmp, _, before = slots[key]
            if before is None or before in over:
                held.remove(key)
                job = Piece(kind, key[0], key[1], n, slot, tmp)
                job.key = key
                job.step()
                jobs.append(job)

    def advance(job):
        job.step()
        if job.over() if isinstance(job, Norms) else job.turn > 5:
            jobs.remove(job)
            if isinstance(job, Piece):
                over.add(job.key)
                release()

    def serve():
        while True:
            due = [job for job in jobs if job.ready <= clock[0]]
            if not due:
                return
            advance(min(due, key=lambda job: job.ready))

    def serve_rest():
        while jobs:
            job = min(jobs, key=lambda job: job.ready)
            clock[0] = max(clock[0], job.ready) + 0.3
            advance(job)

    def sum_pair(o, c):
        rs_copy(o, c).wait()
        own = part[c, pl.ds(pl.multiple_of(b * half, half), half), :]
        ysend[c] = (own.astype(F32) + rsbuf[c].astype(F32)).astype(BF16)
        y_copy(o, c).start()

    def norm_back(l, i, v, e):
        xhat, r = norm_parts(v)
        for at, term in ((2 * l + i, e * xhat), (4 + 2 * l + i, e)):
            gacc[at] += jnp.sum(term.reshape(half // 8, 8, width), axis=0)
        eg = e * gain(l, i)
        return r * (eg - jnp.mean(eg, axis=-1, keepdims=True) - xhat * jnp.mean(eg * xhat, axis=-1, keepdims=True))

    def valid_half(c, v):
        pos = lax.broadcasted_iota(jnp.int32, (half, width), 0) + (c * CHUNK + b * half)
        return jnp.where(pos < length, v, 0.0)

    def finish(o, c):
        y_copy(o, c).wait()
        rows = mine(c)
        total = ysend[c].astype(F32) + yrecv[o % 2, c].astype(F32)
        if o in (0, 2):
            l = o // 2
            middle = (xin[rows].astype(F32) if l == 0 else xh[c]) + total
            midh[l, c] = middle
            nmid[l, rows] = norm_rows(middle, gain(l, 1), bias(l, 1)).astype(BF16)
        elif o == 1:
            after = valid_half(c, midh[0, c] + total)
            xh[c] = after
            normed[1, rows] = norm_rows(after, gain(1, 0), bias(1, 0)).astype(BF16)
        elif o in (3, 5):
            l, dz = (1, dzb[rows].astype(F32)) if o == 3 else (0, xh[c])
            dmiddle = dz + norm_back(l, 1, midh[l, c], total)
            dmh[c] = dmiddle
            dmidb[rows] = dmiddle.astype(BF16)
        elif o == 4:
            dz = valid_half(c, dmh[c] + norm_back(1, 0, xh[c], total))
            xh[c] = dz
            dzb[rows] = dz.astype(BF16)
        elif o == 6:
            dmh[c] = dmh[c] + norm_back(0, 0, xin[rows].astype(F32), total)
        else:
            ysend[c] = valid_half(c, midh[1, c] + total).astype(BF16)
        ag_copy(o, c).start()
        if o >= 6:
            own_copy(o, c).start()

    gacc[...] = jnp.zeros_like(gacc)
    pending, done = [], set()

    def finish_next():
        step = pending.pop(0)
        finish(*step)
        done.add(step)
        clock[0] += STEP_US
        if step == (6, 0):
            jobs.append(Norms())
        serve()

    for o in range(8):
        for c in (range(C) if o < 4 else reversed(range(C))):
            if o > 0:
                while (o - 1, c) not in done:
                    finish_next()
                ag_copy(o - 1, c).wait()
                if o == 7:
                    own_copy(6, c).wait()
            compute(o, c)
            rs_copy(o, c).start()
            if len(pending) >= C - 1:
                finish_next()
            sum_pair(o, c)
            pending.append((o, c))
        if o in (3, 5):
            weights_of_feed(1 if o == 3 else 0)
        if o in (4, 6):
            weights_of_attend(1 if o == 4 else 0)
    while pending:
        finish_next()
    for c in range(C):
        ag_copy(7, c).wait()
        own_copy(7, c).wait()
    serve_rest()
    gnorm_out[...] = nsum[len(greeted) - 1]


def step_call(mesh, lengths, x, cot, wqkv, wout, wup, wdown, gain, bias):
    rows, width = x.shape
    layers, ff = wup.shape[0], wup.shape[2]
    C = rows // CHUNK
    half = (C, CHUNK // 2, width)
    grads = (layers, width + ff + 4 * 3 * HEAD_DIM, width)
    pieces = cut_pieces(grads[1])
    n_dp = mesh.shape["dp"]
    hops = 4 + (n_dp // 8).bit_length() - 1
    two = (layers, rows, PAD)

    def vmem(shape, kind=BF16):
        return pltpu.VMEM(shape, kind)

    scratch = [
        vmem(x.shape), vmem(x.shape), vmem(wqkv.shape), vmem(wout.shape), vmem(wup.shape), vmem(wdown.shape),
        vmem((layers, rows, width)), vmem((layers, rows, width)),
        vmem(two), vmem(two), vmem((layers, PAD, rows)), vmem(two), vmem(two), vmem((layers, 8, rows), F32),
        vmem(half, F32), vmem((layers,) + half, F32), vmem((layers, rows, ff)), vmem((layers, rows, ff)),
        vmem((C, CHUNK, width)), vmem(half), vmem(half), vmem((2,) + half),
        vmem(x.shape), vmem(half, F32), vmem((rows, 3 * PAD)), vmem((rows, PAD), F32), vmem((rows, PAD), F32),
        vmem(grads), vmem((8, 8, width), F32), vmem((ring_free_rows(pieces), width)),
        vmem((hops + 1, 8, width), F32), vmem((hops, 8, width), F32),
        pltpu.SemaphoreType.DMA((6,)), pltpu.SemaphoreType.DMA((C, 2)), pltpu.SemaphoreType.DMA((2, C, 2)),
        pltpu.SemaphoreType.DMA((2, C, 2)), pltpu.SemaphoreType.DMA((2, C)),
        pltpu.SemaphoreType.DMA((len(pieces), 6, 2)), pltpu.SemaphoreType.DMA((len(pieces),)), pltpu.SemaphoreType.DMA((hops, 2)),
        pltpu.SemaphoreType.DMA((max(hops - 4, 1), 2)), pltpu.SemaphoreType.REGULAR((max(hops - 4, 1),)),
    ]
    return pl.pallas_call(
        functools.partial(step_kernel, mesh.shape["tensor"], n_dp, pieces),
        out_shape=(jax.ShapeDtypeStruct(x.shape, BF16), jax.ShapeDtypeStruct(x.shape, F32),
                   jax.ShapeDtypeStruct(grads, BF16), jax.ShapeDtypeStruct((8, width), F32)),
        in_specs=[SMEM] + [ANY] * 6 + [VMEM, VMEM], out_specs=(ANY, ANY, ANY, VMEM), scratch_shapes=scratch,
        compiler_params=pltpu.CompilerParams(collective_id=0, has_side_effects=True, vmem_limit_bytes=62 * 2**20),
        name="step",
    )(lengths, x, cot, wqkv, wout, wup, wdown, gain, bias)


def per_device(
    mesh, inputs, lengths, qkv_weight, out_weight, up_weight, down_weight, norm_gain, norm_bias, cotangent
):
    layers, width, three, part_width = qkv_weight.shape
    ff = up_weight.shape[2]
    wqkv = jnp.pad(qkv_weight, ((0, 0), (0, 0), (0, 0), (0, PAD - part_width))).reshape(layers, width, three * PAD)
    wout = jnp.pad(out_weight, ((0, 0), (0, PAD - part_width), (0, 0)))
    outputs, input_grad, grads, gnorm = step_call(
        mesh, lengths, inputs, cotangent, wqkv, wout, up_weight, down_weight,
        norm_gain.reshape(2 * layers, width), norm_bias.reshape(2 * layers, width),
    )
    grads = grads.astype(F32)
    gnorm = gnorm.reshape(2, layers, 2, width)
    grad_up, grad_down, grad_out, grad_qkv = jnp.split(grads, (width, width + ff, width + ff + part_width), axis=1)
    grad_qkv = grad_qkv.reshape(layers, three, part_width, width).transpose(0, 3, 1, 2)
    return (outputs, input_grad, grad_qkv, grad_out, grad_up, grad_down, gnorm[0], gnorm[1])


def solution(mesh):
    in_specs = (
        P("dp", None),
        P("dp"),
        P(None, None, None, "tensor"),
        P(None, "tensor", None),
        P(None, None, "tensor"),
        P(None, "tensor", None),
        P(),
        P(),
        P("dp", None),
    )
    out_specs = (
        P("dp", None),
        P("dp", None),
        P(None, None, None, "tensor"),
        P(None, "tensor", None),
        P(None, None, "tensor"),
        P(None, "tensor", None),
        P(),
        P(),
    )
    return jax.shard_map(
        functools.partial(per_device, mesh), mesh=mesh, in_specs=in_specs, out_specs=out_specs, check_vma=False
    )
```

```python
import functools

import jax
import jax.numpy as jnp
from jax import lax
from jax.experimental import pallas as pl
from jax.experimental.pallas import tpu as pltpu
from jax.sharding import PartitionSpec as P

HEAD_DIM = 64
LANES = 128
PAD = 256
CHUNK = 256
STEP_US = 4.6
HOP_US = 3.0
US_PER_ROW = 0.0335
PIECE = 192
ORDERS = "zzxxxxxxxxxzxxxxzxzxzzxx"
BF16 = jnp.bfloat16
F32 = jnp.float32
MESH = pl.DeviceIdType.MESH
ANY = pl.BlockSpec(memory_space=pl.ANY)
VMEM = pl.BlockSpec(memory_space=pltpu.VMEM)
SMEM = pl.BlockSpec(memory_space=pltpu.SMEM)


def dot_nn(a, b):
    return lax.dot_general(a, b, (((1,), (0,)), ((), ())), preferred_element_type=F32)


def dot_nt(a, b):
    return lax.dot_general(a, b, (((1,), (1,)), ((), ())), preferred_element_type=F32)


def dot_tn(a, b):
    return lax.dot_general(a, b, (((0,), (0,)), ((), ())), preferred_element_type=F32)


def norm_parts(v):
    centre = v - jnp.mean(v, axis=-1, keepdims=True)
    r = lax.rsqrt(jnp.mean(centre * centre, axis=-1, keepdims=True) + 1e-05)
    return centre * r, r


def norm_rows(v, gain_row, bias_row):
    return norm_parts(v)[0] * gain_row + bias_row


def gelu_pair(u):
    bell = jnp.exp(u * u * -0.5)
    t = 1.0 / (1.0 + 0.23164189 * jnp.abs(u))
    series = t * (0.127414796 + t * (-0.142248368 + t * (0.7107068705 + t * (-0.7265760135 + t * 0.5307027145))))
    tail = series * bell
    phi_cdf = jnp.where(u >= 0.0, 1.0 - tail, tail)
    return u * phi_cdf, phi_cdf + u * bell * 0.3989422804014327


def cut_pieces(rows, late):
    return [(ORDERS[i], 1 - i // (rows // PIECE), i % (rows // PIECE) * PIECE, PIECE) for i in range(2 * rows // PIECE)]


def takes_over(pieces, i, late):
    kind, l, at, n = pieces[i]
    if l == 1 or at < late:
        return None
    return next(k for k, p in enumerate(pieces) if p == (kind, 1, at - late, n))


def scratch_rows(pieces, late):
    total = 0
    for i, (kind, _, _, n) in enumerate(pieces):
        total += n // 2 if takes_over(pieces, i, late) is not None else (3 * n // 2 if kind == "x" else 2 * n)
    return total


def step_kernel(n_tensor, n_dp, pieces, len_ref, x_hbm, cot_hbm, wqkv_hbm, wout_hbm, wup_hbm, wdown_hbm, gain_ref, bias_ref,
                act_out, ig_out, grads_out, ggain_out, gbias_out,
                xin, dzb, wqkv, wout, wup, wdown, normed, nmid, q_s, k_s, kt_s, v_s, ctx, lse, xh, midh, act, gpr,
                part, rsbuf, ysend, yrecv, dmidb, dmh, dk_s, dv_s, grads, gacc, art, nsum, nrecv,
                sems_in, rs_sem, y_sem, ag_sem, out_sem, ar_sem, own_sem, norm_sem, extra_sem, ready_sem):
    layers = wqkv.shape[0]
    rows_all, width = xin.shape
    ff = wup.shape[2]
    C, half = rows_all // CHUNK, CHUNK // 2
    part_width = 3 * HEAD_DIM
    dp, t = lax.axis_index("dp"), lax.axis_index("tensor")
    b = lax.rem(t, 2)
    sib = (dp, t + 1 - 2 * b)
    peer = (dp, lax.rem(t + 2, n_tensor))
    x_at, z_at = lax.rem(dp, 2), lax.rem(lax.div(dp, 2), 4)
    x_dev = (dp + 1 - 2 * x_at, t)
    z_dev = (dp + 2 - 4 * lax.rem(z_at, 2), t)
    mid_dev = (dp + 6 - 4 * z_at, t)
    more = [(dp + d - 2 * d * lax.rem(lax.div(dp, d), 2), t) for d in (8 * 2**i for i in range((n_dp // 8).bit_length() - 1))]
    outer = lax.rem(z_at, 3) == 0
    inner = jnp.logical_not(outer)
    z_half = lax.div(z_at, 2)
    length = len_ref[0]

    pairs = [(x_hbm, xin)]
    for l in range(layers):
        for j in range(3):
            pairs.append((wqkv_hbm.at[l, pl.ds(j * part_width, part_width)], wqkv.at[l, pl.ds(j * PAD, part_width)]))
    pairs += [(wout_hbm.at[l], wout.at[l, pl.ds(0, part_width)]) for l in range(layers)]
    pairs += [(wup_hbm, wup), (wdown_hbm, wdown), (cot_hbm, dzb)]
    loads = [pltpu.make_async_copy(a, o, sems_in.at[i]) for i, (a, o) in enumerate(pairs)]
    need_x, need_qkv, need_out, need_up, need_down, need_cot = 0, 1, 1 + 3 * layers, 1 + 4 * layers, 2 + 4 * layers, 3 + 4 * layers
    for cp in loads:
        cp.start()
    for l in range(layers):
        for j in range(3):
            wqkv[l, j * PAD + part_width:(j + 1) * PAD] = jnp.zeros((PAD - part_width, width), BF16)
        wout[l, part_width:PAD] = jnp.zeros((PAD - part_width, width), BF16)
    pg = gpr.at[layers - 1]
    waited = set()

    def need(i):
        if i not in waited:
            waited.add(i)
            loads[i].wait()

    barrier = pltpu.get_barrier_semaphore()
    greeted = [sib, peer, x_dev, z_dev, mid_dev] + more
    for other in greeted:
        pl.semaphore_signal(barrier, inc=1, device_id=other, device_id_type=MESH)
    pl.semaphore_wait(barrier, len(greeted))

    def remote(src, dst, sem, dev):
        return pltpu.make_async_remote_copy(src_ref=src, dst_ref=dst, send_sem=sem.at[0], recv_sem=sem.at[1],
                                            device_id=dev, device_id_type=MESH)

    def chunk(c):
        return pl.ds(c * CHUNK, CHUNK)

    def mine(c):
        return pl.ds(pl.multiple_of(c * CHUNK + b * half, half), half)

    def rs_copy(o, c):
        theirs = pl.ds(pl.multiple_of((1 - b) * half, half), half)
        return remote(part.at[c, theirs], rsbuf.at[c], rs_sem.at[c], sib)

    def y_copy(o, c):
        return remote(ysend.at[c], yrecv.at[o % 2, c], y_sem.at[o % 2, c], peer)

    def ag_pair(o, c):
        rows = mine(c)
        whole = {0: nmid.at[0], 1: normed.at[1], 2: nmid.at[1], 3: dmidb, 4: dzb, 5: dmidb}
        if o in whole:
            return whole[o].at[rows], whole[o].at[rows]
        return (dmh.at[c], ig_out.at[rows]) if o == 6 else (ysend.at[c], act_out.at[rows])

    def ag_copy(o, c):
        return remote(*ag_pair(o, c), ag_sem.at[o % 2, c], sib)

    def own_copy(o, c):
        return pltpu.make_async_copy(*ag_pair(o, c), out_sem.at[o - 6, c])

    def gain(l, i):
        return gain_ref[l, i:i + 1, :]

    def bias(l, i):
        return bias_ref[l, i:i + 1, :]

    low = lax.broadcasted_iota(jnp.int32, (CHUNK, LANES), 1) < HEAD_DIM
    head_lanes = (slice(0, LANES), slice(0, LANES), slice(LANES, 2 * LANES))

    def one_head(v, h):
        w = v[:, head_lanes[h]]
        if h == 0:
            return jnp.where(low, w, jnp.zeros_like(w))
        return jnp.where(low, jnp.zeros_like(w), w) if h == 1 else w

    def attend(l, c):
        for j in range(3):
            need(need_qkv + 3 * l + j)
        rows = chunk(c)
        if l == 0:
            need(need_x)
            normed[0, rows] = norm_rows(xin[rows].astype(F32), gain(0, 0), bias(0, 0)).astype(BF16)
        nc = normed[l, rows]
        q = dot_nt(nc, wqkv[l, 0:PAD]).astype(BF16) * jnp.asarray(HEAD_DIM ** (-0.5), BF16)
        k = dot_nt(nc, wqkv[l, PAD:2 * PAD])
        q_s[l, rows] = q
        k_s[l, rows] = k.astype(BF16)
        kt_s[l, :, rows] = k.T.astype(BF16)
        v_s[l, rows] = dot_nt(nc, wqkv[l, 2 * PAD:3 * PAD]).astype(BF16)
        wide = (c + 1) * CHUNK
        key_pos = lax.broadcasted_iota(jnp.int32, (CHUNK, wide), 1)
        query_pos = lax.broadcasted_iota(jnp.int32, (CHUNK, wide), 0) + c * CHUNK
        allowed = (key_pos <= query_pos) & (key_pos < length)
        lane = lax.broadcasted_iota(jnp.int32, (CHUNK, LANES), 1)
        outs = []
        logs = jnp.zeros((CHUNK, LANES), F32)
        for h in range(3):
            s = dot_nt(one_head(q, h), k_s[l, 0:wide, head_lanes[h]])
            s = jnp.where(allowed, s, -1e30)
            m = jnp.max(s, axis=-1, keepdims=True)
            p = jnp.exp(s - m)
            z = jnp.sum(p, axis=-1, keepdims=True)
            outs.append(dot_nn(p.astype(BF16), v_s[l, 0:wide, head_lanes[h]]) / z)
            logs = jnp.where(lane == h, m + jnp.log(z), logs)
        lse[l, :, rows] = logs.T[0:8, :]
        ctx[l, rows, 0:LANES] = jnp.where(low, outs[0], outs[1]).astype(BF16)
        ctx[l, rows, LANES:2 * LANES] = outs[2].astype(BF16)
        need(need_out + l)
        part[c] = dot_nn(ctx[l, rows], wout[l]).astype(BF16)

    def feed(l, c):
        need(need_up)
        need(need_down)
        rows = chunk(c)
        nm = nmid[l, rows]
        last = l + 1 == layers
        if last:
            need(need_cot)
            pos = lax.broadcasted_iota(jnp.int32, (CHUNK, width), 0) + c * CHUNK
            dz = jnp.where(pos < length, dzb[rows].astype(F32), 0.0).astype(BF16)
            dzb[rows] = dz
        for n in range(0, ff, 256):
            a, g = gelu_pair(dot_nn(nm, wup[l, :, n:n + 256]))
            act[l, rows, n:n + 256] = a.astype(BF16)
            if last:
                g = g * dot_nt(dz, wdown[l, n:n + 256, :])
            gpr[l, rows, n:n + 256] = g.astype(BF16)
        if last:
            part[c] = dot_nt(gpr[l, rows], wup[l]).astype(BF16)
        else:
            part[c] = dot_nn(act[l, rows], wdown[l]).astype(BF16)

    def feed_back(l, c):
        rows = chunk(c)
        dz = dzb[rows]
        for n in range(0, ff, 256):
            g = gpr[l, rows, n:n + 256].astype(F32) * dot_nt(dz, wdown[l, n:n + 256, :])
            gpr[l, rows, n:n + 256] = g.astype(BF16)
        part[c] = dot_nt(gpr[l, rows], wup[l]).astype(BF16)

    def attend_back(l, c):
        rows = chunk(c)
        dctx = dot_nt(dmidb[rows], wout[l]).astype(BF16)
        prod = dctx.astype(F32) * ctx[l, rows].astype(F32)
        lane = lax.broadcasted_iota(jnp.int32, (CHUNK, LANES), 1)
        inner = jnp.zeros((CHUNK, LANES), F32)
        for h in range(3):
            inner = jnp.where(lane == h, jnp.sum(one_head(prod, h), axis=-1, keepdims=True), inner)
        inner = inner.T
        wide = (c + 1) * CHUNK
        key_pos = lax.broadcasted_iota(jnp.int32, (wide, CHUNK), 0)
        query_pos = lax.broadcasted_iota(jnp.int32, (wide, CHUNK), 1) + c * CHUNK
        allowed = (key_pos <= query_pos) & (key_pos < length)
        q = q_s[l, rows]
        dqs = []
        keys = slice(0, wide)
        for h in range(3):
            lanes = head_lanes[h]
            qh, dch = one_head(q, h), one_head(dctx, h)
            s = jnp.where(allowed, dot_nt(k_s[l, keys, lanes], qh), -1e30)
            p = jnp.exp(s - lse[l, h:h + 1, rows])
            dp_ = dot_nt(v_s[l, keys, lanes], dch)
            ds = (p * (dp_ - inner[h:h + 1, :])).astype(BF16)
            dv = dot_nn(p.astype(BF16), dch)
            dk = dot_nn(ds, qh)
            if c == C - 1 and h != 1:
                dv_s[keys, lanes] = dv
                dk_s[keys, lanes] = dk
            else:
                dv_s[keys, lanes] += dv
                dk_s[keys, lanes] += dk
            dqs.append(dot_nn(kt_s[l, h * HEAD_DIM:(h + 1) * HEAD_DIM, keys], ds) * HEAD_DIM ** (-0.5))
        dqs.append(jnp.zeros((PAD - part_width, CHUNK), F32))
        pg[rows, 0:PAD] = jnp.concatenate(dqs, axis=0).T.astype(BF16)
        pg[rows, PAD:2 * PAD] = dk_s[rows].astype(BF16)
        pg[rows, 2 * PAD:3 * PAD] = dv_s[rows].astype(BF16)
        part[c] = dot_nn(pg[rows], wqkv[l]).astype(BF16)

    def compute(o, c):
        if o == 7:
            part[c] = dot_nn(act[1, chunk(c)], wdown[1]).astype(BF16)
        elif o < 4:
            (attend if o % 2 == 0 else feed)(o // 2, c)
        else:
            (attend_back if o % 2 == 0 else feed_back)(1 if o == 4 else 0, c)

    up_at, down_at, out_at, qkv_at = 0, width, width + ff, width + ff + part_width

    def weights_of_feed(l):
        for m in range(0, width, 384):
            grads[l, up_at + m:up_at + m + 384] = dot_tn(nmid[l, :, m:m + 384], gpr[l]).astype(BF16)
            launch(l, up_at + m)
        for m in range(0, ff, 384):
            grads[l, down_at + m:down_at + m + 384] = dot_tn(act[l, :, m:m + 384], dzb[...]).astype(BF16)
            launch(l, down_at + m)

    def weights_of_attend(l):
        grads[l, out_at:out_at + part_width] = dot_tn(ctx[l], dmidb[...])[0:part_width].astype(BF16)
        launch(l, out_at)
        for j in range(3):
            at = qkv_at + j * part_width
            grads[l, at:at + part_width] = dot_tn(gpr[layers - 1, :, j * PAD:(j + 1) * PAD], normed[l])[0:part_width].astype(BF16)
            launch(l, at)

    def rows_at(at, n):
        return pl.ds(pl.multiple_of(at, 16), n)

    def add_rows(l, at, tmp_at, n):
        def block(i, carry):
            rows = rows_at(at + i * 96, 96)
            grads[l, rows] = (grads[l, rows].astype(F32) + art[rows_at(tmp_at + i * 96, 96)].astype(F32)).astype(BF16)
            return carry

        lax.fori_loop(0, n // 96, block, 0)

    def extra_sums(l, at, tmp_at, n):
        for i, dev in enumerate(more):
            pl.semaphore_signal(ready_sem.at[i], inc=1, device_id=dev, device_id_type=MESH)
            pl.semaphore_wait(ready_sem.at[i], 1)
            copy = remote(grads.at[l, rows_at(at, n)], art.at[pl.ds(tmp_at, n)], extra_sem.at[i], dev)
            copy.start()
            copy.wait()
            add_rows(l, at, tmp_at, n)

    class Piece:
        def __init__(self, kind, l, at, n, slot, tmp):
            self.kind, self.l, self.n, self.at, self.turn, self.ready = kind, l, n, at, 0, 0.0
            h = n // 2
            pick = x_at if kind == "x" else z_half
            self.keep, self.give = at + pick * h, at + (1 - pick) * h
            keep, give, whole = (grads.at[l, rows_at(self.keep, h)], grads.at[l, rows_at(self.give, h)], grads.at[l, pl.ds(at, n)])
            sizes = (h, h, h) if kind == "x" else (n, h, h)
            self.tmp = tmp
            land = [art.at[pl.ds(a, m)] for a, m in zip(tmp, sizes)]
            done_keep, done_give = grads_out.at[l, rows_at(self.keep, h)], grads_out.at[l, rows_at(self.give, h)]
            self.own = pltpu.make_async_copy(keep, done_keep, own_sem.at[slot])
            if kind == "x":
                ends = [(give, land[0], x_dev), (keep, land[1], z_dev), (keep, land[2], mid_dev), (keep, done_keep, z_dev),
                        (keep, done_keep, x_dev), (done_keep, done_keep, x_dev)]
            else:
                ends = [(whole, land[0], z_dev), (give, land[1], mid_dev), (keep, land[2], x_dev), (keep, done_keep, mid_dev),
                        (keep, done_keep, z_dev), (done_give, done_give, z_dev)]
            at_sem = (0, 1, 2, 3, 4, 4) if kind == "x" else (0, 1, 2, 3, 4, 5)
            self.copies = [remote(src, dst, ar_sem.at[slot, i], dev) for i, (src, dst, dev) in zip(at_sem, ends)]
            self.links = ((("x", h),), (("in", h),), (("mid", h),), (("out", h),), (("x", h),)) if kind == "x" else (
                (("in", n),), (("mid", h),), (("x", h),), (("mid", h), ("out", h)), (("out", h),))

        def step(self):
            c, l, n, h = self.copies, self.l, self.n, self.n // 2
            if self.kind == "x":
                if self.turn == 0:
                    c[0].start()
                elif self.turn == 1:
                    c[0].wait()
                    add_rows(l, self.keep, self.tmp[0], h)
                    pl.when(outer)(c[1].start)
                elif self.turn == 2:
                    @pl.when(inner)
                    def _():
                        c[1].wait_recv()
                        add_rows(l, self.keep, self.tmp[1], h)
                        c[2].start()
                    pl.when(outer)(c[1].wait_send)
                elif self.turn == 3:
                    @pl.when(inner)
                    def _():
                        c[2].wait()
                        add_rows(l, self.keep, self.tmp[2], h)
                        extra_sums(l, self.keep, self.tmp[0], h)
                        c[3].start()
                        c[4].start()
                        self.own.start()
                elif self.turn == 4:
                    @pl.when(outer)
                    def _():
                        c[3].wait_recv()
                        c[5].start()
                else:
                    @pl.when(inner)
                    def _():
                        c[3].wait_send()
                        self.own.wait()
                    c[4].wait()
            else:
                if self.turn == 0:
                    pl.when(outer)(c[0].start)
                elif self.turn == 1:
                    @pl.when(inner)
                    def _():
                        c[0].wait_recv()
                        add_rows(l, self.at, self.tmp[0], n)
                        c[1].start()
                    pl.when(outer)(c[0].wait_send)
                elif self.turn == 2:
                    @pl.when(inner)
                    def _():
                        c[1].wait()
                        add_rows(l, self.keep, self.tmp[1], h)
                        c[2].start()
                elif self.turn == 3:
                    @pl.when(inner)
                    def _():
                        c[2].wait()
                        add_rows(l, self.keep, self.tmp[2], h)
                        extra_sums(l, self.keep, self.tmp[1], h)
                        c[3].start()
                        c[4].start()
                        self.own.start()
                elif self.turn == 4:
                    @pl.when(inner)
                    def _():
                        c[3].wait()
                        c[5].start()
                else:
                    @pl.when(inner)
                    def _():
                        c[4].wait_send()
                        c[5].wait_send()
                        self.own.wait()

                    @pl.when(outer)
                    def _():
                        c[4].wait_recv()
                        c[5].wait_recv()
            if self.turn < 5:
                self.ready = 0.0
                for link, rows in self.links[self.turn]:
                    free[link] = max(clock[0], free.get(link, 0.0)) + rows * US_PER_ROW
                    self.ready = max(self.ready, free[link] + HOP_US)
            self.turn += 1

    class Norms:
        def __init__(self):
            self.turn, self.ready = 0, clock[0]
            nsum[0] = jnp.concatenate([jnp.sum(gacc[i], axis=0, keepdims=True) for i in range(8)], axis=0)
            partners = [sib, x_dev, z_dev, mid_dev] + more
            self.copies = [remote(nsum.at[i], nrecv.at[i], norm_sem.at[i], dev) for i, dev in enumerate(partners)]

        def step(self):
            i = self.turn
            if i > 0:
                self.copies[i - 1].wait()
                nsum[i] = nsum[i - 1] + nrecv[i - 1]
            if i < len(self.copies):
                self.copies[i].start()
            self.turn += 1
            self.ready = clock[0] + HOP_US

        def over(self):
            return self.turn > len(self.copies)

    clock, free, jobs, held, over = [0.0], {}, [], [], set()
    slots = {}
    cursor = 0
    for i, (kind, l, at, n) in enumerate(pieces):
        before = takes_over(pieces, i, out_at)
        sizes = (n // 2,) * 3 if kind == "x" else (n, n // 2, n // 2)
        tmp = []
        if before is not None:
            tmp, sizes = slots[pieces[before][1:3]][3][0:2], sizes[2:]
        for m in sizes:
            tmp = tmp + [cursor]
            cursor += m
        slots[(l, at)] = (kind, n, i, tmp, None, None if before is None else pieces[before][1:3])

    def launch(l, at):
        block_end = at + (384 if at < out_at else part_width)
        for (l2, at2), (kind, n, slot, tmp, _, before) in slots.items():
            if l2 == l and at < at2 + n <= block_end:
                held.append((l2, at2))
        release()

    def release():
        for key in list(held):
            kind, n, slot, tmp, _, before = slots[key]
            if before is None or before in over:
                held.remove(key)
                job = Piece(kind, key[0], key[1], n, slot, tmp)
                job.key = key
                job.step()
                jobs.append(job)

    def advance(job):
        job.step()
        if job.over() if isinstance(job, Norms) else job.turn > 5:
            jobs.remove(job)
            if isinstance(job, Piece):
                over.add(job.key)
                release()

    def serve():
        while True:
            due = [job for job in jobs if job.ready <= clock[0]]
            if not due:
                return
            advance(min(due, key=lambda job: job.ready))

    def serve_rest():
        while jobs:
            job = min(jobs, key=lambda job: job.ready)
            clock[0] = max(clock[0], job.ready) + 0.3
            advance(job)

    def sum_pair(o, c):
        rs_copy(o, c).wait()
        own = part[c, pl.ds(pl.multiple_of(b * half, half), half), :]
        ysend[c] = (own.astype(F32) + rsbuf[c].astype(F32)).astype(BF16)
        y_copy(o, c).start()

    def norm_back(l, i, v, e):
        xhat, r = norm_parts(v)
        for at, term in ((2 * l + i, e * xhat), (4 + 2 * l + i, e)):
            gacc[at] += jnp.sum(term.reshape(half // 8, 8, width), axis=0)
        eg = e * gain(l, i)
        return r * (eg - jnp.mean(eg, axis=-1, keepdims=True) - xhat * jnp.mean(eg * xhat, axis=-1, keepdims=True))

    def valid_half(c, v):
        pos = lax.broadcasted_iota(jnp.int32, (half, width), 0) + (c * CHUNK + b * half)
        return jnp.where(pos < length, v, 0.0)

    def finish(o, c):
        y_copy(o, c).wait()
        rows = mine(c)
        total = ysend[c].astype(F32) + yrecv[o % 2, c].astype(F32)
        if o in (0, 2):
            l = o // 2
            middle = (xin[rows].astype(F32) if l == 0 else xh[c]) + total
            midh[l, c] = middle
            nmid[l, rows] = norm_rows(middle, gain(l, 1), bias(l, 1)).astype(BF16)
        elif o == 1:
            after = valid_half(c, midh[0, c] + total)
            xh[c] = after
            normed[1, rows] = norm_rows(after, gain(1, 0), bias(1, 0)).astype(BF16)
        elif o in (3, 5):
            l, dz = (1, dzb[rows].astype(F32)) if o == 3 else (0, xh[c])
            dmiddle = dz + norm_back(l, 1, midh[l, c], total)
            dmh[c] = dmiddle
            dmidb[rows] = dmiddle.astype(BF16)
        elif o == 4:
            dz = valid_half(c, dmh[c] + norm_back(1, 0, xh[c], total))
            xh[c] = dz
            dzb[rows] = dz.astype(BF16)
        elif o == 6:
            dmh[c] = dmh[c] + norm_back(0, 0, xin[rows].astype(F32), total)
        else:
            ysend[c] = valid_half(c, midh[1, c] + total).astype(BF16)
        ag_copy(o, c).start()
        if o >= 6:
            own_copy(o, c).start()

    gacc[...] = jnp.zeros_like(gacc)
    pending, done = [], set()

    def finish_next(paired=False):
        step = pending.pop(0)
        finish(*step)
        done.add(step)
        clock[0] += STEP_US / 2 if paired else STEP_US
        if step == (6, 0):
            jobs.append(Norms())
        serve()

    for o in range(8):
        for c in (range(C) if o < 4 else reversed(range(C))):
            if o > 0:
                while (o - 1, c) not in done:
                    finish_next()
                ag_copy(o - 1, c).wait()
                if o == 7:
                    own_copy(6, c).wait()
            compute(o, c)
            rs_copy(o, c).start()
            if o >= 4:
                clock[0] += STEP_US / 2
                serve()
            if len(pending) >= C - 1:
                finish_next(True)
            sum_pair(o, c)
            pending.append((o, c))
        if o == 3:
            clock[0] = 0.0
        if o in (3, 5):
            weights_of_feed(1 if o == 3 else 0)
        if o in (4, 6):
            weights_of_attend(1 if o == 4 else 0)
    while pending:
        finish_next()
    for c in range(C):
        ag_copy(7, c).wait()
        own_copy(7, c).wait()
    serve_rest()
    norms = nsum[len(greeted) - 1]
    for i in range(2 * layers):
        ggain_out[i // 2, i % 2:i % 2 + 1, :] = norms[i:i + 1]
        gbias_out[i // 2, i % 2:i % 2 + 1, :] = norms[4 + i:5 + i]


def step_call(mesh, lengths, x, cot, wqkv, wout, wup, wdown, gain, bias):
    rows, width = x.shape
    layers, ff = wup.shape[0], wup.shape[2]
    C = rows // CHUNK
    half = (C, CHUNK // 2, width)
    grads = (layers, width + ff + 4 * 3 * HEAD_DIM, width)
    pieces = cut_pieces(grads[1], width + ff)
    n_dp = mesh.shape["dp"]
    hops = 4 + (n_dp // 8).bit_length() - 1
    two = (layers, rows, PAD)

    def vmem(shape, kind=BF16):
        return pltpu.VMEM(shape, kind)

    scratch = [
        vmem(x.shape), vmem(x.shape), vmem((layers, 3 * PAD, width)), vmem((layers, PAD, width)), vmem(wup.shape), vmem(wdown.shape),
        vmem((layers, rows, width)), vmem((layers, rows, width)),
        vmem(two), vmem(two), vmem((layers, PAD, rows)), vmem(two), vmem(two), vmem((layers, 8, rows), F32),
        vmem(half, F32), vmem((layers,) + half, F32), vmem((layers, rows, ff)), vmem((layers, rows, ff)),
        vmem((C, CHUNK, width)), vmem(half), vmem(half), vmem((2,) + half),
        vmem(x.shape), vmem(half, F32), vmem((rows, PAD), F32), vmem((rows, PAD), F32),
        vmem(grads), vmem((8, 8, width), F32), vmem((scratch_rows(pieces, width + ff), width)),
        vmem((hops + 1, 8, width), F32), vmem((hops, 8, width), F32),
        pltpu.SemaphoreType.DMA((4 + 4 * layers,)), pltpu.SemaphoreType.DMA((C, 2)), pltpu.SemaphoreType.DMA((2, C, 2)),
        pltpu.SemaphoreType.DMA((2, C, 2)), pltpu.SemaphoreType.DMA((2, C)),
        pltpu.SemaphoreType.DMA((len(pieces), 6, 2)), pltpu.SemaphoreType.DMA((len(pieces),)), pltpu.SemaphoreType.DMA((hops, 2)),
        pltpu.SemaphoreType.DMA((max(hops - 4, 1), 2)), pltpu.SemaphoreType.REGULAR((max(hops - 4, 1),)),
    ]
    return pl.pallas_call(
        functools.partial(step_kernel, mesh.shape["tensor"], n_dp, pieces),
        out_shape=(jax.ShapeDtypeStruct(x.shape, BF16), jax.ShapeDtypeStruct(x.shape, F32),
                   jax.ShapeDtypeStruct(grads, BF16),
                   jax.ShapeDtypeStruct(gain.shape, F32), jax.ShapeDtypeStruct(gain.shape, F32)),
        in_specs=[SMEM] + [ANY] * 6 + [VMEM, VMEM], out_specs=(ANY, ANY, ANY, VMEM, VMEM), scratch_shapes=scratch,
        compiler_params=pltpu.CompilerParams(collective_id=0, has_side_effects=True, vmem_limit_bytes=62 * 2**20),
        name="step",
    )(lengths, x, cot, wqkv, wout, wup, wdown, gain, bias)


def per_device(
    mesh, inputs, lengths, qkv_weight, out_weight, up_weight, down_weight, norm_gain, norm_bias, cotangent
):
    layers, width, three, part_width = qkv_weight.shape
    ff = up_weight.shape[2]
    outputs, input_grad, grads, grad_gain, grad_bias = step_call(
        mesh, lengths, inputs, cotangent, qkv_weight.transpose(0, 2, 3, 1).reshape(layers, three * part_width, width),
        out_weight, up_weight, down_weight, norm_gain, norm_bias,
    )
    outputs, input_grad, grad_up, grad_down, grad_out, grad_qkv = widen_call(outputs, input_grad, grads, ff, part_width)
    grad_qkv = grad_qkv.reshape(layers, three, part_width, width).transpose(0, 3, 1, 2)
    return (outputs, input_grad, grad_qkv, grad_out, grad_up, grad_down, grad_gain, grad_bias)


def widen_kernel(spans, act_in, ig_in, grads_in, act_out, ig_out, *rest):
    outs, (act, ig, low, wide, sem_in, sem_out) = rest[:len(spans)], rest[len(spans):]
    layers = grads_in.shape[0]
    through = [(act_in, act, act_out), (ig_in, ig, ig_out)]
    blocks = [(l, k, at, at + i, n) for k, (at, rows, n) in enumerate(spans) for l in range(layers) for i in range(0, rows, n)]
    into = [pltpu.make_async_copy(grads_in.at[l, pl.ds(r, n)], low.at[l, pl.ds(r, n)], sem_in.at[i]) for i, (l, _, _, r, n) in enumerate(blocks)]
    into += [pltpu.make_async_copy(a, v, sem_in.at[len(blocks) + i]) for i, (a, v, _) in enumerate(through)]
    for copy in into:
        copy.start()
    back = []
    for i, (l, k, at, r, n) in enumerate(blocks):
        into[i].wait()
        wide[l, pl.ds(r, n)] = low[l, pl.ds(r, n)].astype(F32)
        back.append(pltpu.make_async_copy(wide.at[l, pl.ds(r, n)], outs[k].at[l, pl.ds(r - at, n)], sem_out.at[i]))
        back[-1].start()
    for i, (_, v, o) in enumerate(through):
        into[len(blocks) + i].wait()
        back.append(pltpu.make_async_copy(v, o, sem_out.at[len(blocks) + i]))
        back[-1].start()
    for copy in back:
        copy.wait()


def widen_call(outputs, input_grad, grads, ff, part_width):
    layers, _, width = grads.shape
    spans, at = [], 0
    for rows in (width, ff, part_width, 3 * part_width):
        spans.append((at, rows, PIECE))
        at += rows
    count = sum(layers * rows // n for _, rows, n in spans) + 2
    return pl.pallas_call(
        functools.partial(widen_kernel, spans),
        out_shape=(jax.ShapeDtypeStruct(outputs.shape, BF16), jax.ShapeDtypeStruct(input_grad.shape, F32))
        + tuple(jax.ShapeDtypeStruct((layers, rows, width), F32) for _, rows, _ in spans),
        in_specs=[ANY] * 3, out_specs=(ANY,) * (2 + len(spans)),
        scratch_shapes=[pltpu.VMEM(outputs.shape, BF16), pltpu.VMEM(input_grad.shape, F32), pltpu.VMEM(grads.shape, BF16),
                        pltpu.VMEM(grads.shape, F32), pltpu.SemaphoreType.DMA((count,)), pltpu.SemaphoreType.DMA((count,))],
        compiler_params=pltpu.CompilerParams(vmem_limit_bytes=62 * 2**20),
        name="widen",
    )(outputs, input_grad, grads)


def solution(mesh):
    in_specs = (
        P("dp", None),
        P("dp"),
        P(None, None, None, "tensor"),
        P(None, "tensor", None),
        P(None, None, "tensor"),
        P(None, "tensor", None),
        P(),
        P(),
        P("dp", None),
    )
    out_specs = (
        P("dp", None),
        P("dp", None),
        P(None, None, None, "tensor"),
        P(None, "tensor", None),
        P(None, None, "tensor"),
        P(None, "tensor", None),
        P(),
        P(),
    )
    return jax.shard_map(
        functools.partial(per_device, mesh), mesh=mesh, in_specs=in_specs, out_specs=out_specs, check_vma=False
    )
```

```python
import functools

import jax
import jax.numpy as jnp
from jax import lax
from jax.experimental import pallas as pl
from jax.experimental.pallas import tpu as pltpu
from jax.sharding import PartitionSpec as P

HEAD_DIM = 64
LANES = 128
PAD = 256
CHUNK = 256
STEP_US = 5.33
HOP_US = 3.83
TAIL_HOP_US = 4.57
US_PER_ROW = 0.0335
PIECE = 192
ORDERS = "xzxzxxxxzzxxzxxxxxxxxzxz"
BF16 = jnp.bfloat16
F32 = jnp.float32
MESH = pl.DeviceIdType.MESH
ANY = pl.BlockSpec(memory_space=pl.ANY)
VMEM = pl.BlockSpec(memory_space=pltpu.VMEM)
SMEM = pl.BlockSpec(memory_space=pltpu.SMEM)


def dot_nn(a, b):
    return lax.dot_general(a, b, (((1,), (0,)), ((), ())), preferred_element_type=F32)


def dot_nt(a, b):
    return lax.dot_general(a, b, (((1,), (1,)), ((), ())), preferred_element_type=F32)


def dot_tn(a, b):
    return lax.dot_general(a, b, (((0,), (0,)), ((), ())), preferred_element_type=F32)


def norm_parts(v):
    centre = v - jnp.mean(v, axis=-1, keepdims=True)
    r = lax.rsqrt(jnp.mean(centre * centre, axis=-1, keepdims=True) + 1e-05)
    return centre * r, r


def norm_rows(v, gain_row, bias_row):
    return norm_parts(v)[0] * gain_row + bias_row


def gelu_pair(u):
    bell = jnp.exp(u * u * -0.5)
    t = 1.0 / (1.0 + 0.23164189 * jnp.abs(u))
    series = t * (0.127414796 + t * (-0.142248368 + t * (0.7107068705 + t * (-0.7265760135 + t * 0.5307027145))))
    tail = series * bell
    phi_cdf = jnp.where(u >= 0.0, 1.0 - tail, tail)
    return u * phi_cdf, phi_cdf + u * bell * 0.3989422804014327


def cut_pieces(rows, late):
    return [(ORDERS[i], 1 - i // (rows // PIECE), i % (rows // PIECE) * PIECE, PIECE) for i in range(2 * rows // PIECE)]


def takes_over(pieces, i, late):
    kind, l, at, n = pieces[i]
    if l == 1 or at < late:
        return None
    return next(k for k, p in enumerate(pieces) if p == (kind, 1, at - late, n))


def scratch_rows(pieces, late):
    total = 0
    for i, (kind, _, _, n) in enumerate(pieces):
        total += n // 2 if takes_over(pieces, i, late) is not None else (3 * n // 2 if kind == "x" else 2 * n)
    return total


def step_kernel(n_tensor, n_dp, pieces, len_ref, x_hbm, cot_hbm, wqkv_hbm, wout_hbm, wup_hbm, wdown_hbm, gain_ref, bias_ref,
                act_out, ig_out, grads_out, ggain_out, gbias_out,
                xin, dzb, wqkv, wout, wup, wdown, normed, nmid, q_s, k_s, kt_s, v_s, ctx, lse, xh, midh, act, gpr,
                part, rsbuf, ysend, yrecv, dmidb, dmh, dk_s, dv_s, grads, gacc, art, nsum, nrecv,
                sems_in, rs_sem, y_sem, ag_sem, out_sem, ar_sem, own_sem, norm_sem, extra_sem, ready_sem):
    layers = wqkv.shape[0]
    rows_all, width = xin.shape
    ff = wup.shape[2]
    C, half = rows_all // CHUNK, CHUNK // 2
    part_width = 3 * HEAD_DIM
    dp, t = lax.axis_index("dp"), lax.axis_index("tensor")
    b = lax.rem(t, 2)
    sib = (dp, t + 1 - 2 * b)
    peer = (dp, lax.rem(t + 2, n_tensor))
    x_at, z_at = lax.rem(dp, 2), lax.rem(lax.div(dp, 2), 4)
    x_dev = (dp + 1 - 2 * x_at, t)
    z_dev = (dp + 2 - 4 * lax.rem(z_at, 2), t)
    mid_dev = (dp + 6 - 4 * z_at, t)
    more = [(dp + d - 2 * d * lax.rem(lax.div(dp, d), 2), t) for d in (8 * 2**i for i in range((n_dp // 8).bit_length() - 1))]
    outer = lax.rem(z_at, 3) == 0
    inner = jnp.logical_not(outer)
    z_half = lax.div(z_at, 2)
    length = len_ref[0]

    pairs = [(x_hbm, xin)]
    for l in range(layers):
        for j in range(3):
            pairs.append((wqkv_hbm.at[l, pl.ds(j * part_width, part_width)], wqkv.at[l, pl.ds(j * PAD, part_width)]))
    pairs += [(wout_hbm.at[l], wout.at[l, pl.ds(0, part_width)]) for l in range(layers)]
    pairs += [(wup_hbm, wup), (wdown_hbm, wdown), (cot_hbm, dzb)]
    loads = [pltpu.make_async_copy(a, o, sems_in.at[i]) for i, (a, o) in enumerate(pairs)]
    need_x, need_qkv, need_out, need_up, need_down, need_cot = 0, 1, 1 + 3 * layers, 1 + 4 * layers, 2 + 4 * layers, 3 + 4 * layers
    first_loads = [need_x, need_qkv, need_qkv + 1, need_qkv + 2, need_out]
    for i in first_loads:
        loads[i].start()
    for l in range(layers):
        for j in range(3):
            wqkv[l, j * PAD + part_width:(j + 1) * PAD] = jnp.zeros((PAD - part_width, width), BF16)
        wout[l, part_width:PAD] = jnp.zeros((PAD - part_width, width), BF16)
    pg = gpr.at[layers - 1]
    waited = set()

    def need(i):
        if i not in waited:
            waited.add(i)
            loads[i].wait()
            if i == need_qkv + 2:
                for k in range(len(loads)):
                    if k not in first_loads:
                        loads[k].start()

    barrier = pltpu.get_barrier_semaphore()
    greeted = [sib, peer, x_dev, z_dev, mid_dev] + more
    for other in greeted:
        pl.semaphore_signal(barrier, inc=1, device_id=other, device_id_type=MESH)
    pl.semaphore_wait(barrier, len(greeted))

    def remote(src, dst, sem, dev):
        return pltpu.make_async_remote_copy(src_ref=src, dst_ref=dst, send_sem=sem.at[0], recv_sem=sem.at[1],
                                            device_id=dev, device_id_type=MESH)

    def chunk(c):
        return pl.ds(c * CHUNK, CHUNK)

    def mine(c):
        return pl.ds(pl.multiple_of(c * CHUNK + b * half, half), half)

    def rs_copy(o, c):
        theirs = pl.ds(pl.multiple_of((1 - b) * half, half), half)
        return remote(part.at[c, theirs], rsbuf.at[c], rs_sem.at[c], sib)

    def y_copy(o, c):
        return remote(ysend.at[c], yrecv.at[o % 2, c], y_sem.at[o % 2, c], peer)

    def ag_pair(o, c):
        rows = mine(c)
        whole = {0: nmid.at[0], 1: normed.at[1], 2: nmid.at[1], 3: dmidb, 4: dzb, 5: dmidb}
        if o in whole:
            return whole[o].at[rows], whole[o].at[rows]
        return (dmh.at[c], ig_out.at[rows]) if o == 6 else (ysend.at[c], act_out.at[rows])

    def ag_copy(o, c):
        return remote(*ag_pair(o, c), ag_sem.at[o % 2, c], sib)

    def own_copy(o, c):
        return pltpu.make_async_copy(*ag_pair(o, c), out_sem.at[o - 6, c])

    def gain(l, i):
        return gain_ref[l, i:i + 1, :]

    def bias(l, i):
        return bias_ref[l, i:i + 1, :]

    low = lax.broadcasted_iota(jnp.int32, (CHUNK, LANES), 1) < HEAD_DIM
    head_lanes = (slice(0, LANES), slice(0, LANES), slice(LANES, 2 * LANES))

    def one_head(v, h):
        w = v[:, head_lanes[h]]
        if h == 0:
            return jnp.where(low, w, jnp.zeros_like(w))
        return jnp.where(low, jnp.zeros_like(w), w) if h == 1 else w

    def attend(l, c):
        rows = chunk(c)
        if l == 0:
            need(need_x)
            normed[0, rows] = norm_rows(xin[rows].astype(F32), gain(0, 0), bias(0, 0)).astype(BF16)
        for j in range(3):
            need(need_qkv + 3 * l + j)
        nc = normed[l, rows]
        q = dot_nt(nc, wqkv[l, 0:PAD]).astype(BF16) * jnp.asarray(HEAD_DIM ** (-0.5), BF16)
        k = dot_nt(nc, wqkv[l, PAD:2 * PAD])
        q_s[l, rows] = q
        k_s[l, rows] = k.astype(BF16)
        kt_s[l, :, rows] = k.T.astype(BF16)
        v_s[l, rows] = dot_nt(nc, wqkv[l, 2 * PAD:3 * PAD]).astype(BF16)
        wide = (c + 1) * CHUNK
        key_pos = lax.broadcasted_iota(jnp.int32, (CHUNK, wide), 1)
        query_pos = lax.broadcasted_iota(jnp.int32, (CHUNK, wide), 0) + c * CHUNK
        allowed = (key_pos <= query_pos) & (key_pos < length)
        lane = lax.broadcasted_iota(jnp.int32, (CHUNK, LANES), 1)
        outs = []
        logs = jnp.zeros((CHUNK, LANES), F32)
        for h in range(3):
            s = dot_nt(one_head(q, h), k_s[l, 0:wide, head_lanes[h]])
            s = jnp.where(allowed, s, -1e30)
            m = jnp.max(s, axis=-1, keepdims=True)
            p = jnp.exp(s - m)
            z = jnp.sum(p, axis=-1, keepdims=True)
            outs.append(dot_nn(p.astype(BF16), v_s[l, 0:wide, head_lanes[h]]) / z)
            logs = jnp.where(lane == h, m + jnp.log(z), logs)
        lse[l, :, rows] = logs.T[0:8, :]
        ctx[l, rows, 0:LANES] = jnp.where(low, outs[0], outs[1]).astype(BF16)
        ctx[l, rows, LANES:2 * LANES] = outs[2].astype(BF16)
        need(need_out + l)
        part[c] = dot_nn(ctx[l, rows], wout[l]).astype(BF16)

    def feed(l, c):
        need(need_up)
        need(need_down)
        rows = chunk(c)
        nm = nmid[l, rows]
        last = l + 1 == layers
        if last:
            need(need_cot)
            pos = lax.broadcasted_iota(jnp.int32, (CHUNK, width), 0) + c * CHUNK
            dz = jnp.where(pos < length, dzb[rows].astype(F32), 0.0).astype(BF16)
            dzb[rows] = dz
        for n in range(0, ff, 256):
            a, g = gelu_pair(dot_nn(nm, wup[l, :, n:n + 256]))
            act[l, rows, n:n + 256] = a.astype(BF16)
            if last:
                g = g * dot_nt(dz, wdown[l, n:n + 256, :])
            gpr[l, rows, n:n + 256] = g.astype(BF16)
        if last:
            part[c] = dot_nt(gpr[l, rows], wup[l]).astype(BF16)
        else:
            part[c] = dot_nn(act[l, rows], wdown[l]).astype(BF16)

    def feed_back(l, c):
        rows = chunk(c)
        dz = dzb[rows]
        for n in range(0, ff, 256):
            g = gpr[l, rows, n:n + 256].astype(F32) * dot_nt(dz, wdown[l, n:n + 256, :])
            gpr[l, rows, n:n + 256] = g.astype(BF16)
        part[c] = dot_nt(gpr[l, rows], wup[l]).astype(BF16)

    def attend_back(l, c):
        rows = chunk(c)
        dctx = dot_nt(dmidb[rows], wout[l]).astype(BF16)
        prod = dctx.astype(F32) * ctx[l, rows].astype(F32)
        lane = lax.broadcasted_iota(jnp.int32, (CHUNK, LANES), 1)
        inner = jnp.zeros((CHUNK, LANES), F32)
        for h in range(3):
            inner = jnp.where(lane == h, jnp.sum(one_head(prod, h), axis=-1, keepdims=True), inner)
        inner = inner.T
        wide = (c + 1) * CHUNK
        key_pos = lax.broadcasted_iota(jnp.int32, (wide, CHUNK), 0)
        query_pos = lax.broadcasted_iota(jnp.int32, (wide, CHUNK), 1) + c * CHUNK
        allowed = (key_pos <= query_pos) & (key_pos < length)
        q = q_s[l, rows]
        dqs = []
        keys = slice(0, wide)
        for h in range(3):
            lanes = head_lanes[h]
            qh, dch = one_head(q, h), one_head(dctx, h)
            s = jnp.where(allowed, dot_nt(k_s[l, keys, lanes], qh), -1e30)
            p = jnp.exp(s - lse[l, h:h + 1, rows])
            dp_ = dot_nt(v_s[l, keys, lanes], dch)
            ds = (p * (dp_ - inner[h:h + 1, :])).astype(BF16)
            dv = dot_nn(p.astype(BF16), dch)
            dk = dot_nn(ds, qh)
            if c == C - 1 and h != 1:
                dv_s[keys, lanes] = dv
                dk_s[keys, lanes] = dk
            else:
                dv_s[keys, lanes] += dv
                dk_s[keys, lanes] += dk
            dqs.append(dot_nn(kt_s[l, h * HEAD_DIM:(h + 1) * HEAD_DIM, keys], ds) * HEAD_DIM ** (-0.5))
        dqs.append(jnp.zeros((PAD - part_width, CHUNK), F32))
        pg[rows, 0:PAD] = jnp.concatenate(dqs, axis=0).T.astype(BF16)
        pg[rows, PAD:2 * PAD] = dk_s[rows].astype(BF16)
        pg[rows, 2 * PAD:3 * PAD] = dv_s[rows].astype(BF16)
        part[c] = dot_nn(pg[rows], wqkv[l]).astype(BF16)

    def compute(o, c):
        if o == 7:
            part[c] = dot_nn(act[1, chunk(c)], wdown[1]).astype(BF16)
        elif o < 4:
            (attend if o % 2 == 0 else feed)(o // 2, c)
        else:
            (attend_back if o % 2 == 0 else feed_back)(1 if o == 4 else 0, c)

    up_at, down_at, out_at, qkv_at = 0, width, width + ff, width + ff + part_width

    def weights_of_feed(l):
        for m in range(0, width, 384):
            grads[l, up_at + m:up_at + m + 384] = dot_tn(nmid[l, :, m:m + 384], gpr[l]).astype(BF16)
            launch(l, up_at + m)
        for m in range(0, ff, 384):
            grads[l, down_at + m:down_at + m + 384] = dot_tn(act[l, :, m:m + 384], dzb[...]).astype(BF16)
            launch(l, down_at + m)

    def weights_of_attend(l):
        grads[l, out_at:out_at + part_width] = dot_tn(ctx[l], dmidb[...])[0:part_width].astype(BF16)
        launch(l, out_at)
        for j in range(3):
            at = qkv_at + j * part_width
            grads[l, at:at + part_width] = dot_tn(gpr[layers - 1, :, j * PAD:(j + 1) * PAD], normed[l])[0:part_width].astype(BF16)
            launch(l, at)

    def rows_at(at, n):
        return pl.ds(pl.multiple_of(at, 16), n)

    def add_rows(l, at, tmp_at, n):
        def block(i, carry):
            rows = rows_at(at + i * 96, 96)
            grads[l, rows] = (grads[l, rows].astype(F32) + art[rows_at(tmp_at + i * 96, 96)].astype(F32)).astype(BF16)
            return carry

        lax.fori_loop(0, n // 96, block, 0)

    def extra_sums(l, at, tmp_at, n):
        for i, dev in enumerate(more):
            pl.semaphore_signal(ready_sem.at[i], inc=1, device_id=dev, device_id_type=MESH)
            pl.semaphore_wait(ready_sem.at[i], 1)
            copy = remote(grads.at[l, rows_at(at, n)], art.at[pl.ds(tmp_at, n)], extra_sem.at[i], dev)
            copy.start()
            copy.wait()
            add_rows(l, at, tmp_at, n)

    class Piece:
        def __init__(self, kind, l, at, n, slot, tmp):
            self.kind, self.l, self.n, self.at, self.turn, self.ready = kind, l, n, at, 0, 0.0
            h = n // 2
            pick = x_at if kind == "x" else z_half
            self.keep, self.give = at + pick * h, at + (1 - pick) * h
            keep, give, whole = (grads.at[l, rows_at(self.keep, h)], grads.at[l, rows_at(self.give, h)], grads.at[l, pl.ds(at, n)])
            sizes = (h, h, h) if kind == "x" else (n, h, h)
            self.tmp = tmp
            land = [art.at[pl.ds(a, m)] for a, m in zip(tmp, sizes)]
            done_keep, done_give = grads_out.at[l, rows_at(self.keep, h)], grads_out.at[l, rows_at(self.give, h)]
            self.own = pltpu.make_async_copy(keep, done_keep, own_sem.at[slot])
            if kind == "x":
                ends = [(give, land[0], x_dev), (keep, land[1], z_dev), (keep, land[2], mid_dev), (keep, done_keep, z_dev),
                        (keep, done_keep, x_dev), (done_keep, done_keep, x_dev)]
            else:
                ends = [(whole, land[0], z_dev), (give, land[1], mid_dev), (keep, land[2], x_dev), (keep, done_keep, mid_dev),
                        (keep, done_keep, z_dev), (done_give, done_give, z_dev)]
            at_sem = (0, 1, 2, 3, 4, 4) if kind == "x" else (0, 1, 2, 3, 4, 5)
            self.copies = [remote(src, dst, ar_sem.at[slot, i], dev) for i, (src, dst, dev) in zip(at_sem, ends)]
            self.links = (
                ((("x", "outer"), h), (("x", "inner"), h)), ((("z", "outer"), h),), ((("mid", "inner"), h),),
                ((("z", "inner"), h), (("x", "inner"), h)), ((("x", "outer"), h),),
            ) if kind == "x" else (
                ((("z", "outer"), n),), ((("mid", "inner"), h),), ((("x", "inner"), h),),
                ((("mid", "inner"), h), (("z", "inner"), h)), ((("z", "inner"), h),),
            )

        def step(self):
            c, l, n, h = self.copies, self.l, self.n, self.n // 2
            if self.kind == "x":
                if self.turn == 0:
                    c[0].start()
                elif self.turn == 1:
                    c[0].wait()
                    add_rows(l, self.keep, self.tmp[0], h)
                    pl.when(outer)(c[1].start)
                elif self.turn == 2:
                    @pl.when(inner)
                    def _():
                        c[1].wait_recv()
                        add_rows(l, self.keep, self.tmp[1], h)
                        c[2].start()
                    pl.when(outer)(c[1].wait_send)
                elif self.turn == 3:
                    @pl.when(inner)
                    def _():
                        c[2].wait()
                        add_rows(l, self.keep, self.tmp[2], h)
                        extra_sums(l, self.keep, self.tmp[0], h)
                        c[3].start()
                        c[4].start()
                        self.own.start()
                elif self.turn == 4:
                    @pl.when(outer)
                    def _():
                        c[3].wait_recv()
                        c[5].start()
                else:
                    @pl.when(inner)
                    def _():
                        c[3].wait_send()
                        self.own.wait()
                    c[4].wait()
            else:
                if self.turn == 0:
                    pl.when(outer)(c[0].start)
                elif self.turn == 1:
                    @pl.when(inner)
                    def _():
                        c[0].wait_recv()
                        add_rows(l, self.at, self.tmp[0], n)
                        c[1].start()
                    pl.when(outer)(c[0].wait_send)
                elif self.turn == 2:
                    @pl.when(inner)
                    def _():
                        c[1].wait()
                        add_rows(l, self.keep, self.tmp[1], h)
                        c[2].start()
                elif self.turn == 3:
                    @pl.when(inner)
                    def _():
                        c[2].wait()
                        add_rows(l, self.keep, self.tmp[2], h)
                        extra_sums(l, self.keep, self.tmp[1], h)
                        c[3].start()
                        c[4].start()
                        self.own.start()
                elif self.turn == 4:
                    @pl.when(inner)
                    def _():
                        c[3].wait()
                        c[5].start()
                else:
                    @pl.when(inner)
                    def _():
                        c[4].wait_send()
                        c[5].wait_send()
                        self.own.wait()

                    @pl.when(outer)
                    def _():
                        c[4].wait_recv()
                        c[5].wait_recv()
            if self.turn < 5:
                self.ready = 0.0
                for link, rows in self.links[self.turn]:
                    free[link] = max(clock[0], free.get(link, 0.0)) + rows * US_PER_ROW
                    self.ready = max(self.ready, free[link] + HOP_US)
            self.turn += 1

    class Norms:
        def __init__(self):
            self.turn, self.ready = 0, clock[0]
            nsum[0] = jnp.concatenate([jnp.sum(gacc[i], axis=0, keepdims=True) for i in range(8)], axis=0)
            partners = [sib, x_dev, z_dev, mid_dev] + more
            self.copies = [remote(nsum.at[i], nrecv.at[i], norm_sem.at[i], dev) for i, dev in enumerate(partners)]

        def step(self):
            i = self.turn
            if i > 0:
                self.copies[i - 1].wait()
                nsum[i] = nsum[i - 1] + nrecv[i - 1]
            if i < len(self.copies):
                self.copies[i].start()
            self.turn += 1
            links = ((), ("x",), ("z",), ("z", "mid"))[min(i, 3)]
            self.ready = max([clock[0]] + [free.get((link, role), 0.0) for link in links for role in ("outer", "inner")]) + HOP_US

        def over(self):
            return self.turn > len(self.copies)

    clock, free, jobs, held, over = [0.0], {}, [], [], set()
    slots = {}
    cursor = 0
    for i, (kind, l, at, n) in enumerate(pieces):
        before = takes_over(pieces, i, out_at)
        sizes = (n // 2,) * 3 if kind == "x" else (n, n // 2, n // 2)
        tmp = []
        if before is not None:
            tmp, sizes = slots[pieces[before][1:3]][3][0:2], sizes[2:]
        for m in sizes:
            tmp = tmp + [cursor]
            cursor += m
        slots[(l, at)] = (kind, n, i, tmp, None, None if before is None else pieces[before][1:3])

    def launch(l, at):
        block_end = at + (384 if at < out_at else part_width)
        for (l2, at2), (kind, n, slot, tmp, _, before) in slots.items():
            if l2 == l and at < at2 + n <= block_end:
                held.append((l2, at2))
        release()

    def release():
        for key in list(held):
            kind, n, slot, tmp, _, before = slots[key]
            if before is None or before in over:
                held.remove(key)
                job = Piece(kind, key[0], key[1], n, slot, tmp)
                job.key = key
                job.step()
                jobs.append(job)

    def advance(job):
        job.step()
        if job.over() if isinstance(job, Norms) else job.turn > 5:
            jobs.remove(job)
            if isinstance(job, Piece):
                over.add(job.key)
                release()

    def serve():
        while True:
            due = [job for job in jobs if job.ready <= clock[0]]
            if not due:
                return
            advance(min(due, key=lambda job: job.ready))

    def serve_rest():
        while jobs:
            job = min(jobs, key=lambda job: job.ready)
            clock[0] = max(clock[0], job.ready - HOP_US + TAIL_HOP_US) + 0.3
            advance(job)

    def sum_pair(o, c):
        rs_copy(o, c).wait()
        own = part[c, pl.ds(pl.multiple_of(b * half, half), half), :]
        ysend[c] = (own.astype(F32) + rsbuf[c].astype(F32)).astype(BF16)
        y_copy(o, c).start()

    def norm_back(l, i, v, e):
        xhat, r = norm_parts(v)
        for at, term in ((2 * l + i, e * xhat), (4 + 2 * l + i, e)):
            gacc[at] += jnp.sum(term.reshape(half // 8, 8, width), axis=0)
        eg = e * gain(l, i)
        return r * (eg - jnp.mean(eg, axis=-1, keepdims=True) - xhat * jnp.mean(eg * xhat, axis=-1, keepdims=True))

    def valid_half(c, v):
        pos = lax.broadcasted_iota(jnp.int32, (half, width), 0) + (c * CHUNK + b * half)
        return jnp.where(pos < length, v, 0.0)

    def finish(o, c):
        y_copy(o, c).wait()
        rows = mine(c)
        total = ysend[c].astype(F32) + yrecv[o % 2, c].astype(F32)
        if o in (0, 2):
            l = o // 2
            middle = (xin[rows].astype(F32) if l == 0 else xh[c]) + total
            midh[l, c] = middle
            nmid[l, rows] = norm_rows(middle, gain(l, 1), bias(l, 1)).astype(BF16)
        elif o == 1:
            after = valid_half(c, midh[0, c] + total)
            xh[c] = after
            normed[1, rows] = norm_rows(after, gain(1, 0), bias(1, 0)).astype(BF16)
        elif o in (3, 5):
            l, dz = (1, dzb[rows].astype(F32)) if o == 3 else (0, xh[c])
            dmiddle = dz + norm_back(l, 1, midh[l, c], total)
            dmh[c] = dmiddle
            dmidb[rows] = dmiddle.astype(BF16)
        elif o == 4:
            dz = valid_half(c, dmh[c] + norm_back(1, 0, xh[c], total))
            xh[c] = dz
            dzb[rows] = dz.astype(BF16)
        elif o == 6:
            dmh[c] = dmh[c] + norm_back(0, 0, xin[rows].astype(F32), total)
        else:
            ysend[c] = valid_half(c, midh[1, c] + total).astype(BF16)
        ag_copy(o, c).start()
        if o >= 6:
            own_copy(o, c).start()

    gacc[...] = jnp.zeros_like(gacc)
    pending, done = [], set()

    def finish_next(paired=False):
        step = pending.pop(0)
        finish(*step)
        done.add(step)
        clock[0] += STEP_US / 2 if paired else STEP_US
        if step == (6, 0):
            jobs.append(Norms())
        serve()

    for o in range(8):
        for c in (range(C) if o < 4 else reversed(range(C))):
            if o > 0:
                while (o - 1, c) not in done:
                    finish_next()
                ag_copy(o - 1, c).wait()
                if o == 7:
                    own_copy(6, c).wait()
            compute(o, c)
            rs_copy(o, c).start()
            if o >= 4:
                clock[0] += STEP_US / 2
                serve()
            if len(pending) >= C - 1:
                finish_next(True)
            sum_pair(o, c)
            pending.append((o, c))
        if o == 3:
            clock[0] = 0.0
        if o in (3, 5):
            weights_of_feed(1 if o == 3 else 0)
        if o in (4, 6):
            weights_of_attend(1 if o == 4 else 0)
    while pending:
        finish_next()
    for c in range(C):
        ag_copy(7, c).wait()
        own_copy(7, c).wait()
    serve_rest()
    norms = nsum[len(greeted) - 1]
    for i in range(2 * layers):
        ggain_out[i // 2, i % 2:i % 2 + 1, :] = norms[i:i + 1]
        gbias_out[i // 2, i % 2:i % 2 + 1, :] = norms[4 + i:5 + i]


def step_call(mesh, lengths, x, cot, wqkv, wout, wup, wdown, gain, bias):
    rows, width = x.shape
    layers, ff = wup.shape[0], wup.shape[2]
    C = rows // CHUNK
    half = (C, CHUNK // 2, width)
    grads = (layers, width + ff + 4 * 3 * HEAD_DIM, width)
    pieces = cut_pieces(grads[1], width + ff)
    n_dp = mesh.shape["dp"]
    hops = 4 + (n_dp // 8).bit_length() - 1
    two = (layers, rows, PAD)

    def vmem(shape, kind=BF16):
        return pltpu.VMEM(shape, kind)

    scratch = [
        vmem(x.shape), vmem(x.shape), vmem((layers, 3 * PAD, width)), vmem((layers, PAD, width)), vmem(wup.shape), vmem(wdown.shape),
        vmem((layers, rows, width)), vmem((layers, rows, width)),
        vmem(two), vmem(two), vmem((layers, PAD, rows)), vmem(two), vmem(two), vmem((layers, 8, rows), F32),
        vmem(half, F32), vmem((layers,) + half, F32), vmem((layers, rows, ff)), vmem((layers, rows, ff)),
        vmem((C, CHUNK, width)), vmem(half), vmem(half), vmem((2,) + half),
        vmem(x.shape), vmem(half, F32), vmem((rows, PAD), F32), vmem((rows, PAD), F32),
        vmem(grads), vmem((8, 8, width), F32), vmem((scratch_rows(pieces, width + ff), width)),
        vmem((hops + 1, 8, width), F32), vmem((hops, 8, width), F32),
        pltpu.SemaphoreType.DMA((4 + 4 * layers,)), pltpu.SemaphoreType.DMA((C, 2)), pltpu.SemaphoreType.DMA((2, C, 2)),
        pltpu.SemaphoreType.DMA((2, C, 2)), pltpu.SemaphoreType.DMA((2, C)),
        pltpu.SemaphoreType.DMA((len(pieces), 6, 2)), pltpu.SemaphoreType.DMA((len(pieces),)), pltpu.SemaphoreType.DMA((hops, 2)),
        pltpu.SemaphoreType.DMA((max(hops - 4, 1), 2)), pltpu.SemaphoreType.REGULAR((max(hops - 4, 1),)),
    ]
    return pl.pallas_call(
        functools.partial(step_kernel, mesh.shape["tensor"], n_dp, pieces),
        out_shape=(jax.ShapeDtypeStruct(x.shape, BF16), jax.ShapeDtypeStruct(x.shape, F32),
                   jax.ShapeDtypeStruct(grads, BF16),
                   jax.ShapeDtypeStruct(gain.shape, F32), jax.ShapeDtypeStruct(gain.shape, F32)),
        in_specs=[SMEM] + [ANY] * 6 + [VMEM, VMEM], out_specs=(ANY, ANY, ANY, VMEM, VMEM), scratch_shapes=scratch,
        compiler_params=pltpu.CompilerParams(collective_id=0, has_side_effects=True, vmem_limit_bytes=62 * 2**20),
        name="step",
    )(lengths, x, cot, wqkv, wout, wup, wdown, gain, bias)


def per_device(
    mesh, inputs, lengths, qkv_weight, out_weight, up_weight, down_weight, norm_gain, norm_bias, cotangent
):
    layers, width, three, part_width = qkv_weight.shape
    ff = up_weight.shape[2]
    outputs, input_grad, grads, grad_gain, grad_bias = step_call(
        mesh, lengths, inputs, cotangent, qkv_weight.transpose(0, 2, 3, 1).reshape(layers, three * part_width, width),
        out_weight, up_weight, down_weight, norm_gain, norm_bias,
    )
    outputs, input_grad, grad_gain, grad_bias, grad_up, grad_down, grad_out, grad_qkv = widen_call(
        outputs, input_grad, grad_gain, grad_bias, grads, ff, part_width
    )
    grad_qkv = grad_qkv.reshape(layers, three, part_width, width).transpose(0, 3, 1, 2)
    return (outputs, input_grad, grad_qkv, grad_out, grad_up, grad_down, grad_gain, grad_bias)


def widen_kernel(spans, act_in, ig_in, gain_in, bias_in, grads_in, act_out, ig_out, gain_out, bias_out, *rest):
    gain_out[...] = gain_in[...]
    bias_out[...] = bias_in[...]
    outs, (act, ig, low, wide, sem_in, sem_out) = rest[:len(spans)], rest[len(spans):]
    layers = grads_in.shape[0]
    through = [(act_in, act, act_out), (ig_in, ig, ig_out)]
    blocks = [(l, k, at, at + i, n) for k, (at, rows, n) in enumerate(spans) for l in range(layers) for i in range(0, rows, n)]
    into = [pltpu.make_async_copy(grads_in.at[l, pl.ds(r, n)], low.at[l, pl.ds(r, n)], sem_in.at[i]) for i, (l, _, _, r, n) in enumerate(blocks)]
    into += [pltpu.make_async_copy(a, v, sem_in.at[len(blocks) + i]) for i, (a, v, _) in enumerate(through)]
    for copy in into:
        copy.start()
    back = []
    for i, (l, k, at, r, n) in enumerate(blocks):
        into[i].wait()
        wide[l, pl.ds(r, n)] = low[l, pl.ds(r, n)].astype(F32)
        back.append(pltpu.make_async_copy(wide.at[l, pl.ds(r, n)], outs[k].at[l, pl.ds(r - at, n)], sem_out.at[i]))
        back[-1].start()
    for i, (_, v, o) in enumerate(through):
        into[len(blocks) + i].wait()
        back.append(pltpu.make_async_copy(v, o, sem_out.at[len(blocks) + i]))
        back[-1].start()
    for copy in back:
        copy.wait()


def widen_call(outputs, input_grad, grad_gain, grad_bias, grads, ff, part_width):
    layers, _, width = grads.shape
    spans, at = [], 0
    for rows in (width, ff, part_width, 3 * part_width):
        spans.append((at, rows, PIECE))
        at += rows
    count = sum(layers * rows // n for _, rows, n in spans) + 2
    return pl.pallas_call(
        functools.partial(widen_kernel, spans),
        out_shape=(jax.ShapeDtypeStruct(outputs.shape, BF16), jax.ShapeDtypeStruct(input_grad.shape, F32))
        + (jax.ShapeDtypeStruct(grad_gain.shape, F32),) * 2
        + tuple(jax.ShapeDtypeStruct((layers, rows, width), F32) for _, rows, _ in spans),
        in_specs=[ANY, ANY, VMEM, VMEM, ANY], out_specs=(ANY, ANY, VMEM, VMEM) + (ANY,) * len(spans),
        scratch_shapes=[pltpu.VMEM(outputs.shape, BF16), pltpu.VMEM(input_grad.shape, F32), pltpu.VMEM(grads.shape, BF16),
                        pltpu.VMEM(grads.shape, F32), pltpu.SemaphoreType.DMA((count,)), pltpu.SemaphoreType.DMA((count,))],
        compiler_params=pltpu.CompilerParams(vmem_limit_bytes=62 * 2**20),
        name="widen",
    )(outputs, input_grad, grad_gain, grad_bias, grads)


def solution(mesh):
    in_specs = (
        P("dp", None),
        P("dp"),
        P(None, None, None, "tensor"),
        P(None, "tensor", None),
        P(None, None, "tensor"),
        P(None, "tensor", None),
        P(),
        P(),
        P("dp", None),
    )
    out_specs = (
        P("dp", None),
        P("dp", None),
        P(None, None, None, "tensor"),
        P(None, "tensor", None),
        P(None, None, "tensor"),
        P(None, "tensor", None),
        P(),
        P(),
    )
    return jax.shard_map(
        functools.partial(per_device, mesh), mesh=mesh, in_specs=in_specs, out_specs=out_specs, check_vma=False
    )
```

```python
import functools

import jax
import jax.numpy as jnp
from jax import lax
from jax.experimental import pallas as pl
from jax.experimental.pallas import tpu as pltpu
from jax.sharding import PartitionSpec as P

HEAD_DIM = 64
LANES = 128
PAD = 256
CHUNK = 256
STEP_US = 5.33
HOP_US = 0.94
TAIL_HOP_US = 2.54
US_PER_ROW = 0.0335
PIECE = 192
ORDERS = "xzxxxzwxxzwxxzzwxxxwxzxx"
BF16 = jnp.bfloat16
F32 = jnp.float32
MESH = pl.DeviceIdType.MESH
ANY = pl.BlockSpec(memory_space=pl.ANY)
VMEM = pl.BlockSpec(memory_space=pltpu.VMEM)
SMEM = pl.BlockSpec(memory_space=pltpu.SMEM)


def dot_nn(a, b):
    return lax.dot_general(a, b, (((1,), (0,)), ((), ())), preferred_element_type=F32)


def dot_nt(a, b):
    return lax.dot_general(a, b, (((1,), (1,)), ((), ())), preferred_element_type=F32)


def dot_tn(a, b):
    return lax.dot_general(a, b, (((0,), (0,)), ((), ())), preferred_element_type=F32)


def norm_parts(v):
    centre = v - jnp.mean(v, axis=-1, keepdims=True)
    r = lax.rsqrt(jnp.mean(centre * centre, axis=-1, keepdims=True) + 1e-05)
    return centre * r, r


def norm_rows(v, gain_row, bias_row):
    return norm_parts(v)[0] * gain_row + bias_row


def gelu_pair(u):
    bell = jnp.exp(u * u * -0.5)
    t = 1.0 / (1.0 + 0.23164189 * jnp.abs(u))
    series = t * (0.127414796 + t * (-0.142248368 + t * (0.7107068705 + t * (-0.7265760135 + t * 0.5307027145))))
    tail = series * bell
    phi_cdf = jnp.where(u >= 0.0, 1.0 - tail, tail)
    return u * phi_cdf, phi_cdf + u * bell * 0.3989422804014327


def cut_pieces(rows, late):
    return [(ORDERS[i], 1 - i // (rows // PIECE), i % (rows // PIECE) * PIECE, PIECE) for i in range(2 * rows // PIECE)]


def takes_over(pieces, i, late):
    kind, l, at, n = pieces[i]
    if l == 1 or at < late:
        return None
    return next(k for k, p in enumerate(pieces) if p == (kind, 1, at - late, n))


def scratch_rows(pieces, late):
    total = 0
    for i, (kind, _, _, n) in enumerate(pieces):
        total += n // 2 if takes_over(pieces, i, late) is not None else (2 * n if kind == "z" else 3 * n // 2)
    return total


def step_kernel(n_tensor, n_dp, pieces, len_ref, x_hbm, cot_hbm, wqkv_hbm, wout_hbm, wup_hbm, wdown_hbm, gain_ref, bias_ref,
                act_out, ig_out, grads_out, ggain_out, gbias_out,
                xin, dzb, wqkv, wout, wup, wdown, normed, nmid, q_s, k_s, kt_s, v_s, ctx, lse, xh, midh, act, gpr,
                part, rsbuf, ysend, yrecv, dmidb, dmh, dk_s, dv_s, grads, gacc, art, nsum, nrecv,
                sems_in, rs_sem, y_sem, ag_sem, out_sem, ar_sem, own_sem, norm_sem, extra_sem, ready_sem):
    layers = wqkv.shape[0]
    rows_all, width = xin.shape
    ff = wup.shape[2]
    C, half = rows_all // CHUNK, CHUNK // 2
    part_width = 3 * HEAD_DIM
    dp, t = lax.axis_index("dp"), lax.axis_index("tensor")
    b = lax.rem(t, 2)
    sib = (dp, t + 1 - 2 * b)
    peer = (dp, lax.rem(t + 2, n_tensor))
    x_at, z_at = lax.rem(dp, 2), lax.rem(lax.div(dp, 2), 4)
    x_dev = (dp + 1 - 2 * x_at, t)
    z_dev = (dp + 2 - 4 * lax.rem(z_at, 2), t)
    mid_dev = (dp + 6 - 4 * z_at, t)
    more = [(dp + d - 2 * d * lax.rem(lax.div(dp, d), 2), t) for d in (8 * 2**i for i in range((n_dp // 8).bit_length() - 1))]
    outer = lax.rem(z_at, 3) == 0
    inner = jnp.logical_not(outer)
    z_half = lax.div(z_at, 2)
    length = len_ref[0]

    pairs = [(x_hbm, xin)]
    for l in range(layers):
        for j in range(3):
            pairs.append((wqkv_hbm.at[l, pl.ds(j * part_width, part_width)], wqkv.at[l, pl.ds(j * PAD, part_width)]))
    pairs += [(wout_hbm.at[l], wout.at[l, pl.ds(0, part_width)]) for l in range(layers)]
    pairs += [(wup_hbm, wup), (wdown_hbm, wdown), (cot_hbm, dzb)]
    loads = [pltpu.make_async_copy(a, o, sems_in.at[i]) for i, (a, o) in enumerate(pairs)]
    need_x, need_qkv, need_out, need_up, need_down, need_cot = 0, 1, 1 + 3 * layers, 1 + 4 * layers, 2 + 4 * layers, 3 + 4 * layers
    first_loads = [need_x, need_qkv, need_qkv + 1, need_qkv + 2, need_out]
    for i in first_loads:
        loads[i].start()

    def clear_pad(l):
        for j in range(3):
            wqkv[l, j * PAD + part_width:(j + 1) * PAD] = jnp.zeros((PAD - part_width, width), BF16)
        wout[l, part_width:PAD] = jnp.zeros((PAD - part_width, width), BF16)

    clear_pad(0)
    pg = gpr.at[layers - 1]
    waited = set()

    def need(i):
        if i not in waited:
            waited.add(i)
            loads[i].wait()
            if i == need_qkv + 2:
                for k in range(len(loads)):
                    if k not in first_loads:
                        loads[k].start()
                for l in range(1, layers):
                    clear_pad(l)

    barrier = pltpu.get_barrier_semaphore()
    greeted = [sib, peer, x_dev, z_dev, mid_dev] + more
    for other in greeted:
        pl.semaphore_signal(barrier, inc=1, device_id=other, device_id_type=MESH)

    def remote(src, dst, sem, dev):
        return pltpu.make_async_remote_copy(src_ref=src, dst_ref=dst, send_sem=sem.at[0], recv_sem=sem.at[1],
                                            device_id=dev, device_id_type=MESH)

    def chunk(c):
        return pl.ds(c * CHUNK, CHUNK)

    def mine(c):
        return pl.ds(pl.multiple_of(c * CHUNK + b * half, half), half)

    def rs_copy(o, c):
        theirs = pl.ds(pl.multiple_of((1 - b) * half, half), half)
        return remote(part.at[c, theirs], rsbuf.at[c], rs_sem.at[c], sib)

    def y_copy(o, c):
        return remote(ysend.at[c], yrecv.at[o % 2, c], y_sem.at[o % 2, c], peer)

    def ag_pair(o, c):
        rows = mine(c)
        whole = {0: nmid.at[0], 1: normed.at[1], 2: nmid.at[1], 3: dmidb, 4: dzb, 5: dmidb}
        if o in whole:
            return whole[o].at[rows], whole[o].at[rows]
        return (dmh.at[c], ig_out.at[rows]) if o == 6 else (ysend.at[c], act_out.at[rows])

    def ag_copy(o, c):
        return remote(*ag_pair(o, c), ag_sem.at[o % 2, c], sib)

    def own_copy(o, c):
        return pltpu.make_async_copy(*ag_pair(o, c), out_sem.at[o - 6, c])

    def gain(l, i):
        return gain_ref[l, i:i + 1, :]

    def bias(l, i):
        return bias_ref[l, i:i + 1, :]

    low = lax.broadcasted_iota(jnp.int32, (CHUNK, LANES), 1) < HEAD_DIM
    head_lanes = (slice(0, LANES), slice(0, LANES), slice(LANES, 2 * LANES))

    def one_head(v, h):
        w = v[:, head_lanes[h]]
        if h == 0:
            return jnp.where(low, w, jnp.zeros_like(w))
        return jnp.where(low, jnp.zeros_like(w), w) if h == 1 else w

    def attend(l, c):
        rows = chunk(c)
        if l == 0:
            need(need_x)
            normed[0, rows] = norm_rows(xin[rows].astype(F32), gain(0, 0), bias(0, 0)).astype(BF16)
        for j in range(3):
            need(need_qkv + 3 * l + j)
        nc = normed[l, rows]
        q = dot_nt(nc, wqkv[l, 0:PAD]).astype(BF16) * jnp.asarray(HEAD_DIM ** (-0.5), BF16)
        k = dot_nt(nc, wqkv[l, PAD:2 * PAD])
        q_s[l, rows] = q
        k_s[l, rows] = k.astype(BF16)
        kt_s[l, :, rows] = k.T.astype(BF16)
        v_s[l, rows] = dot_nt(nc, wqkv[l, 2 * PAD:3 * PAD]).astype(BF16)
        wide = (c + 1) * CHUNK
        key_pos = lax.broadcasted_iota(jnp.int32, (CHUNK, wide), 1)
        query_pos = lax.broadcasted_iota(jnp.int32, (CHUNK, wide), 0) + c * CHUNK
        allowed = (key_pos <= query_pos) & (key_pos < length)
        lane = lax.broadcasted_iota(jnp.int32, (CHUNK, LANES), 1)
        outs = []
        logs = jnp.zeros((CHUNK, LANES), F32)
        for h in range(3):
            s = dot_nt(one_head(q, h), k_s[l, 0:wide, head_lanes[h]])
            s = jnp.where(allowed, s, -1e30)
            m = jnp.max(s, axis=-1, keepdims=True)
            p = jnp.exp(s - m)
            z = jnp.sum(p, axis=-1, keepdims=True)
            outs.append(dot_nn(p.astype(BF16), v_s[l, 0:wide, head_lanes[h]]) / z)
            logs = jnp.where(lane == h, m + jnp.log(z), logs)
        lse[l, :, rows] = logs.T[0:8, :]
        ctx[l, rows, 0:LANES] = jnp.where(low, outs[0], outs[1]).astype(BF16)
        ctx[l, rows, LANES:2 * LANES] = outs[2].astype(BF16)
        need(need_out + l)
        part[c] = dot_nn(ctx[l, rows], wout[l]).astype(BF16)

    def feed(l, c):
        need(need_up)
        need(need_down)
        rows = chunk(c)
        nm = nmid[l, rows]
        last = l + 1 == layers
        if last:
            need(need_cot)
            pos = lax.broadcasted_iota(jnp.int32, (CHUNK, width), 0) + c * CHUNK
            dz = jnp.where(pos < length, dzb[rows].astype(F32), 0.0).astype(BF16)
            dzb[rows] = dz
        for n in range(0, ff, 256):
            a, g = gelu_pair(dot_nn(nm, wup[l, :, n:n + 256]))
            act[l, rows, n:n + 256] = a.astype(BF16)
            if last:
                g = g * dot_nt(dz, wdown[l, n:n + 256, :])
            gpr[l, rows, n:n + 256] = g.astype(BF16)
        if last:
            part[c] = dot_nt(gpr[l, rows], wup[l]).astype(BF16)
        else:
            part[c] = dot_nn(act[l, rows], wdown[l]).astype(BF16)

    def feed_back(l, c):
        rows = chunk(c)
        dz = dzb[rows]
        for n in range(0, ff, 256):
            g = gpr[l, rows, n:n + 256].astype(F32) * dot_nt(dz, wdown[l, n:n + 256, :])
            gpr[l, rows, n:n + 256] = g.astype(BF16)
        part[c] = dot_nt(gpr[l, rows], wup[l]).astype(BF16)

    def attend_back(l, c):
        rows = chunk(c)
        dctx = dot_nt(dmidb[rows], wout[l]).astype(BF16)
        prod = dctx.astype(F32) * ctx[l, rows].astype(F32)
        lane = lax.broadcasted_iota(jnp.int32, (CHUNK, LANES), 1)
        inner = jnp.zeros((CHUNK, LANES), F32)
        for h in range(3):
            inner = jnp.where(lane == h, jnp.sum(one_head(prod, h), axis=-1, keepdims=True), inner)
        inner = inner.T
        wide = (c + 1) * CHUNK
        key_pos = lax.broadcasted_iota(jnp.int32, (wide, CHUNK), 0)
        query_pos = lax.broadcasted_iota(jnp.int32, (wide, CHUNK), 1) + c * CHUNK
        allowed = (key_pos <= query_pos) & (key_pos < length)
        q = q_s[l, rows]
        dqs = []
        keys = slice(0, wide)
        for h in range(3):
            lanes = head_lanes[h]
            qh, dch = one_head(q, h), one_head(dctx, h)
            s = jnp.where(allowed, dot_nt(k_s[l, keys, lanes], qh), -1e30)
            p = jnp.exp(s - lse[l, h:h + 1, rows])
            dp_ = dot_nt(v_s[l, keys, lanes], dch)
            ds = (p * (dp_ - inner[h:h + 1, :])).astype(BF16)
            dv = dot_nn(p.astype(BF16), dch)
            dk = dot_nn(ds, qh)
            if c == C - 1 and h != 1:
                dv_s[keys, lanes] = dv
                dk_s[keys, lanes] = dk
            else:
                dv_s[keys, lanes] += dv
                dk_s[keys, lanes] += dk
            dqs.append(dot_nn(kt_s[l, h * HEAD_DIM:(h + 1) * HEAD_DIM, keys], ds) * HEAD_DIM ** (-0.5))
        dqs.append(jnp.zeros((PAD - part_width, CHUNK), F32))
        pg[rows, 0:PAD] = jnp.concatenate(dqs, axis=0).T.astype(BF16)
        pg[rows, PAD:2 * PAD] = dk_s[rows].astype(BF16)
        pg[rows, 2 * PAD:3 * PAD] = dv_s[rows].astype(BF16)
        part[c] = dot_nn(pg[rows], wqkv[l]).astype(BF16)

    def compute(o, c):
        if o == 7:
            part[c] = dot_nn(act[1, chunk(c)], wdown[1]).astype(BF16)
        elif o < 4:
            (attend if o % 2 == 0 else feed)(o // 2, c)
        else:
            (attend_back if o % 2 == 0 else feed_back)(1 if o == 4 else 0, c)

    up_at, down_at, out_at, qkv_at = 0, width, width + ff, width + ff + part_width

    def weights_of_feed(l):
        for m in range(0, width, 384):
            grads[l, up_at + m:up_at + m + 384] = dot_tn(nmid[l, :, m:m + 384], gpr[l]).astype(BF16)
            launch(l, up_at + m)
        for m in range(0, ff, 384):
            grads[l, down_at + m:down_at + m + 384] = dot_tn(act[l, :, m:m + 384], dzb[...]).astype(BF16)
            launch(l, down_at + m)

    def weights_of_attend(l):
        grads[l, out_at:out_at + part_width] = dot_tn(ctx[l], dmidb[...])[0:part_width].astype(BF16)
        launch(l, out_at)
        for j in range(3):
            at = qkv_at + j * part_width
            grads[l, at:at + part_width] = dot_tn(gpr[layers - 1, :, j * PAD:(j + 1) * PAD], normed[l])[0:part_width].astype(BF16)
            launch(l, at)

    def rows_at(at, n):
        return pl.ds(pl.multiple_of(at, 16), n)

    def add_rows(l, at, tmp_at, n):
        def block(i, carry):
            rows = rows_at(at + i * 96, 96)
            grads[l, rows] = (grads[l, rows].astype(F32) + art[rows_at(tmp_at + i * 96, 96)].astype(F32)).astype(BF16)
            return carry

        lax.fori_loop(0, n // 96, block, 0)

    def extra_sums(l, at, tmp_at, n):
        for i, dev in enumerate(more):
            pl.semaphore_signal(ready_sem.at[i], inc=1, device_id=dev, device_id_type=MESH)
            pl.semaphore_wait(ready_sem.at[i], 1)
            copy = remote(grads.at[l, rows_at(at, n)], art.at[pl.ds(tmp_at, n)], extra_sem.at[i], dev)
            copy.start()
            copy.wait()
            add_rows(l, at, tmp_at, n)

    class Piece:
        def __init__(self, kind, l, at, n, slot, tmp):
            self.kind, self.l, self.n, self.at, self.turn, self.ready = kind, l, n, at, 0, 0.0
            h = n // 2
            pick = z_half if kind == "z" else x_at
            self.keep, self.give = at + pick * h, at + (1 - pick) * h
            keep, give, whole = (grads.at[l, rows_at(self.keep, h)], grads.at[l, rows_at(self.give, h)], grads.at[l, pl.ds(at, n)])
            sizes = (n, h, h) if kind == "z" else (h, h, h)
            self.tmp = tmp
            land = [art.at[pl.ds(a, m)] for a, m in zip(tmp, sizes)]
            done_keep, done_give = grads_out.at[l, rows_at(self.keep, h)], grads_out.at[l, rows_at(self.give, h)]
            self.own = pltpu.make_async_copy(keep, done_keep, own_sem.at[slot])
            if kind != "z":
                ends = [(give, land[0], x_dev), (keep, land[1], z_dev), (keep, land[2], mid_dev), (keep, done_keep, z_dev),
                        (keep, done_keep, x_dev), (done_keep, done_keep, x_dev), (done_give, done_give, z_dev)]
            else:
                ends = [(whole, land[0], z_dev), (give, land[1], mid_dev), (keep, land[2], x_dev), (keep, done_keep, mid_dev),
                        (keep, done_keep, z_dev), (done_give, done_give, z_dev)]
            at_sem = (0, 1, 2, 3, 4, 5) if kind == "z" else (0, 1, 2, 3, 4, 4, 5)
            self.copies = [remote(src, dst, ar_sem.at[slot, i], dev) for i, (src, dst, dev) in zip(at_sem, ends)]
            x_out, x_in, z_out, z_in, mid = (("x", "outer"), h), (("x", "inner"), h), (("z", "outer"), h), (("z", "inner"), h), (("mid", "inner"), h)
            self.links = {
                "x": ((x_out, x_in), (z_out,), (mid,), (z_in, x_in), (x_out,)),
                "w": ((x_out, x_in), (z_out,), (mid,), (z_in,), (x_out,), (z_out,)),
                "z": (((("z", "outer"), n),), (mid,), (x_in,), (mid, z_in), (z_in,)),
            }[kind]

        def step(self):
            c, l, n, h = self.copies, self.l, self.n, self.n // 2
            if self.kind != "z":
                if self.turn == 0:
                    c[0].start()
                elif self.turn == 1:
                    c[0].wait()
                    add_rows(l, self.keep, self.tmp[0], h)
                    pl.when(outer)(c[1].start)
                elif self.turn == 2:
                    @pl.when(inner)
                    def _():
                        c[1].wait_recv()
                        add_rows(l, self.keep, self.tmp[1], h)
                        c[2].start()
                    pl.when(outer)(c[1].wait_send)
                elif self.turn == 3:
                    @pl.when(inner)
                    def _():
                        c[2].wait()
                        add_rows(l, self.keep, self.tmp[2], h)
                        extra_sums(l, self.keep, self.tmp[0], h)
                        c[3].start()
                        if self.kind == "x":
                            c[4].start()
                        self.own.start()
                elif self.turn == 4:
                    @pl.when(outer)
                    def _():
                        c[3].wait_recv()
                        c[5].start()
                elif self.turn == 5:
                    @pl.when(inner)
                    def _():
                        c[3].wait_send()
                        self.own.wait()
                    if self.kind == "x":
                        c[4].wait()
                    else:
                        @pl.when(outer)
                        def _():
                            c[5].wait()
                            c[6].start()
                else:
                    pl.when(outer)(c[6].wait_send)
                    pl.when(inner)(c[6].wait_recv)
            else:
                if self.turn == 0:
                    pl.when(outer)(c[0].start)
                elif self.turn == 1:
                    @pl.when(inner)
                    def _():
                        c[0].wait_recv()
                        add_rows(l, self.at, self.tmp[0], n)
                        c[1].start()
                    pl.when(outer)(c[0].wait_send)
                elif self.turn == 2:
                    @pl.when(inner)
                    def _():
                        c[1].wait()
                        add_rows(l, self.keep, self.tmp[1], h)
                        c[2].start()
                elif self.turn == 3:
                    @pl.when(inner)
                    def _():
                        c[2].wait()
                        add_rows(l, self.keep, self.tmp[2], h)
                        extra_sums(l, self.keep, self.tmp[1], h)
                        c[3].start()
                        c[4].start()
                        self.own.start()
                elif self.turn == 4:
                    @pl.when(inner)
                    def _():
                        c[3].wait()
                        c[5].start()
                else:
                    @pl.when(inner)
                    def _():
                        c[4].wait_send()
                        c[5].wait_send()
                        self.own.wait()

                    @pl.when(outer)
                    def _():
                        c[4].wait_recv()
                        c[5].wait_recv()
            if self.turn < len(self.links):
                self.ready = 0.0
                for link, rows in self.links[self.turn]:
                    free[link] = max(clock[0], free.get(link, 0.0)) + rows * US_PER_ROW
                    self.ready = max(self.ready, free[link] + HOP_US)
            self.turn += 1

    class Norms:
        def __init__(self):
            self.turn, self.ready = 0, clock[0]
            nsum[0] = jnp.concatenate([jnp.sum(gacc[i], axis=0, keepdims=True) for i in range(8)], axis=0)
            partners = [sib, x_dev, z_dev, mid_dev] + more
            self.copies = [remote(nsum.at[i], nrecv.at[i], norm_sem.at[i], dev) for i, dev in enumerate(partners)]

        def step(self):
            i = self.turn
            if i > 0:
                self.copies[i - 1].wait()
                nsum[i] = nsum[i - 1] + nrecv[i - 1]
            if i < len(self.copies):
                self.copies[i].start()
            self.turn += 1
            links = ((), ("x",), ("z",), ("z", "mid"))[min(i, 3)]
            self.ready = max([clock[0]] + [free.get((link, role), 0.0) for link in links for role in ("outer", "inner")]) + HOP_US

        def over(self):
            return self.turn > len(self.copies)

    clock, free, jobs, held, over = [0.0], {}, [], [], set()
    slots = {}
    cursor = 0
    for i, (kind, l, at, n) in enumerate(pieces):
        before = takes_over(pieces, i, out_at)
        sizes = (n, n // 2, n // 2) if kind == "z" else (n // 2,) * 3
        tmp = []
        if before is not None:
            tmp, sizes = slots[pieces[before][1:3]][3][0:2], sizes[2:]
        for m in sizes:
            tmp = tmp + [cursor]
            cursor += m
        slots[(l, at)] = (kind, n, i, tmp, None, None if before is None else pieces[before][1:3])

    def launch(l, at):
        block_end = at + (384 if at < out_at else part_width)
        for (l2, at2), (kind, n, slot, tmp, _, before) in slots.items():
            if l2 == l and at < at2 + n <= block_end:
                held.append((l2, at2))
        release()

    def release():
        for key in list(held):
            kind, n, slot, tmp, _, before = slots[key]
            if before is None or before in over:
                held.remove(key)
                job = Piece(kind, key[0], key[1], n, slot, tmp)
                job.key = key
                job.step()
                jobs.append(job)

    def advance(job):
        job.step()
        if job.over() if isinstance(job, Norms) else job.turn > len(job.links):
            jobs.remove(job)
            if isinstance(job, Piece):
                over.add(job.key)
                release()

    def serve():
        while True:
            due = [job for job in jobs if job.ready <= clock[0]]
            if not due:
                return
            advance(min(due, key=lambda job: job.ready))

    def serve_rest():
        while jobs:
            job = min(jobs, key=lambda job: job.ready)
            clock[0] = max(clock[0], job.ready - HOP_US + TAIL_HOP_US) + 0.3
            advance(job)

    def sum_pair(o, c):
        rs_copy(o, c).wait()
        own = part[c, pl.ds(pl.multiple_of(b * half, half), half), :]
        ysend[c] = (own.astype(F32) + rsbuf[c].astype(F32)).astype(BF16)
        y_copy(o, c).start()

    def norm_back(l, i, v, e):
        xhat, r = norm_parts(v)
        for at, term in ((2 * l + i, e * xhat), (4 + 2 * l + i, e)):
            gacc[at] += jnp.sum(term.reshape(half // 8, 8, width), axis=0)
        eg = e * gain(l, i)
        return r * (eg - jnp.mean(eg, axis=-1, keepdims=True) - xhat * jnp.mean(eg * xhat, axis=-1, keepdims=True))

    def valid_half(c, v):
        pos = lax.broadcasted_iota(jnp.int32, (half, width), 0) + (c * CHUNK + b * half)
        return jnp.where(pos < length, v, 0.0)

    def finish(o, c):
        y_copy(o, c).wait()
        rows = mine(c)
        total = ysend[c].astype(F32) + yrecv[o % 2, c].astype(F32)
        if o in (0, 2):
            l = o // 2
            middle = (xin[rows].astype(F32) if l == 0 else xh[c]) + total
            midh[l, c] = middle
            nmid[l, rows] = norm_rows(middle, gain(l, 1), bias(l, 1)).astype(BF16)
        elif o == 1:
            after = valid_half(c, midh[0, c] + total)
            xh[c] = after
            normed[1, rows] = norm_rows(after, gain(1, 0), bias(1, 0)).astype(BF16)
        elif o in (3, 5):
            l, dz = (1, dzb[rows].astype(F32)) if o == 3 else (0, xh[c])
            dmiddle = dz + norm_back(l, 1, midh[l, c], total)
            dmh[c] = dmiddle
            dmidb[rows] = dmiddle.astype(BF16)
        elif o == 4:
            dz = valid_half(c, dmh[c] + norm_back(1, 0, xh[c], total))
            xh[c] = dz
            dzb[rows] = dz.astype(BF16)
        elif o == 6:
            dmh[c] = dmh[c] + norm_back(0, 0, xin[rows].astype(F32), total)
        else:
            ysend[c] = valid_half(c, midh[1, c] + total).astype(BF16)
        ag_copy(o, c).start()
        if o >= 6:
            own_copy(o, c).start()

    gacc[...] = jnp.zeros_like(gacc)
    pending, done = [], set()

    def finish_next(paired=False):
        step = pending.pop(0)
        finish(*step)
        done.add(step)
        clock[0] += STEP_US / 2 if paired else STEP_US
        if step == (6, 0):
            jobs.append(Norms())
        serve()

    for o in range(8):
        for c in (range(C) if o < 4 else reversed(range(C))):
            if o > 0:
                while (o - 1, c) not in done:
                    finish_next()
                ag_copy(o - 1, c).wait()
                if o == 7:
                    own_copy(6, c).wait()
            compute(o, c)
            if (o, c) == (0, 0):
                pl.semaphore_wait(barrier, len(greeted))
            rs_copy(o, c).start()
            if o >= 4:
                clock[0] += STEP_US / 2
                serve()
            if len(pending) >= C - 1:
                finish_next(True)
            sum_pair(o, c)
            pending.append((o, c))
        if o == 3:
            clock[0] = 0.0
        if o in (3, 5):
            weights_of_feed(1 if o == 3 else 0)
        if o in (4, 6):
            weights_of_attend(1 if o == 4 else 0)
    while pending:
        finish_next()
    for c in range(C):
        ag_copy(7, c).wait()
        own_copy(7, c).wait()
    serve_rest()
    norms = nsum[len(greeted) - 1]
    for i in range(2 * layers):
        ggain_out[i // 2, i % 2:i % 2 + 1, :] = norms[i:i + 1]
        gbias_out[i // 2, i % 2:i % 2 + 1, :] = norms[4 + i:5 + i]


def step_call(mesh, lengths, x, cot, wqkv, wout, wup, wdown, gain, bias):
    rows, width = x.shape
    layers, ff = wup.shape[0], wup.shape[2]
    C = rows // CHUNK
    half = (C, CHUNK // 2, width)
    grads = (layers, width + ff + 4 * 3 * HEAD_DIM, width)
    pieces = cut_pieces(grads[1], width + ff)
    n_dp = mesh.shape["dp"]
    hops = 4 + (n_dp // 8).bit_length() - 1
    two = (layers, rows, PAD)

    def vmem(shape, kind=BF16):
        return pltpu.VMEM(shape, kind)

    scratch = [
        vmem(x.shape), vmem(x.shape), vmem((layers, 3 * PAD, width)), vmem((layers, PAD, width)), vmem(wup.shape), vmem(wdown.shape),
        vmem((layers, rows, width)), vmem((layers, rows, width)),
        vmem(two), vmem(two), vmem((layers, PAD, rows)), vmem(two), vmem(two), vmem((layers, 8, rows), F32),
        vmem(half, F32), vmem((layers,) + half, F32), vmem((layers, rows, ff)), vmem((layers, rows, ff)),
        vmem((C, CHUNK, width)), vmem(half), vmem(half), vmem((2,) + half),
        vmem(x.shape), vmem(half, F32), vmem((rows, PAD), F32), vmem((rows, PAD), F32),
        vmem(grads), vmem((8, 8, width), F32), vmem((scratch_rows(pieces, width + ff), width)),
        vmem((hops + 1, 8, width), F32), vmem((hops, 8, width), F32),
        pltpu.SemaphoreType.DMA((4 + 4 * layers,)), pltpu.SemaphoreType.DMA((C, 2)), pltpu.SemaphoreType.DMA((2, C, 2)),
        pltpu.SemaphoreType.DMA((2, C, 2)), pltpu.SemaphoreType.DMA((2, C)),
        pltpu.SemaphoreType.DMA((len(pieces), 6, 2)), pltpu.SemaphoreType.DMA((len(pieces),)), pltpu.SemaphoreType.DMA((hops, 2)),
        pltpu.SemaphoreType.DMA((max(hops - 4, 1), 2)), pltpu.SemaphoreType.REGULAR((max(hops - 4, 1),)),
    ]
    return pl.pallas_call(
        functools.partial(step_kernel, mesh.shape["tensor"], n_dp, pieces),
        out_shape=(jax.ShapeDtypeStruct(x.shape, BF16), jax.ShapeDtypeStruct(x.shape, F32),
                   jax.ShapeDtypeStruct(grads, BF16),
                   jax.ShapeDtypeStruct(gain.shape, F32), jax.ShapeDtypeStruct(gain.shape, F32)),
        in_specs=[SMEM] + [ANY] * 6 + [VMEM, VMEM], out_specs=(ANY, ANY, ANY, VMEM, VMEM), scratch_shapes=scratch,
        compiler_params=pltpu.CompilerParams(collective_id=0, has_side_effects=True, vmem_limit_bytes=62 * 2**20),
        name="step",
    )(lengths, x, cot, wqkv, wout, wup, wdown, gain, bias)


def per_device(
    mesh, inputs, lengths, qkv_weight, out_weight, up_weight, down_weight, norm_gain, norm_bias, cotangent
):
    layers, width, three, part_width = qkv_weight.shape
    ff = up_weight.shape[2]
    outputs, input_grad, grads, grad_gain, grad_bias = step_call(
        mesh, lengths, inputs, cotangent, qkv_weight.transpose(0, 2, 3, 1).reshape(layers, three * part_width, width),
        out_weight, up_weight, down_weight, norm_gain, norm_bias,
    )
    outputs, input_grad, grad_gain, grad_bias, grad_up, grad_down, grad_out, grad_qkv = widen_call(
        outputs, input_grad, grad_gain, grad_bias, grads, ff, part_width
    )
    grad_qkv = grad_qkv.reshape(layers, three, part_width, width).transpose(0, 3, 1, 2)
    return (outputs, input_grad, grad_qkv, grad_out, grad_up, grad_down, grad_gain, grad_bias)


def widen_kernel(spans, act_in, ig_in, gain_in, bias_in, grads_in, act_out, ig_out, gain_out, bias_out, *rest):
    outs, (act, ig, gain, bias, low, wide, sem_in, sem_out) = rest[:len(spans)], rest[len(spans):]
    layers = grads_in.shape[0]
    through = [(act_in, act, act_out), (ig_in, ig, ig_out), (gain_in, gain, gain_out), (bias_in, bias, bias_out)]
    blocks = [(l, k, at, at + i, n) for k, (at, rows, n) in enumerate(spans) for l in range(layers) for i in range(0, rows, n)]
    into = [pltpu.make_async_copy(grads_in.at[l, pl.ds(r, n)], low.at[l, pl.ds(r, n)], sem_in.at[i]) for i, (l, _, _, r, n) in enumerate(blocks)]
    into += [pltpu.make_async_copy(a, v, sem_in.at[len(blocks) + i]) for i, (a, v, _) in enumerate(through)]
    for copy in into:
        copy.start()
    back = []
    for i, (l, k, at, r, n) in enumerate(blocks):
        into[i].wait()
        wide[l, pl.ds(r, n)] = low[l, pl.ds(r, n)].astype(F32)
        back.append(pltpu.make_async_copy(wide.at[l, pl.ds(r, n)], outs[k].at[l, pl.ds(r - at, n)], sem_out.at[i]))
        back[-1].start()
    for i, (_, v, o) in enumerate(through):
        into[len(blocks) + i].wait()
        back.append(pltpu.make_async_copy(v, o, sem_out.at[len(blocks) + i]))
        back[-1].start()
    for copy in back:
        copy.wait()


def widen_call(outputs, input_grad, grad_gain, grad_bias, grads, ff, part_width):
    layers, _, width = grads.shape
    spans, at = [], 0
    for rows in (width, ff, part_width, 3 * part_width):
        spans.append((at, rows, PIECE))
        at += rows
    count = sum(layers * rows // n for _, rows, n in spans) + 4
    return pl.pallas_call(
        functools.partial(widen_kernel, spans),
        out_shape=(jax.ShapeDtypeStruct(outputs.shape, BF16), jax.ShapeDtypeStruct(input_grad.shape, F32))
        + (jax.ShapeDtypeStruct(grad_gain.shape, F32),) * 2
        + tuple(jax.ShapeDtypeStruct((layers, rows, width), F32) for _, rows, _ in spans),
        in_specs=[ANY] * 5, out_specs=(ANY,) * (4 + len(spans)),
        scratch_shapes=[pltpu.VMEM(outputs.shape, BF16), pltpu.VMEM(input_grad.shape, F32),
                        pltpu.VMEM(grad_gain.shape, F32), pltpu.VMEM(grad_bias.shape, F32), pltpu.VMEM(grads.shape, BF16),
                        pltpu.VMEM(grads.shape, F32), pltpu.SemaphoreType.DMA((count,)), pltpu.SemaphoreType.DMA((count,))],
        compiler_params=pltpu.CompilerParams(vmem_limit_bytes=62 * 2**20),
        name="widen",
    )(outputs, input_grad, grad_gain, grad_bias, grads)


def solution(mesh):
    in_specs = (
        P("dp", None),
        P("dp"),
        P(None, None, None, "tensor"),
        P(None, "tensor", None),
        P(None, None, "tensor"),
        P(None, "tensor", None),
        P(),
        P(),
        P("dp", None),
    )
    out_specs = (
        P("dp", None),
        P("dp", None),
        P(None, None, None, "tensor"),
        P(None, "tensor", None),
        P(None, None, "tensor"),
        P(None, "tensor", None),
        P(),
        P(),
    )
    return jax.shard_map(
        functools.partial(per_device, mesh), mesh=mesh, in_specs=in_specs, out_specs=out_specs, check_vma=False
    )
```

```python
import functools

import jax
import jax.numpy as jnp
from jax import lax
from jax.experimental import pallas as pl
from jax.experimental.pallas import tpu as pltpu
from jax.sharding import PartitionSpec as P

HEAD_DIM = 64
LANES = 128
PAD = 256
CHUNK = 256
STEP_US = 5.33
HOP_US = 0.94
TAIL_HOP_US = 2.54
US_PER_ROW = 0.0335
PIECE = 192
ORDERS = "xzxxxzwxxzwxxzzwxxxwxzxx"
BF16 = jnp.bfloat16
F32 = jnp.float32
MESH = pl.DeviceIdType.MESH
ANY = pl.BlockSpec(memory_space=pl.ANY)
VMEM = pl.BlockSpec(memory_space=pltpu.VMEM)
SMEM = pl.BlockSpec(memory_space=pltpu.SMEM)


def dot_nn(a, b):
    return lax.dot_general(a, b, (((1,), (0,)), ((), ())), preferred_element_type=F32)


def dot_nt(a, b):
    return lax.dot_general(a, b, (((1,), (1,)), ((), ())), preferred_element_type=F32)


def dot_tn(a, b):
    return lax.dot_general(a, b, (((0,), (0,)), ((), ())), preferred_element_type=F32)


def norm_parts(v):
    centre = v - jnp.mean(v, axis=-1, keepdims=True)
    r = lax.rsqrt(jnp.mean(centre * centre, axis=-1, keepdims=True) + 1e-05)
    return centre * r, r


def norm_rows(v, gain_row, bias_row):
    return norm_parts(v)[0] * gain_row + bias_row


def gelu_pair(u):
    bell = jnp.exp(u * u * -0.5)
    t = 1.0 / (1.0 + 0.23164189 * jnp.abs(u))
    series = t * (0.127414796 + t * (-0.142248368 + t * (0.7107068705 + t * (-0.7265760135 + t * 0.5307027145))))
    tail = series * bell
    phi_cdf = jnp.where(u >= 0.0, 1.0 - tail, tail)
    return u * phi_cdf, phi_cdf + u * bell * 0.3989422804014327


def cut_pieces(rows, late):
    return [(ORDERS[i], 1 - i // (rows // PIECE), i % (rows // PIECE) * PIECE, PIECE) for i in range(2 * rows // PIECE)]


def takes_over(pieces, i, late):
    kind, l, at, n = pieces[i]
    if l == 1 or at < late:
        return None
    return next(k for k, p in enumerate(pieces) if p == (kind, 1, at - late, n))


def scratch_rows(pieces, late):
    total = 0
    for i, (kind, _, _, n) in enumerate(pieces):
        total += n // 2 if takes_over(pieces, i, late) is not None else (2 * n if kind == "z" else 3 * n // 2)
    return total


def step_kernel(n_tensor, n_dp, pieces, len_ref, x_hbm, cot_hbm, wqkv_hbm, wout_hbm, wup_hbm, wdown_hbm, gain_ref, bias_ref,
                act_out, ig_out, grads_out, ggain_out, gbias_out,
                xin, dzb, wqkv, wout, wup, wdown, normed, nmid, q_s, k_s, kt_s, v_s, ctx, lse, xh, midh, act, gpr,
                part, rsbuf, ysend, yrecv, dmidb, dmh, dk_s, dv_s, grads, gacc, art, nsum, nrecv,
                sems_in, rs_sem, y_sem, ag_sem, out_sem, ar_sem, own_sem, norm_sem, extra_sem, ready_sem):
    layers = wqkv.shape[0]
    rows_all, width = xin.shape
    ff = wup.shape[2]
    C, half = rows_all // CHUNK, CHUNK // 2
    part_width = 3 * HEAD_DIM
    dp, t = lax.axis_index("dp"), lax.axis_index("tensor")
    b = lax.rem(t, 2)
    sib = (dp, t + 1 - 2 * b)
    peer = (dp, lax.rem(t + 2, n_tensor))
    x_at, z_at = lax.rem(dp, 2), lax.rem(lax.div(dp, 2), 4)
    x_dev = (dp + 1 - 2 * x_at, t)
    z_dev = (dp + 2 - 4 * lax.rem(z_at, 2), t)
    mid_dev = (dp + 6 - 4 * z_at, t)
    more = [(dp + d - 2 * d * lax.rem(lax.div(dp, d), 2), t) for d in (8 * 2**i for i in range((n_dp // 8).bit_length() - 1))]
    outer = lax.rem(z_at, 3) == 0
    inner = jnp.logical_not(outer)
    z_half = lax.div(z_at, 2)
    length = len_ref[0]

    pairs = [(x_hbm, xin)]
    for l in range(layers):
        for j in range(3):
            pairs.append((wqkv_hbm.at[l, pl.ds(j * part_width, part_width)], wqkv.at[l, pl.ds(j * PAD, part_width)]))
    pairs += [(wout_hbm.at[l], wout.at[l, pl.ds(0, part_width)]) for l in range(layers)]
    pairs += [(wup_hbm, wup), (wdown_hbm, wdown), (cot_hbm, dzb)]
    loads = [pltpu.make_async_copy(a, o, sems_in.at[i]) for i, (a, o) in enumerate(pairs)]
    need_x, need_qkv, need_out, need_up, need_down, need_cot = 0, 1, 1 + 3 * layers, 1 + 4 * layers, 2 + 4 * layers, 3 + 4 * layers
    first_loads = [need_x, need_qkv, need_qkv + 1, need_qkv + 2, need_out]
    for i in first_loads:
        loads[i].start()

    def clear_pad(l):
        for j in range(3):
            wqkv[l, j * PAD + part_width:(j + 1) * PAD] = jnp.zeros((PAD - part_width, width), BF16)
        wout[l, part_width:PAD] = jnp.zeros((PAD - part_width, width), BF16)

    clear_pad(0)
    pg = gpr.at[layers - 1]
    waited = set()

    def need(i):
        if i not in waited:
            waited.add(i)
            loads[i].wait()
            if i == need_qkv + 2:
                for k in range(len(loads)):
                    if k not in first_loads:
                        loads[k].start()
                for l in range(1, layers):
                    clear_pad(l)

    barrier = pltpu.get_barrier_semaphore()
    greeted = [sib, peer, x_dev, z_dev, mid_dev] + more
    for other in greeted:
        pl.semaphore_signal(barrier, inc=1, device_id=other, device_id_type=MESH)

    def remote(src, dst, sem, dev):
        return pltpu.make_async_remote_copy(src_ref=src, dst_ref=dst, send_sem=sem.at[0], recv_sem=sem.at[1],
                                            device_id=dev, device_id_type=MESH)

    def chunk(c):
        return pl.ds(c * CHUNK, CHUNK)

    def mine(c):
        return pl.ds(pl.multiple_of(c * CHUNK + b * half, half), half)

    def rs_copy(o, c):
        theirs = pl.ds(pl.multiple_of((1 - b) * half, half), half)
        return remote(part.at[c, theirs], rsbuf.at[c], rs_sem.at[c], sib)

    def y_copy(o, c):
        return remote(ysend.at[c], yrecv.at[o % 2, c], y_sem.at[o % 2, c], peer)

    def ag_pair(o, c):
        rows = mine(c)
        whole = {0: nmid.at[0], 1: normed.at[1], 2: nmid.at[1], 3: dmidb, 4: dzb, 5: dmidb}
        if o in whole:
            return whole[o].at[rows], whole[o].at[rows]
        return (dmh.at[c], ig_out.at[rows]) if o == 6 else (ysend.at[c], act_out.at[rows])

    def ag_copy(o, c):
        return remote(*ag_pair(o, c), ag_sem.at[o % 2, c], sib)

    def own_copy(o, c):
        return pltpu.make_async_copy(*ag_pair(o, c), out_sem.at[o - 6, c])

    def gain(l, i):
        return gain_ref[l, i:i + 1, :]

    def bias(l, i):
        return bias_ref[l, i:i + 1, :]

    low = lax.broadcasted_iota(jnp.int32, (CHUNK, LANES), 1) < HEAD_DIM
    head_lanes = (slice(0, LANES), slice(0, LANES), slice(LANES, 2 * LANES))

    def one_head(v, h):
        w = v[:, head_lanes[h]]
        if h == 0:
            return jnp.where(low, w, jnp.zeros_like(w))
        return jnp.where(low, jnp.zeros_like(w), w) if h == 1 else w

    def attend(l, c):
        rows = chunk(c)
        if l == 0:
            need(need_x)
            normed[0, rows] = norm_rows(xin[rows].astype(F32), gain(0, 0), bias(0, 0)).astype(BF16)
        for j in range(3):
            need(need_qkv + 3 * l + j)
        nc = normed[l, rows]
        q = dot_nt(nc, wqkv[l, 0:PAD]).astype(BF16) * jnp.asarray(HEAD_DIM ** (-0.5), BF16)
        k = dot_nt(nc, wqkv[l, PAD:2 * PAD])
        q_s[l, rows] = q
        k_s[l, rows] = k.astype(BF16)
        kt_s[l, :, rows] = k.T.astype(BF16)
        v_s[l, rows] = dot_nt(nc, wqkv[l, 2 * PAD:3 * PAD]).astype(BF16)
        wide = (c + 1) * CHUNK
        key_pos = lax.broadcasted_iota(jnp.int32, (CHUNK, wide), 1)
        query_pos = lax.broadcasted_iota(jnp.int32, (CHUNK, wide), 0) + c * CHUNK
        allowed = (key_pos <= query_pos) & (key_pos < length)
        lane = lax.broadcasted_iota(jnp.int32, (CHUNK, LANES), 1)
        outs = []
        logs = jnp.zeros((CHUNK, LANES), F32)
        for h in range(3):
            s = dot_nt(one_head(q, h), k_s[l, 0:wide, head_lanes[h]])
            s = jnp.where(allowed, s, -1e30)
            m = jnp.max(s, axis=-1, keepdims=True)
            p = jnp.exp(s - m)
            z = jnp.sum(p, axis=-1, keepdims=True)
            outs.append(dot_nn(p.astype(BF16), v_s[l, 0:wide, head_lanes[h]]) / z)
            logs = jnp.where(lane == h, m + jnp.log(z), logs)
        lse[l, :, rows] = logs.T[0:8, :]
        ctx[l, rows, 0:LANES] = jnp.where(low, outs[0], outs[1]).astype(BF16)
        ctx[l, rows, LANES:2 * LANES] = outs[2].astype(BF16)
        need(need_out + l)
        part[c] = dot_nn(ctx[l, rows], wout[l]).astype(BF16)

    def feed(l, c):
        need(need_up)
        need(need_down)
        rows = chunk(c)
        nm = nmid[l, rows]
        last = l + 1 == layers
        if last:
            need(need_cot)
            pos = lax.broadcasted_iota(jnp.int32, (CHUNK, width), 0) + c * CHUNK
            dz = jnp.where(pos < length, dzb[rows].astype(F32), 0.0).astype(BF16)
            dzb[rows] = dz
        for n in range(0, ff, 256):
            a, g = gelu_pair(dot_nn(nm, wup[l, :, n:n + 256]))
            act[l, rows, n:n + 256] = a.astype(BF16)
            if last:
                g = g * dot_nt(dz, wdown[l, n:n + 256, :])
            gpr[l, rows, n:n + 256] = g.astype(BF16)
        if last:
            part[c] = dot_nt(gpr[l, rows], wup[l]).astype(BF16)
        else:
            part[c] = dot_nn(act[l, rows], wdown[l]).astype(BF16)

    def feed_back(l, c):
        rows = chunk(c)
        dz = dzb[rows]
        for n in range(0, ff, 256):
            g = gpr[l, rows, n:n + 256].astype(F32) * dot_nt(dz, wdown[l, n:n + 256, :])
            gpr[l, rows, n:n + 256] = g.astype(BF16)
        part[c] = dot_nt(gpr[l, rows], wup[l]).astype(BF16)

    def attend_back(l, c):
        rows = chunk(c)
        dctx = dot_nt(dmidb[rows], wout[l]).astype(BF16)
        wide = (c + 1) * CHUNK
        key_pos = lax.broadcasted_iota(jnp.int32, (wide, CHUNK), 0)
        query_pos = lax.broadcasted_iota(jnp.int32, (wide, CHUNK), 1) + c * CHUNK
        allowed = (key_pos <= query_pos) & (key_pos < length)
        q = q_s[l, rows]
        dqs = []
        keys = slice(0, wide)
        for h in range(3):
            lanes = head_lanes[h]
            qh, dch = one_head(q, h), one_head(dctx, h)
            s = jnp.where(allowed, dot_nt(k_s[l, keys, lanes], qh), -1e30)
            p = jnp.exp(s - lse[l, h:h + 1, rows])
            weighed = p * dot_nt(v_s[l, keys, lanes], dch)
            ds = (weighed - p * jnp.sum(weighed, axis=0, keepdims=True)).astype(BF16)
            dv = dot_nn(p.astype(BF16), dch)
            dk = dot_nn(ds, qh)
            if c == C - 1 and h != 1:
                dv_s[keys, lanes] = dv
                dk_s[keys, lanes] = dk
            else:
                dv_s[keys, lanes] += dv
                dk_s[keys, lanes] += dk
            dqs.append(dot_nn(kt_s[l, h * HEAD_DIM:(h + 1) * HEAD_DIM, keys], ds) * HEAD_DIM ** (-0.5))
        dqs.append(jnp.zeros((PAD - part_width, CHUNK), F32))
        pg[rows, 0:PAD] = jnp.concatenate(dqs, axis=0).T.astype(BF16)
        pg[rows, PAD:2 * PAD] = dk_s[rows].astype(BF16)
        pg[rows, 2 * PAD:3 * PAD] = dv_s[rows].astype(BF16)
        part[c] = dot_nn(pg[rows], wqkv[l]).astype(BF16)

    def compute(o, c):
        if o == 7:
            part[c] = dot_nn(act[1, chunk(c)], wdown[1]).astype(BF16)
        elif o < 4:
            (attend if o % 2 == 0 else feed)(o // 2, c)
        else:
            (attend_back if o % 2 == 0 else feed_back)(1 if o == 4 else 0, c)

    up_at, down_at, out_at, qkv_at = 0, width, width + ff, width + ff + part_width

    def weights_of_feed(l):
        for m in range(0, width, 384):
            grads[l, up_at + m:up_at + m + 384] = dot_tn(nmid[l, :, m:m + 384], gpr[l]).astype(BF16)
            launch(l, up_at + m)
        for m in range(0, ff, 384):
            grads[l, down_at + m:down_at + m + 384] = dot_tn(act[l, :, m:m + 384], dzb[...]).astype(BF16)
            launch(l, down_at + m)

    def weights_of_attend(l):
        grads[l, out_at:out_at + part_width] = dot_tn(ctx[l], dmidb[...])[0:part_width].astype(BF16)
        launch(l, out_at)
        for j in range(3):
            at = qkv_at + j * part_width
            grads[l, at:at + part_width] = dot_tn(gpr[layers - 1, :, j * PAD:(j + 1) * PAD], normed[l])[0:part_width].astype(BF16)
            launch(l, at)

    def rows_at(at, n):
        return pl.ds(pl.multiple_of(at, 16), n)

    def add_rows(l, at, tmp_at, n):
        def block(i, carry):
            rows = rows_at(at + i * 96, 96)
            grads[l, rows] = (grads[l, rows].astype(F32) + art[rows_at(tmp_at + i * 96, 96)].astype(F32)).astype(BF16)
            return carry

        lax.fori_loop(0, n // 96, block, 0)

    def extra_sums(l, at, tmp_at, n):
        for i, dev in enumerate(more):
            pl.semaphore_signal(ready_sem.at[i], inc=1, device_id=dev, device_id_type=MESH)
            pl.semaphore_wait(ready_sem.at[i], 1)
            copy = remote(grads.at[l, rows_at(at, n)], art.at[pl.ds(tmp_at, n)], extra_sem.at[i], dev)
            copy.start()
            copy.wait()
            add_rows(l, at, tmp_at, n)

    class Piece:
        def __init__(self, kind, l, at, n, slot, tmp):
            self.kind, self.l, self.n, self.at, self.turn, self.ready = kind, l, n, at, 0, 0.0
            h = n // 2
            pick = z_half if kind == "z" else x_at
            self.keep, self.give = at + pick * h, at + (1 - pick) * h
            keep, give, whole = (grads.at[l, rows_at(self.keep, h)], grads.at[l, rows_at(self.give, h)], grads.at[l, pl.ds(at, n)])
            sizes = (n, h, h) if kind == "z" else (h, h, h)
            self.tmp = tmp
            land = [art.at[pl.ds(a, m)] for a, m in zip(tmp, sizes)]
            done_keep, done_give = grads_out.at[l, rows_at(self.keep, h)], grads_out.at[l, rows_at(self.give, h)]
            self.own = pltpu.make_async_copy(keep, done_keep, own_sem.at[slot])
            if kind != "z":
                ends = [(give, land[0], x_dev), (keep, land[1], z_dev), (keep, land[2], mid_dev), (keep, done_keep, z_dev),
                        (keep, done_keep, x_dev), (done_keep, done_keep, x_dev), (done_give, done_give, z_dev)]
            else:
                ends = [(whole, land[0], z_dev), (give, land[1], mid_dev), (keep, land[2], x_dev), (keep, done_keep, mid_dev),
                        (keep, done_keep, z_dev), (done_give, done_give, z_dev)]
            at_sem = (0, 1, 2, 3, 4, 5) if kind == "z" else (0, 1, 2, 3, 4, 4, 5)
            self.copies = [remote(src, dst, ar_sem.at[slot, i], dev) for i, (src, dst, dev) in zip(at_sem, ends)]
            x_out, x_in, z_out, z_in, mid = (("x", "outer"), h), (("x", "inner"), h), (("z", "outer"), h), (("z", "inner"), h), (("mid", "inner"), h)
            self.links = {
                "x": ((x_out, x_in), (z_out,), (mid,), (z_in, x_in), (x_out,)),
                "w": ((x_out, x_in), (z_out,), (mid,), (z_in,), (x_out,), (z_out,)),
                "z": (((("z", "outer"), n),), (mid,), (x_in,), (mid, z_in), (z_in,)),
            }[kind]

        def step(self):
            c, l, n, h = self.copies, self.l, self.n, self.n // 2
            if self.kind != "z":
                if self.turn == 0:
                    c[0].start()
                elif self.turn == 1:
                    c[0].wait()
                    add_rows(l, self.keep, self.tmp[0], h)
                    pl.when(outer)(c[1].start)
                elif self.turn == 2:
                    @pl.when(inner)
                    def _():
                        c[1].wait_recv()
                        add_rows(l, self.keep, self.tmp[1], h)
                        c[2].start()
                    pl.when(outer)(c[1].wait_send)
                elif self.turn == 3:
                    @pl.when(inner)
                    def _():
                        c[2].wait()
                        add_rows(l, self.keep, self.tmp[2], h)
                        extra_sums(l, self.keep, self.tmp[0], h)
                        c[3].start()
                        if self.kind == "x":
                            c[4].start()
                        self.own.start()
                elif self.turn == 4:
                    @pl.when(outer)
                    def _():
                        c[3].wait_recv()
                        c[5].start()
                elif self.turn == 5:
                    @pl.when(inner)
                    def _():
                        c[3].wait_send()
                        self.own.wait()
                    if self.kind == "x":
                        c[4].wait()
                    else:
                        @pl.when(outer)
                        def _():
                            c[5].wait()
                            c[6].start()
                else:
                    pl.when(outer)(c[6].wait_send)
                    pl.when(inner)(c[6].wait_recv)
            else:
                if self.turn == 0:
                    pl.when(outer)(c[0].start)
                elif self.turn == 1:
                    @pl.when(inner)
                    def _():
                        c[0].wait_recv()
                        add_rows(l, self.at, self.tmp[0], n)
                        c[1].start()
                    pl.when(outer)(c[0].wait_send)
                elif self.turn == 2:
                    @pl.when(inner)
                    def _():
                        c[1].wait()
                        add_rows(l, self.keep, self.tmp[1], h)
                        c[2].start()
                elif self.turn == 3:
                    @pl.when(inner)
                    def _():
                        c[2].wait()
                        add_rows(l, self.keep, self.tmp[2], h)
                        extra_sums(l, self.keep, self.tmp[1], h)
                        c[3].start()
                        c[4].start()
                        self.own.start()
                elif self.turn == 4:
                    @pl.when(inner)
                    def _():
                        c[3].wait()
                        c[5].start()
                else:
                    @pl.when(inner)
                    def _():
                        c[4].wait_send()
                        c[5].wait_send()
                        self.own.wait()

                    @pl.when(outer)
                    def _():
                        c[4].wait_recv()
                        c[5].wait_recv()
            if self.turn < len(self.links):
                self.ready = 0.0
                for link, rows in self.links[self.turn]:
                    free[link] = max(clock[0], free.get(link, 0.0)) + rows * US_PER_ROW
                    self.ready = max(self.ready, free[link] + HOP_US)
            self.turn += 1

    class Norms:
        def __init__(self):
            self.turn, self.ready = 0, clock[0]
            nsum[0] = jnp.concatenate([jnp.sum(gacc[i], axis=0, keepdims=True) for i in range(8)], axis=0)
            partners = [sib, x_dev, z_dev, mid_dev] + more
            self.copies = [remote(nsum.at[i], nrecv.at[i], norm_sem.at[i], dev) for i, dev in enumerate(partners)]

        def step(self):
            i = self.turn
            if i > 0:
                self.copies[i - 1].wait()
                nsum[i] = nsum[i - 1] + nrecv[i - 1]
            if i < len(self.copies):
                self.copies[i].start()
            self.turn += 1
            links = ((), ("x",), ("z",), ("z", "mid"))[min(i, 3)]
            self.ready = max([clock[0]] + [free.get((link, role), 0.0) for link in links for role in ("outer", "inner")]) + HOP_US

        def over(self):
            return self.turn > len(self.copies)

    clock, free, jobs, held, over = [0.0], {}, [], [], set()
    slots = {}
    cursor = 0
    for i, (kind, l, at, n) in enumerate(pieces):
        before = takes_over(pieces, i, out_at)
        sizes = (n, n // 2, n // 2) if kind == "z" else (n // 2,) * 3
        tmp = []
        if before is not None:
            tmp, sizes = slots[pieces[before][1:3]][3][0:2], sizes[2:]
        for m in sizes:
            tmp = tmp + [cursor]
            cursor += m
        slots[(l, at)] = (kind, n, i, tmp, None, None if before is None else pieces[before][1:3])

    def launch(l, at):
        block_end = at + (384 if at < out_at else part_width)
        for (l2, at2), (kind, n, slot, tmp, _, before) in slots.items():
            if l2 == l and at < at2 + n <= block_end:
                held.append((l2, at2))
        release()

    def release():
        for key in list(held):
            kind, n, slot, tmp, _, before = slots[key]
            if before is None or before in over:
                held.remove(key)
                job = Piece(kind, key[0], key[1], n, slot, tmp)
                job.key = key
                job.step()
                jobs.append(job)

    def advance(job):
        job.step()
        if job.over() if isinstance(job, Norms) else job.turn > len(job.links):
            jobs.remove(job)
            if isinstance(job, Piece):
                over.add(job.key)
                release()

    def serve():
        while True:
            due = [job for job in jobs if job.ready <= clock[0]]
            if not due:
                return
            advance(min(due, key=lambda job: job.ready))

    def serve_rest():
        while jobs:
            job = min(jobs, key=lambda job: job.ready)
            clock[0] = max(clock[0], job.ready - HOP_US + TAIL_HOP_US) + 0.3
            advance(job)

    def sum_pair(o, c):
        rs_copy(o, c).wait()
        own = part[c, pl.ds(pl.multiple_of(b * half, half), half), :]
        ysend[c] = (own.astype(F32) + rsbuf[c].astype(F32)).astype(BF16)
        y_copy(o, c).start()

    def norm_back(l, i, v, e):
        xhat, r = norm_parts(v)
        for at, term in ((2 * l + i, e * xhat), (4 + 2 * l + i, e)):
            gacc[at] += jnp.sum(term.reshape(half // 8, 8, width), axis=0)
        eg = e * gain(l, i)
        return r * (eg - jnp.mean(eg, axis=-1, keepdims=True) - xhat * jnp.mean(eg * xhat, axis=-1, keepdims=True))

    def valid_half(c, v):
        pos = lax.broadcasted_iota(jnp.int32, (half, width), 0) + (c * CHUNK + b * half)
        return jnp.where(pos < length, v, 0.0)

    def finish(o, c):
        y_copy(o, c).wait()
        rows = mine(c)
        total = ysend[c].astype(F32) + yrecv[o % 2, c].astype(F32)
        if o in (0, 2):
            l = o // 2
            middle = (xin[rows].astype(F32) if l == 0 else xh[c]) + total
            midh[l, c] = middle
            nmid[l, rows] = norm_rows(middle, gain(l, 1), bias(l, 1)).astype(BF16)
        elif o == 1:
            after = valid_half(c, midh[0, c] + total)
            xh[c] = after
            normed[1, rows] = norm_rows(after, gain(1, 0), bias(1, 0)).astype(BF16)
        elif o in (3, 5):
            l, dz = (1, dzb[rows].astype(F32)) if o == 3 else (0, xh[c])
            dmiddle = dz + norm_back(l, 1, midh[l, c], total)
            dmh[c] = dmiddle
            dmidb[rows] = dmiddle.astype(BF16)
        elif o == 4:
            dz = valid_half(c, dmh[c] + norm_back(1, 0, xh[c], total))
            xh[c] = dz
            dzb[rows] = dz.astype(BF16)
        elif o == 6:
            dmh[c] = dmh[c] + norm_back(0, 0, xin[rows].astype(F32), total)
        else:
            ysend[c] = valid_half(c, midh[1, c] + total).astype(BF16)
        ag_copy(o, c).start()
        if o >= 6:
            own_copy(o, c).start()

    gacc[...] = jnp.zeros_like(gacc)
    pending, done = [], set()

    def finish_next(paired=False):
        step = pending.pop(0)
        finish(*step)
        done.add(step)
        clock[0] += STEP_US / 2 if paired else STEP_US
        if step == (6, 0):
            jobs.append(Norms())
        serve()

    for o in range(8):
        for c in (range(C) if o < 4 else reversed(range(C))):
            if o > 0:
                while (o - 1, c) not in done:
                    finish_next()
                ag_copy(o - 1, c).wait()
                if o == 7:
                    own_copy(6, c).wait()
            compute(o, c)
            if (o, c) == (0, 0):
                pl.semaphore_wait(barrier, len(greeted))
            rs_copy(o, c).start()
            if o >= 4:
                clock[0] += STEP_US / 2
                serve()
            if len(pending) >= C - 1:
                finish_next(True)
            sum_pair(o, c)
            pending.append((o, c))
        if o == 3:
            clock[0] = 0.0
        if o in (3, 5):
            weights_of_feed(1 if o == 3 else 0)
        if o in (4, 6):
            weights_of_attend(1 if o == 4 else 0)
    while pending:
        finish_next()
    for c in range(C):
        ag_copy(7, c).wait()
        own_copy(7, c).wait()
    serve_rest()
    norms = nsum[len(greeted) - 1]
    for i in range(2 * layers):
        ggain_out[i // 2, i % 2:i % 2 + 1, :] = norms[i:i + 1]
        gbias_out[i // 2, i % 2:i % 2 + 1, :] = norms[4 + i:5 + i]


def step_call(mesh, lengths, x, cot, wqkv, wout, wup, wdown, gain, bias):
    rows, width = x.shape
    layers, ff = wup.shape[0], wup.shape[2]
    C = rows // CHUNK
    half = (C, CHUNK // 2, width)
    grads = (layers, width + ff + 4 * 3 * HEAD_DIM, width)
    pieces = cut_pieces(grads[1], width + ff)
    n_dp = mesh.shape["dp"]
    hops = 4 + (n_dp // 8).bit_length() - 1
    two = (layers, rows, PAD)

    def vmem(shape, kind=BF16):
        return pltpu.VMEM(shape, kind)

    scratch = [
        vmem(x.shape), vmem(x.shape), vmem((layers, 3 * PAD, width)), vmem((layers, PAD, width)), vmem(wup.shape), vmem(wdown.shape),
        vmem((layers, rows, width)), vmem((layers, rows, width)),
        vmem(two), vmem(two), vmem((layers, PAD, rows)), vmem(two), vmem(two), vmem((layers, 8, rows), F32),
        vmem(half, F32), vmem((layers,) + half, F32), vmem((layers, rows, ff)), vmem((layers, rows, ff)),
        vmem((C, CHUNK, width)), vmem(half), vmem(half), vmem((2,) + half),
        vmem(x.shape), vmem(half, F32), vmem((rows, PAD), F32), vmem((rows, PAD), F32),
        vmem(grads), vmem((8, 8, width), F32), vmem((scratch_rows(pieces, width + ff), width)),
        vmem((hops + 1, 8, width), F32), vmem((hops, 8, width), F32),
        pltpu.SemaphoreType.DMA((4 + 4 * layers,)), pltpu.SemaphoreType.DMA((C, 2)), pltpu.SemaphoreType.DMA((2, C, 2)),
        pltpu.SemaphoreType.DMA((2, C, 2)), pltpu.SemaphoreType.DMA((2, C)),
        pltpu.SemaphoreType.DMA((len(pieces), 6, 2)), pltpu.SemaphoreType.DMA((len(pieces),)), pltpu.SemaphoreType.DMA((hops, 2)),
        pltpu.SemaphoreType.DMA((max(hops - 4, 1), 2)), pltpu.SemaphoreType.REGULAR((max(hops - 4, 1),)),
    ]
    return pl.pallas_call(
        functools.partial(step_kernel, mesh.shape["tensor"], n_dp, pieces),
        out_shape=(jax.ShapeDtypeStruct(x.shape, BF16), jax.ShapeDtypeStruct(x.shape, F32),
                   jax.ShapeDtypeStruct(grads, BF16),
                   jax.ShapeDtypeStruct(gain.shape, F32), jax.ShapeDtypeStruct(gain.shape, F32)),
        in_specs=[SMEM] + [ANY] * 6 + [VMEM, VMEM], out_specs=(ANY, ANY, ANY, VMEM, VMEM), scratch_shapes=scratch,
        compiler_params=pltpu.CompilerParams(collective_id=0, has_side_effects=True, vmem_limit_bytes=62 * 2**20),
        name="step",
    )(lengths, x, cot, wqkv, wout, wup, wdown, gain, bias)


def per_device(
    mesh, inputs, lengths, qkv_weight, out_weight, up_weight, down_weight, norm_gain, norm_bias, cotangent
):
    layers, width, three, part_width = qkv_weight.shape
    ff = up_weight.shape[2]
    outputs, input_grad, grads, grad_gain, grad_bias = step_call(
        mesh, lengths, inputs, cotangent, qkv_weight.transpose(0, 2, 3, 1).reshape(layers, three * part_width, width),
        out_weight, up_weight, down_weight, norm_gain, norm_bias,
    )
    outputs, input_grad, grad_gain, grad_bias, grad_up, grad_down, grad_out, grad_qkv = widen_call(
        outputs, input_grad, grad_gain, grad_bias, grads, ff, part_width
    )
    grad_qkv = grad_qkv.reshape(layers, three, part_width, width).transpose(0, 3, 1, 2)
    return (outputs, input_grad, grad_qkv, grad_out, grad_up, grad_down, grad_gain, grad_bias)


def widen_kernel(spans, act_in, ig_in, gain_in, bias_in, grads_in, act_out, ig_out, gain_out, bias_out, *rest):
    outs, (act, ig, gain, bias, low, wide, sem_in, sem_out) = rest[:len(spans)], rest[len(spans):]
    layers = grads_in.shape[0]
    through = [(act_in, act, act_out), (ig_in, ig, ig_out), (gain_in, gain, gain_out), (bias_in, bias, bias_out)]
    blocks = [(l, k, at, at + i, n) for k, (at, rows, n) in enumerate(spans) for l in range(layers) for i in range(0, rows, n)]
    into = [pltpu.make_async_copy(grads_in.at[l, pl.ds(r, n)], low.at[l, pl.ds(r, n)], sem_in.at[i]) for i, (l, _, _, r, n) in enumerate(blocks)]
    into += [pltpu.make_async_copy(a, v, sem_in.at[len(blocks) + i]) for i, (a, v, _) in enumerate(through)]
    for copy in into:
        copy.start()
    back = []
    for i, (l, k, at, r, n) in enumerate(blocks):
        into[i].wait()
        wide[l, pl.ds(r, n)] = low[l, pl.ds(r, n)].astype(F32)
        back.append(pltpu.make_async_copy(wide.at[l, pl.ds(r, n)], outs[k].at[l, pl.ds(r - at, n)], sem_out.at[i]))
        back[-1].start()
    for i, (_, v, o) in enumerate(through):
        into[len(blocks) + i].wait()
        back.append(pltpu.make_async_copy(v, o, sem_out.at[len(blocks) + i]))
        back[-1].start()
    for copy in back:
        copy.wait()


def widen_call(outputs, input_grad, grad_gain, grad_bias, grads, ff, part_width):
    layers, _, width = grads.shape
    spans, at = [], 0
    for rows in (width, ff, part_width, 3 * part_width):
        spans.append((at, rows, PIECE))
        at += rows
    count = sum(layers * rows // n for _, rows, n in spans) + 4
    return pl.pallas_call(
        functools.partial(widen_kernel, spans),
        out_shape=(jax.ShapeDtypeStruct(outputs.shape, BF16), jax.ShapeDtypeStruct(input_grad.shape, F32))
        + (jax.ShapeDtypeStruct(grad_gain.shape, F32),) * 2
        + tuple(jax.ShapeDtypeStruct((layers, rows, width), F32) for _, rows, _ in spans),
        in_specs=[ANY] * 5, out_specs=(ANY,) * (4 + len(spans)),
        scratch_shapes=[pltpu.VMEM(outputs.shape, BF16), pltpu.VMEM(input_grad.shape, F32),
                        pltpu.VMEM(grad_gain.shape, F32), pltpu.VMEM(grad_bias.shape, F32), pltpu.VMEM(grads.shape, BF16),
                        pltpu.VMEM(grads.shape, F32), pltpu.SemaphoreType.DMA((count,)), pltpu.SemaphoreType.DMA((count,))],
        compiler_params=pltpu.CompilerParams(vmem_limit_bytes=62 * 2**20),
        name="widen",
    )(outputs, input_grad, grad_gain, grad_bias, grads)


def solution(mesh):
    in_specs = (
        P("dp", None),
        P("dp"),
        P(None, None, None, "tensor"),
        P(None, "tensor", None),
        P(None, None, "tensor"),
        P(None, "tensor", None),
        P(),
        P(),
        P("dp", None),
    )
    out_specs = (
        P("dp", None),
        P("dp", None),
        P(None, None, None, "tensor"),
        P(None, "tensor", None),
        P(None, None, "tensor"),
        P(None, "tensor", None),
        P(),
        P(),
    )
    return jax.shard_map(
        functools.partial(per_device, mesh), mesh=mesh, in_specs=in_specs, out_specs=out_specs, check_vma=False
    )
```
